32 devices in a mesh: sfc: 16 (over z, x, core), sub: 2 (over y).
Axes of the slice: x: 2, y: 2, z: 4, core: 2. Of those that a mesh axis runs over, the one named last changes fastest.
Arguments:
- fine_state: float32 [16, 2, 2, 5, 512], P('sfc', 'sub'), as said below
- coarse_old: float32 [16, 2, 5, 512], P('sfc', 'sub'), as said below
- box_count: int32 [16, 2], P('sfc', 'sub'), may hold values from 1 to 2, as said below
- fine_links: int32 [16, 2, 2, 6], P('sfc', 'sub'), may hold values from -1 to 5, as said below
- coarse_links: int32 [16, 2, 2, 6, 4], P('sfc', 'sub'), may hold values from 0 to 4, as said below
Outputs:
- advanced_state: float32 [16, 2, 2, 5, 512], P('sfc', 'sub')
The draws below stay inside these ranges and needn't reach their ends.
Inputs may be any that keep to these rules, and one draw needn't show every extreme that they name: Slots 0 to box_count - 1 of a device are live. Some device holds 2 live boxes in every draw. `fine_links`: A value v >= 0 names slot v mod 2 of the device at curve segment offset v div 2 - 1 (-1, 0 or +1) in the same group member, and that slot is live; the first segment has no offset -1 and the last no offset +1. Dead slots hold -1. Of one device's faces at most 2 take ghosts from offset -1 and at most 2 from offset +1; both bounds are reached in every draw. `coarse_links`: entry 0 is a group member index; entries 1 to 3 are a corner such that the region described in the reference program lies inside the coarse box. `fine_state`: mass and pressure of every cell are positive and of order one, each velocity component below one in magnitude. `coarse_old`: as for fine_state.
All inputs are finite; a program needn't handle non-finite values.
Results may differ from the reference program's by a relative error of at most 0.0003.
Values sent between devices are 32-bit elements; how exact they have to be, the bound alone decides.
No kernel may reach another device: no remote copies, remote signals or barrier semaphores. Data moves between devices by JAX's collectives and lax.ppermute only.
A program may use at most 64 MiB of HBM per device.

```python
import math
import jax
import jax.numpy as jnp
import numpy as np
from jax import lax

B = 8
MAXB = 2
FCAP = 2
SEGMENTS = 16
GROUP = 2


def conserved_from(density, motion, pressure):
    momentum = density * motion
    energy = pressure / 0.4 + 0.5 * density * jnp.sum(motion * motion, axis=-2, keepdims=True)
    return jnp.concatenate([density, momentum, energy], axis=-2).astype(jnp.float32)


def lognormal_state(key, leading):
    cell_count = B * B * B
    parts_key = jax.random.split(key, 3)
    density = jnp.exp(jax.random.uniform(parts_key[0], leading + (1, cell_count), jnp.float32, math.log(0.5), math.log(2.0)))
    motion = jnp.clip(0.4 * jax.random.normal(parts_key[1], leading + (3, cell_count), jnp.float32), -0.9, 0.9)
    pressure = jnp.exp(jax.random.uniform(parts_key[2], leading + (1, cell_count), jnp.float32, math.log(0.5), math.log(2.0)))
    return conserved_from(density, motion, pressure)


def draw_fine_state(key, part):
    key = jax.random.fold_in(key, 1)
    return lognormal_state(key, (SEGMENTS, GROUP, MAXB))


def draw_coarse_old(key, part):
    key = jax.random.fold_in(key, 2)
    return lognormal_state(key, (SEGMENTS, GROUP))


def box_layout(key):
    layout_key = jax.random.split(jax.random.fold_in(key, 11), 4)
    heavy = jax.random.randint(layout_key[0], (SEGMENTS, GROUP), 0, 4, dtype=jnp.int32) == 0
    light = jax.random.randint(layout_key[1], (SEGMENTS, GROUP), 1, max(MAXB // 2, 1) + 1, dtype=jnp.int32)
    counts = jnp.where(heavy, MAXB, light).astype(jnp.int32)
    pick_row = jax.random.randint(layout_key[2], (), 1, SEGMENTS - 1, dtype=jnp.int32)
    pick_col = jax.random.randint(layout_key[3], (), 0, GROUP, dtype=jnp.int32)
    row_ids = jnp.arange(SEGMENTS, dtype=jnp.int32)[:, None]
    col_ids = jnp.arange(GROUP, dtype=jnp.int32)[None, :]
    forced = (row_ids == pick_row) & (col_ids == pick_col)
    counts = jnp.where(forced, MAXB, counts).astype(jnp.int32)
    return (counts, forced)


def draw_box_count(key, part):
    counts, forced = box_layout(key)
    return counts


def draw_fine_links(key, part):
    counts, forced = box_layout(key)
    key = jax.random.fold_in(key, 5)
    kind_key, slot_key = jax.random.split(key)
    face_total = 6 * MAXB
    kinds = jax.random.randint(kind_key, (SEGMENTS, GROUP, face_total), 0, 4, dtype=jnp.int32)
    face_ids = jnp.arange(face_total, dtype=jnp.int32)[None, None, :]
    row_ids = jnp.arange(SEGMENTS, dtype=jnp.int32)[:, None, None]
    forced_faces = forced[:, :, None]
    kinds = jnp.where(forced_faces & (face_ids < FCAP), 3, kinds)
    kinds = jnp.where(forced_faces & (face_ids >= FCAP) & (face_ids < 2 * FCAP), 2, kinds)
    kinds = jnp.where((row_ids == 0) & (kinds == 2), 1, kinds)
    kinds = jnp.where((row_ids == SEGMENTS - 1) & (kinds == 3), 1, kinds)
    live_faces = face_ids // 6 < counts[:, :, None]
    kinds = jnp.where(live_faces, kinds, 0)
    for remote_kind in (2, 3):
        hits = kinds == remote_kind
        rank_order = jnp.cumsum(hits.astype(jnp.int32), axis=-1)
        kinds = jnp.where(hits & (rank_order > FCAP), 1, kinds)
    offsets = jnp.where(kinds == 2, 0, jnp.where(kinds == 3, 2, 1)).astype(jnp.int32)
    count_below = jnp.roll(counts, 1, axis=0)[:, :, None]
    count_above = jnp.roll(counts, -1, axis=0)[:, :, None]
    target_count = jnp.where(kinds == 2, count_below, jnp.where(kinds == 3, count_above, counts[:, :, None]))
    target_count = jnp.maximum(target_count, 1)
    raw_slot = jax.random.randint(slot_key, (SEGMENTS, GROUP, face_total), 0, 1 << 20, dtype=jnp.int32)
    target_slot = raw_slot % target_count
    values = jnp.where(kinds == 0, -1, offsets * MAXB + target_slot).astype(jnp.int32)
    return values.reshape(SEGMENTS, GROUP, MAXB, 6)


def draw_coarse_links(key, part):
    key = jax.random.fold_in(key, 7)
    owner_key, corner_key = jax.random.split(key)
    owners = jax.random.randint(owner_key, (SEGMENTS, GROUP, MAXB, 6, 1), 0, GROUP, dtype=jnp.int32)
    raw_corner = jax.random.randint(corner_key, (SEGMENTS, GROUP, MAXB, 6, 3), 0, 1 << 20, dtype=jnp.int32)
    face_dir = (jnp.arange(6, dtype=jnp.int32) // 2)[:, None]
    axis_ids = jnp.arange(3, dtype=jnp.int32)[None, :]
    bounds = jnp.where(face_dir == axis_ids, B - 3, B // 2 - 1).astype(jnp.int32)
    corners = raw_corner % bounds
    return jnp.concatenate([owners, corners], axis=-1).astype(jnp.int32)


def setup_inputs(seed: int = 0) -> dict:
    splits = jax.random.split(jax.random.key(seed), 6)
    fine_state = draw_fine_state(jax.random.fold_in(splits[5], 71), 0)
    coarse_old = draw_coarse_old(jax.random.fold_in(splits[5], 71), 0)
    box_count = draw_box_count(jax.random.fold_in(splits[5], 71), 0)
    fine_links = draw_fine_links(jax.random.fold_in(splits[5], 71), 0)
    coarse_links = draw_coarse_links(jax.random.fold_in(splits[5], 71), 0)
    return dict(fine_state=fine_state, coarse_old=coarse_old, box_count=box_count, fine_links=fine_links, coarse_links=coarse_links)


GAMMA = 1.4
FLOOR = 0.1
WENO_EPS = 1e-06
TIME_STEP = 0.1
FIELD_ORDER = ((0, 1, 2, 3, 4), (0, 2, 1, 3, 4), (0, 3, 1, 2, 4))
FIELD_BACK = ((0, 1, 2, 3, 4), (0, 2, 1, 3, 4), (0, 2, 3, 1, 4))
OPPOSITE = (1, 0, 3, 2, 5, 4)

def primitives(conserved):
    density = jnp.maximum(conserved[:, 0], FLOOR)
    normal = conserved[:, 1] / density
    side_one = conserved[:, 2] / density
    side_two = conserved[:, 3] / density
    kinetic = 0.5 * density * (normal * normal + side_one * side_one + side_two * side_two)
    pressure = jnp.maximum((GAMMA - 1.0) * (conserved[:, 4] - kinetic), FLOOR)
    return jnp.stack([density, normal, side_one, side_two, pressure], axis=1)

def weno_face(far_left, near_left, centre, near_right, far_right):
    cand_a = (2.0 * far_left - 7.0 * near_left + 11.0 * centre) / 6.0
    cand_b = (-near_left + 5.0 * centre + 2.0 * near_right) / 6.0
    cand_c = (2.0 * centre + 5.0 * near_right - far_right) / 6.0
    smooth_a = 13.0 / 12.0 * (far_left - 2.0 * near_left + centre) ** 2 + 0.25 * (far_left - 4.0 * near_left + 3.0 * centre) ** 2
    smooth_b = 13.0 / 12.0 * (near_left - 2.0 * centre + near_right) ** 2 + 0.25 * (near_left - near_right) ** 2
    smooth_c = 13.0 / 12.0 * (centre - 2.0 * near_right + far_right) ** 2 + 0.25 * (3.0 * centre - 4.0 * near_right + far_right) ** 2
    weight_a = 0.1 / (WENO_EPS + smooth_a) ** 2
    weight_b = 0.6 / (WENO_EPS + smooth_b) ** 2
    weight_c = 0.3 / (WENO_EPS + smooth_c) ** 2
    return (weight_a * cand_a + weight_b * cand_b + weight_c * cand_c) / (weight_a + weight_b + weight_c)

def floor_faces(face_state):
    return jnp.concatenate([jnp.maximum(face_state[:, :1], FLOOR), face_state[:, 1:4], jnp.maximum(face_state[:, 4:], FLOOR)], axis=1)

def side_terms(face_state):
    density = face_state[:, 0]
    normal = face_state[:, 1]
    side_one = face_state[:, 2]
    side_two = face_state[:, 3]
    pressure = face_state[:, 4]
    energy = pressure / (GAMMA - 1.0) + 0.5 * density * (normal * normal + side_one * side_one + side_two * side_two)
    sound_speed = jnp.sqrt(GAMMA * pressure / density)
    conserved = [density, density * normal, density * side_one, density * side_two, energy]
    face_flux = [density * normal, density * normal * normal + pressure, density * normal * side_one, density * normal * side_two, normal * (energy + pressure)]
    return (density, normal, side_one, side_two, pressure, energy, sound_speed, conserved, face_flux)

def star_flux(terms, wave_speed, contact):
    density, normal, side_one, side_two, pressure, energy, sound_speed, conserved, face_flux = terms
    mass_rate = density * (wave_speed - normal)
    factor = mass_rate / (wave_speed - contact)
    star_state = [factor, factor * contact, factor * side_one, factor * side_two, factor * (energy / density + (contact - normal) * (contact + pressure / mass_rate))]
    return [face_flux[field_number] + wave_speed * (star_state[field_number] - conserved[field_number]) for field_number in range(5)]

def hllc_flux(left_state, right_state):
    left_terms = side_terms(left_state)
    right_terms = side_terms(right_state)
    speed_left = jnp.minimum(left_terms[1] - left_terms[6], right_terms[1] - right_terms[6])
    speed_right = jnp.maximum(left_terms[1] + left_terms[6], right_terms[1] + right_terms[6])
    mass_left = left_terms[0] * (speed_left - left_terms[1])
    mass_right = right_terms[0] * (speed_right - right_terms[1])
    contact = (right_terms[4] - left_terms[4] + mass_left * left_terms[1] - mass_right * right_terms[1]) / (mass_left - mass_right)
    star_left = star_flux(left_terms, speed_left, contact)
    star_right = star_flux(right_terms, speed_right, contact)
    result_list = []
    for field_number in range(5):
        chosen = jnp.where(speed_left >= 0.0, left_terms[8][field_number], jnp.where(contact >= 0.0, star_left[field_number], jnp.where(speed_right >= 0.0, star_right[field_number], right_terms[8][field_number])))
        result_list.append(chosen)
    return jnp.stack(result_list, axis=1)

def sweep_flux(extended):
    primitive_cells = primitives(extended)
    face_count = extended.shape[2] - 5
    pieces = [primitive_cells[:, :, start_cell:start_cell + face_count] for start_cell in range(6)]
    left_face = floor_faces(weno_face(pieces[0], pieces[1], pieces[2], pieces[3], pieces[4]))
    right_face = floor_faces(weno_face(pieces[5], pieces[4], pieces[3], pieces[2], pieces[1]))
    face_flux = hllc_flux(left_face, right_face)
    return face_flux[:, :, :-1] - face_flux[:, :, 1:]

def lay_along(field, direction):
    reordered = jnp.moveaxis(field, 2 + direction, 2)
    return reordered.reshape(reordered.shape[0], reordered.shape[1], reordered.shape[2], -1)

def back_from(field, direction):
    edge_cells = field.shape[2]
    cube = field.reshape(field.shape[0], field.shape[1], edge_cells, edge_cells, edge_cells)
    return jnp.moveaxis(cube, 2, 2 + direction)

def face_slabs(field):
    slot_count = field.shape[0]
    edge_cells = field.shape[2]
    slab_list = []
    for face_number in range(6):
        interior = lay_along(field, face_number // 2)
        if face_number % 2 == 0:
            layers = interior[:, :, :3]
        else:
            layers = interior[:, :, edge_cells - 3:]
        slab_list.append(layers.reshape(slot_count, 5, -1))
    return jnp.stack(slab_list, axis=1)

def rate_of(field, ghosts):
    slot_count = field.shape[0]
    edge_cells = field.shape[2]
    change_sum = jnp.zeros(field.shape, jnp.float32)
    for direction in range(3):
        interior = lay_along(field, direction)
        lower_ghost = ghosts[:, 2 * direction].reshape(slot_count, 5, 3, edge_cells * edge_cells)
        upper_ghost = ghosts[:, 2 * direction + 1].reshape(slot_count, 5, 3, edge_cells * edge_cells)
        extended = jnp.concatenate([lower_ghost, interior, upper_ghost], axis=2)
        extended = extended[:, np.array(FIELD_ORDER[direction])]
        change = sweep_flux(extended)[:, np.array(FIELD_BACK[direction])]
        change_sum = change_sum + back_from(change, direction)
    return change_sum

def minmod(first_diff, second_diff):
    return 0.5 * (jnp.sign(first_diff) + jnp.sign(second_diff)) * jnp.minimum(jnp.abs(first_diff), jnp.abs(second_diff))

def refine(region):
    interior = region[:, :, 1:-1, 1:-1, 1:-1]
    slope_x = minmod(region[:, :, 2:, 1:-1, 1:-1] - interior, interior - region[:, :, :-2, 1:-1, 1:-1])
    slope_y = minmod(region[:, :, 1:-1, 2:, 1:-1] - interior, interior - region[:, :, 1:-1, :-2, 1:-1])
    slope_z = minmod(region[:, :, 1:-1, 1:-1, 2:] - interior, interior - region[:, :, 1:-1, 1:-1, :-2])
    quarter = jnp.array([-0.25, 0.25], dtype=jnp.float32)

    def spread(values):
        return values[:, :, :, None, :, None, :, None]
    children = spread(interior) + spread(slope_x) * quarter.reshape(2, 1, 1, 1, 1) + spread(slope_y) * quarter.reshape(2, 1, 1) + spread(slope_z) * quarter
    shape_in = interior.shape
    return children.reshape(shape_in[0], shape_in[1], 2 * shape_in[2], 2 * shape_in[3], 2 * shape_in[4])

def coarse_ghosts(group_boxes, link_table):
    edge_cells = group_boxes.shape[2]
    slot_count = link_table.shape[0]
    zero_start = jnp.zeros((), jnp.int32)
    slab_list = []
    for face_number in range(6):
        direction = face_number // 2
        extent = tuple((4 if axis_number == direction else edge_cells // 2 + 2 for axis_number in range(3)))

        def cut_region(link_entry):
            starts = (link_entry[0].astype(jnp.int32), zero_start, link_entry[1].astype(jnp.int32), link_entry[2].astype(jnp.int32), link_entry[3].astype(jnp.int32))
            return lax.dynamic_slice(group_boxes, starts, (1, 5) + extent)[0]
        region = jax.vmap(cut_region)(link_table[:, face_number])
        children = refine(region)
        reordered = jnp.moveaxis(children, 2 + direction, 2)
        reordered = reordered.reshape(slot_count, 5, 4, edge_cells * edge_cells)
        if face_number % 2 == 0:
            layers = reordered[:, :, 1:]
        else:
            layers = reordered[:, :, :3]
        slab_list.append(layers.reshape(slot_count, 5, -1))
    return jnp.stack(slab_list, axis=1)

def ghost_position(face_links, slot_count):
    slot_ids = jnp.arange(slot_count, dtype=jnp.int32)[:, None]
    face_ids = jnp.arange(6, dtype=jnp.int32)[None, :]
    opposite = jnp.array(OPPOSITE, dtype=jnp.int32)[None, :]
    source = face_links // slot_count
    source_slot = face_links % slot_count
    block_id = jnp.where(source == 1, 0, jnp.where(source == 0, 1, 2)).astype(jnp.int32)
    linked_row = block_id * 6 * slot_count + source_slot * 6 + opposite
    coarse_row = 18 * slot_count + slot_ids * 6 + face_ids
    return jnp.where(face_links >= 0, linked_row, coarse_row).astype(jnp.int32)

def device_rate(own_boxes, boxes_below, boxes_above, face_links, group_boxes, link_table):
    slot_count = own_boxes.shape[0]
    ghost_table = jnp.concatenate([face_slabs(own_boxes).reshape(6 * slot_count, 5, -1), face_slabs(boxes_below).reshape(6 * slot_count, 5, -1), face_slabs(boxes_above).reshape(6 * slot_count, 5, -1), coarse_ghosts(group_boxes, link_table).reshape(6 * slot_count, 5, -1)], axis=0)
    ghosts = ghost_table[ghost_position(face_links, slot_count)]
    return rate_of(own_boxes, ghosts)

def section_rate(states, coarse_boxes, fine_links, coarse_links):

    def one_segment(segment):
        own_boxes = lax.dynamic_index_in_dim(states, segment, 0, keepdims=False)
        boxes_below = lax.dynamic_index_in_dim(states, jnp.maximum(segment - 1, 0), 0, keepdims=False)
        boxes_above = lax.dynamic_index_in_dim(states, jnp.minimum(segment + 1, SEGMENTS - 1), 0, keepdims=False)
        group_boxes = lax.dynamic_index_in_dim(coarse_boxes, segment, 0, keepdims=False)
        links_here = lax.dynamic_index_in_dim(fine_links, segment, 0, keepdims=False)
        coarse_here = lax.dynamic_index_in_dim(coarse_links, segment, 0, keepdims=False)
        return jax.vmap(device_rate, in_axes=(0, 0, 0, 0, None, 0))(own_boxes, boxes_below, boxes_above, links_here, group_boxes, coarse_here)
    return lax.map(one_segment, jnp.arange(SEGMENTS, dtype=jnp.int32))

def reference(fine_state, coarse_old, box_count, fine_links, coarse_links):
    states = fine_state.reshape(SEGMENTS, GROUP, MAXB, 5, B, B, B)
    old_boxes = coarse_old.reshape(SEGMENTS, GROUP, 5, B, B, B)
    first_rate = section_rate(states, old_boxes, fine_links, coarse_links)
    middle = states + TIME_STEP * first_rate
    second_rate = section_rate(middle, old_boxes, fine_links, coarse_links)
    updated = 0.5 * states + 0.5 * (middle + TIME_STEP * second_rate)
    updated = updated.reshape(SEGMENTS, GROUP, MAXB, 5, B * B * B)
    live_mask = jnp.arange(MAXB, dtype=jnp.int32)[None, None, :] < box_count[:, :, None]
    return jnp.where(live_mask[:, :, :, None, None], updated, jnp.zeros_like(updated))
```

```python
import jax
import jax.numpy as jnp
from jax import lax
from jax.experimental import pallas as pl
from jax.experimental.pallas import tpu as pltpu
from jax.sharding import PartitionSpec as P

FIELDS = 5
ROWS = 8
LANES = 128
GAMMA = 1.4
FLOOR = 0.1
EPS4 = 4e-06
TIME_STEP = 0.1


def to_tiles(boxes):
    slots, fields = boxes.shape[2], boxes.shape[3]
    parts = boxes.reshape(slots, fields, -1, LANES)
    return parts.transpose(1, 2, 0, 3).reshape(-1, LANES)


def from_tiles(tiles, shape):
    slots, fields = shape[2], shape[3]
    parts = tiles.reshape(fields, -1, slots, LANES)
    return parts.transpose(2, 0, 1, 3).reshape(shape)


def in_vmem(value):
    return pltpu.with_memory_space_constraint(value, pltpu.VMEM)


def exchange(value, partner):
    count, members = lax.axis_size("sfc"), lax.axis_size("sub")
    pairs = []
    for segment in range(count):
        for member in range(members):
            other, other_member = partner(segment, member, count, members)
            pairs.append((segment * members + member, other * members + other_member))
    return lax.ppermute(value, ("sfc", "sub"), pairs)


def even_partner(segment, member, count, members):
    other = segment ^ 1
    return (other, member) if other < count else (segment, member)


def odd_partner(segment, member, count, members):
    other = ((segment - 1) ^ 1) + 1
    if 0 < segment and other < count:
        return (other, member)
    other_member = member ^ 1
    return (segment, other_member) if other_member < members else (segment, member)


def group_shift(steps):
    def partner(segment, member, count, members):
        return (segment, (member + steps) % members)

    return partner


def positions():
    sub = lax.broadcasted_iota(jnp.int32, (ROWS, LANES), 0)
    lane = lax.broadcasted_iota(jnp.int32, (ROWS, LANES), 1)
    return sub, lane


def gather_lanes(value, index):
    return jnp.take_along_axis(value, index, axis=1, mode="promise_in_bounds")


def roll_lanes(value, steps):
    return pltpu.roll(value, steps % LANES, 1)


def roll_rows(value, steps):
    return pltpu.roll(value, steps % ROWS, 0)


def reciprocal(value):
    guess = pl.reciprocal(value, approx=True)
    return guess * (2.0 - value * guess)


def primitives(mass, mom_x, mom_y, mom_z, energy):
    density = jnp.maximum(mass, FLOOR)
    inverse = reciprocal(density)
    vel_x, vel_y, vel_z = mom_x * inverse, mom_y * inverse, mom_z * inverse
    kinetic = 0.5 * density * (vel_x * vel_x + vel_y * vel_y + vel_z * vel_z)
    pressure = jnp.maximum((GAMMA - 1.0) * (energy - kinetic), FLOOR)
    return [density, vel_x, vel_y, vel_z, pressure]


def load_primitives(ref, base=0):
    return primitives(*[ref[pl.ds(base + ROWS * f, ROWS), :] for f in range(FIELDS)])


def minmod(p, q):
    return jnp.maximum(jnp.minimum(p, q), 0.0) + jnp.minimum(jnp.maximum(p, q), 0.0)


def prepare(links_ref, corner_ref, count_ref, *refs):
    coarse_refs, (ghost_ref, pick_ref, live_ref, table, lines) = refs[:-5], refs[-5:]
    members = len(coarse_refs)
    sub, lane = positions()
    low = lane < 64
    y, z = (lane >> 3) & 7, lane & 7
    me = lax.axis_index("sub")
    odd_segment = lax.axis_index("sfc") & 1

    for m in range(members):
        for j in range(4):
            table[m * 16 + j, 0:FIELDS, :] = coarse_refs[m][pl.ds(j, FIELDS, stride=4), :]
    for m in range(members):
        cells = [table[m * 16 + j] for j in range(4)]
        halves = [roll_lanes(c, 64) for c in cells]
        for j in range(4):
            u = cells[j]
            up = jnp.where(low, halves[j], halves[min(j + 1, 3)])
            down = jnp.where(low, halves[max(j - 1, 0)], halves[j])
            table[m * 16 + 4 + j] = 0.25 * minmod(up - u, u - down)
            table[m * 16 + 8 + j] = 0.25 * minmod(roll_lanes(u, -8) - u, u - roll_lanes(u, 8))
            table[m * 16 + 12 + j] = 0.25 * minmod(roll_lanes(u, -1) - u, u - roll_lanes(u, 1))

    sign_x = jnp.where(low, -1.0, 1.0)
    sign_y = jnp.where((y & 1) == 0, -1.0, 1.0)
    sign_z = jnp.where((z & 1) == 0, -1.0, 1.0)
    spread = (y >> 1) * 8 + (z >> 1)

    def children(slot, face, j):
        direction, minus = face // 2, face % 2 == 0
        start = [corner_ref[slot, face * 4 + 1 + a] + (-1 if minus and a == direction else 1) for a in range(3)]
        owner = me - corner_ref[slot, face * 4]
        owner = jnp.where(owner < 0, owner + members, owner)
        along = start[0] + j
        index = (spread + ((along & 1) * 64 + start[1] * 8 + start[2])) & (LANES - 1)
        row = owner * 16 + (along >> 1)
        parts = [gather_lanes(table[row + 4 * q], index) for q in range(4)]
        return parts[0] + sign_x * parts[1] + sign_y * parts[2] + sign_z * parts[3]

    for direction in range(3):
        for slot in range(2):
            for j in range(4):
                minus, plus = 2 * direction, 2 * direction + 1
                if direction == 0:
                    value = children(slot, minus if j >= 2 else plus, j)
                else:
                    lower = (y if direction == 1 else z) < 4
                    value = jnp.where(lower, children(slot, plus, j), children(slot, minus, j))
                rows = pl.ds(direction * 40 + j * 2 + slot, FIELDS, stride=ROWS)
                lines[rows, :] = value[0:FIELDS, :]
        made = load_primitives(lines, direction * 40)
        for f in range(FIELDS):
            ghost_ref[pl.ds(direction * 40 + f * ROWS, ROWS), :] = made[f]

    def choice(slot, face):
        link = links_ref[slot, face]
        offset = link >> 1
        below = jnp.where(offset == 0, 1, 0)
        block = jnp.where(offset == 1, 0, jnp.where(below == odd_segment, 1, 2))
        swapped = (link & 1) ^ slot
        return jnp.where(link < 0, 0, 1 + block * 2 + swapped)

    first = (sub & 1) == 0
    for direction in range(3):
        lower = (sub < 4) if direction == 0 else ((y if direction == 1 else z) < 4)
        minus = jnp.where(first, choice(0, 2 * direction), choice(1, 2 * direction))
        plus = jnp.where(first, choice(0, 2 * direction + 1), choice(1, 2 * direction + 1))
        pick_ref[pl.ds(direction * ROWS, ROWS), :] = jnp.where(lower, plus, minus)
    live_ref[...] = jnp.where((sub & 1) < count_ref[0, 0], 1, 0)


def weno(p):
    e = [p[k + 1] - p[k] for k in range(5)]
    d = [e[k + 1] - e[k] for k in range(4)]
    q = [(13.0 / 3.0) * (dk * dk) + EPS4 for dk in d]
    t1, t2, t3 = 3.0 * e[1], 3.0 * e[2], 3.0 * e[3]
    middle = 0.5 * (p[2] + p[3])

    def side(qa, sa, qb, sb, qc, sc, da, db, dc):
        a, b, c = qa + sa * sa, qb + sb * sb, qc + sc * sc
        bc, ac, ab = b * c, a * c, a * b
        wa, wb, wc = bc * bc, 6.0 * (ac * ac), 3.0 * (ab * ab)
        top = wa * (3.0 * db - 2.0 * da) + wb * db + wc * dc
        return middle - top * reciprocal(6.0 * (wa + wb + wc))

    left = side(q[0], t1 - e[0], q[1], e[1] + e[2], q[2], e[3] - t2, d[0], d[1], d[2])
    right = side(q[3], e[4] - t3, q[2], e[2] + e[3], q[1], t2 - e[1], d[3], d[2], d[1])
    return left, right


def hllc(left, right):
    rl, ul, vl, wl, pl_ = jnp.maximum(left[0], FLOOR), left[1], left[2], left[3], jnp.maximum(left[4], FLOOR)
    rr, ur, vr, wr, pr = jnp.maximum(right[0], FLOOR), right[1], right[2], right[3], jnp.maximum(right[4], FLOOR)
    gl, gr = GAMMA * pl_, GAMMA * pr
    cl, cr = gl * lax.rsqrt(gl * rl), gr * lax.rsqrt(gr * rr)
    speed_left = jnp.minimum(ul - cl, ur - cr)
    speed_right = jnp.maximum(ul + cl, ur + cr)
    ml, mr = rl * (speed_left - ul), rr * (speed_right - ur)
    contact = (pr - pl_ + ml * ul - mr * ur) * reciprocal(ml - mr)
    from_left = (speed_left >= 0.0) | (contact >= 0.0)
    r = jnp.where(from_left, rl, rr)
    u = jnp.where(from_left, ul, ur)
    v = jnp.where(from_left, vl, vr)
    w = jnp.where(from_left, wl, wr)
    p = jnp.where(from_left, pl_, pr)
    s = jnp.where(from_left, speed_left, speed_right)
    m = jnp.where(from_left, ml, mr)
    star = (speed_left < 0.0) & ((contact >= 0.0) | (speed_right >= 0.0))
    energy = p * (1.0 / (GAMMA - 1.0)) + 0.5 * r * (u * u + v * v + w * w)
    inverse = reciprocal(s - contact)
    star_p = p + m * (contact - u)
    star_e = ((s - u) * energy - p * u + star_p * contact) * inverse
    density = jnp.where(star, m * inverse, r)
    normal = jnp.where(star, contact, u)
    pressure = jnp.where(star, star_p, p)
    energy = jnp.where(star, star_e, energy)
    mass = density * normal
    return [mass, mass * normal + pressure, mass * v, mass * w, normal * (energy + pressure)]


def rate(own, blocks, ghost_ref, pick_ref):
    sub, lane = positions()
    low = lane < 64
    y, z = (lane >> 3) & 7, lane & 7
    half = lane & 64
    x = (sub >> 1) * 2 + (lane >> 6)
    even_row = (sub & 1) == 0

    candidates = []
    for block in blocks:
        candidates.append(block)
        candidates.append([jnp.where(even_row, roll_rows(v, -1), roll_rows(v, 1)) for v in block])
    ghosts = []
    for direction in range(3):
        pick = pick_ref[pl.ds(direction * ROWS, ROWS), :]
        wanted = [pick == c + 1 for c in range(len(candidates))]
        chosen = []
        for f in range(FIELDS):
            value = ghost_ref[pl.ds(direction * 40 + f * ROWS, ROWS), :]
            for c, candidate in enumerate(candidates):
                value = jnp.where(wanted[c], candidate[f], value)
            chosen.append(value)
        ghosts.append(chosen)

    def shifts_x(value):
        other = roll_lanes(value, 64)
        minus2, plus2 = roll_rows(other, 2), roll_rows(other, -2)
        return {
            -3: jnp.where(low, roll_rows(other, 4), minus2),
            -2: roll_rows(value, 2),
            -1: jnp.where(low, minus2, other),
            0: value,
            1: jnp.where(low, other, plus2),
            2: roll_rows(value, -2),
        }

    def index_along(direction, steps):
        if direction == 1:
            return half | (((y + steps) & 7) << 3) | z
        return half | (y << 3) | ((z + steps) & 7)

    ninth_x = low & (sub < 2)
    is_y = (lane >= 64) & (lane < 80)
    part, inner = ((lane >> 3) & 1) << 6, lane & 7

    def ninth_index(layer):
        return jnp.where(is_y, part | (layer << 3) | inner, part | (inner << 3) | layer)

    mains = [[], [], []]
    ninths = []
    for f in range(FIELDS):
        own_x, ghost_x = shifts_x(own[f]), shifts_x(ghosts[0][f])
        cells = []
        for k in range(6):
            s = k - 3
            outside = (x + s < 0) | (x + s > 7)
            cells.append(jnp.where(outside, ghost_x[s], own_x[s]) if s else own[f])
        mains[0].append(cells)
        for direction in (1, 2):
            place = y if direction == 1 else z
            cells = []
            for k in range(6):
                s = k - 3
                if s == 0:
                    cells.append(own[f])
                    continue
                outside = (place >= 8 + s) if s < 0 else (place < s)
                merged = jnp.where(outside, ghosts[direction][f], own[f])
                cells.append(gather_lanes(merged, index_along(direction, s)))
            mains[direction].append(cells)
        cells = []
        for k in range(6):
            if k < 3:
                beside = gather_lanes(own[f], ninth_index(5 + k))
                value = own_x[k - 3]
            else:
                index = ninth_index(k - 3)
                beside = jnp.where(is_y, gather_lanes(ghosts[1][f], index), gather_lanes(ghosts[2][f], index))
                value = ghost_x[k - 3]
            cells.append(jnp.where(ninth_x, value, beside))
        ninths.append(cells)

    orders = ((0, 1, 2, 3, 4), (0, 2, 1, 3, 4), (0, 3, 1, 2, 4))
    fluxes = []
    for direction in range(3):
        states = [weno(mains[direction][f]) for f in orders[direction]]
        fluxes.append(hllc([st[0] for st in states], [st[1] for st in states]))
    states = [weno(ninths[f]) for f in range(FIELDS)]
    is_z = lane >= 80

    def turned(side):
        values = [st[side] for st in states]
        normal = jnp.where(is_y, values[2], jnp.where(is_z, values[3], values[1]))
        one = jnp.where(is_y | is_z, values[1], values[2])
        two = jnp.where(is_z, values[2], values[3])
        return [values[0], normal, one, two, values[4]]

    last = hllc(turned(0), turned(1))

    back_index = (
        None,
        64 + ((lane >> 6) << 3) + z,
        80 + ((lane >> 6) << 3) + y,
    )
    backs = ((0, 1, 2, 3, 4), (0, 2, 1, 3, 4), (0, 2, 3, 1, 4))
    total = [None] * FIELDS
    for direction in range(3):
        for place in range(FIELDS):
            flux = fluxes[direction][place]
            if direction == 0:
                merged = roll_lanes(jnp.where(x == 0, last[place], flux), 64)
                after = jnp.where(low, merged, roll_rows(merged, -2))
            else:
                end = (y if direction == 1 else z) == 7
                after = jnp.where(
                    end,
                    gather_lanes(last[place], back_index[direction]),
                    gather_lanes(flux, index_along(direction, 1)),
                )
            change = flux - after
            f = backs[direction].index(place)
            total[f] = change if total[f] is None else total[f] + change
    return total


def first_stage(own_ref, even_ref, odd_ref, ghost_ref, pick_ref, out_ref):
    own = load_primitives(own_ref)
    change = rate(own, [own, load_primitives(even_ref), load_primitives(odd_ref)], ghost_ref, pick_ref)
    for f in range(FIELDS):
        rows = pl.ds(f * ROWS, ROWS)
        out_ref[rows, :] = own_ref[rows, :] + TIME_STEP * change[f]


def second_stage(start_ref, own_ref, even_ref, odd_ref, ghost_ref, pick_ref, live_ref, out_ref):
    own = load_primitives(own_ref)
    change = rate(own, [own, load_primitives(even_ref), load_primitives(odd_ref)], ghost_ref, pick_ref)
    live = live_ref[...] != 0
    for f in range(FIELDS):
        rows = pl.ds(f * ROWS, ROWS)
        value = 0.5 * start_ref[rows, :] + 0.5 * (own_ref[rows, :] + TIME_STEP * change[f])
        out_ref[rows, :] = jnp.where(live, value, 0.0)


def vmem_spec():
    return pl.BlockSpec(memory_space=pltpu.VMEM)


def smem_spec():
    return pl.BlockSpec(memory_space=pltpu.SMEM)


def body(fine_state, coarse_old, box_count, fine_links, coarse_links):
    members = lax.axis_size("sub")
    tile_rows = FIELDS * ROWS
    start = to_tiles(fine_state)
    coarse = coarse_old.reshape(-1, LANES)

    even = exchange(start, even_partner)
    odd = exchange(start, odd_partner)
    group = [coarse] + [exchange(coarse, group_shift(r)) for r in range(1, members)]

    ghosts, picks, live = pl.pallas_call(
        prepare,
        out_shape=(
            pltpu.VMEM((3 * tile_rows, LANES), jnp.float32),
            pltpu.VMEM((3 * ROWS, LANES), jnp.int32),
            pltpu.VMEM((ROWS, LANES), jnp.int32),
        ),
        in_specs=[smem_spec()] * 3 + [vmem_spec()] * members,
        out_specs=(vmem_spec(),) * 3,
        scratch_shapes=[
            pltpu.VMEM((members * 16, ROWS, LANES), jnp.float32),
            pltpu.VMEM((3 * tile_rows, LANES), jnp.float32),
        ],
        name="prepare",
    )(
        fine_links.reshape(2, 6),
        coarse_links.reshape(2, 24),
        box_count,
        *[in_vmem(c) for c in group],
    )

    middle = pl.pallas_call(
        first_stage,
        out_shape=pltpu.VMEM((tile_rows, LANES), jnp.float32),
        in_specs=[vmem_spec()] * 5,
        out_specs=vmem_spec(),
        name="first_stage",
    )(in_vmem(start), in_vmem(even), in_vmem(odd), in_vmem(ghosts), in_vmem(picks))

    even = exchange(middle, even_partner)
    odd = exchange(middle, odd_partner)
    result = pl.pallas_call(
        second_stage,
        out_shape=jax.ShapeDtypeStruct((tile_rows, LANES), jnp.float32),
        in_specs=[vmem_spec()] * 7,
        out_specs=vmem_spec(),
        name="second_stage",
    )(
        in_vmem(start),
        in_vmem(middle),
        in_vmem(even),
        in_vmem(odd),
        in_vmem(ghosts),
        in_vmem(picks),
        in_vmem(live),
    )
    return from_tiles(result, fine_state.shape)


def solution(mesh):
    placed = (
        P("sfc", "sub", None, None, None),
        P("sfc", "sub", None, None),
        P("sfc", "sub"),
        P("sfc", "sub", None, None),
        P("sfc", "sub", None, None, None),
    )
    return jax.shard_map(
        body,
        mesh=mesh,
        in_specs=placed,
        out_specs=P("sfc", "sub", None, None, None),
        check_vma=False,
    )
```

```python
import jax
import jax.numpy as jnp
from jax import lax
from jax.experimental import pallas as pl
from jax.experimental.pallas import tpu as pltpu
from jax.sharding import PartitionSpec as P

FIELDS = 5
ROWS = 8
LANES = 128
GAMMA = 1.4
FLOOR = 0.1
EPS4 = 4e-06
TIME_STEP = 0.1


def to_tiles(boxes):
    slots, fields = boxes.shape[2], boxes.shape[3]
    parts = boxes.reshape(slots, fields, -1, LANES)
    return parts.transpose(1, 2, 0, 3).reshape(-1, LANES)


def from_tiles(tiles, shape):
    slots, fields = shape[2], shape[3]
    parts = tiles.reshape(fields, -1, slots, LANES)
    return parts.transpose(2, 0, 1, 3).reshape(shape)


def in_vmem(value):
    return pltpu.with_memory_space_constraint(value, pltpu.VMEM)


def in_smem(value):
    return pltpu.with_memory_space_constraint(value, pltpu.SMEM)


def exchange(value, partner):
    count, members = lax.axis_size("sfc"), lax.axis_size("sub")
    pairs = []
    for segment in range(count):
        for member in range(members):
            other, other_member = partner(segment, member, count, members)
            pairs.append((segment * members + member, other * members + other_member))
    return lax.ppermute(value, ("sfc", "sub"), pairs)


def even_partner(segment, member, count, members):
    other = segment ^ 1
    return (other, member) if other < count else (segment, member)


def odd_partner(segment, member, count, members):
    other = ((segment - 1) ^ 1) + 1
    if 0 < segment and other < count:
        return (other, member)
    other_member = member ^ 1
    return (segment, other_member) if other_member < members else (segment, member)


def group_shift(steps):
    def partner(segment, member, count, members):
        return (segment, (member + steps) % members)

    return partner


def positions():
    sub = lax.broadcasted_iota(jnp.int32, (ROWS, LANES), 0)
    lane = lax.broadcasted_iota(jnp.int32, (ROWS, LANES), 1)
    return sub, lane


def gather_lanes(value, index):
    return jnp.take_along_axis(value, index, axis=1, mode="promise_in_bounds")


def roll_lanes(value, steps):
    return pltpu.roll(value, steps % LANES, 1)


def roll_rows(value, steps):
    return pltpu.roll(value, steps % ROWS, 0)


def reciprocal(value):
    guess = pl.reciprocal(value, approx=True)
    return guess * (2.0 - value * guess)


def primitives(mass, mom_x, mom_y, mom_z, energy):
    density = jnp.maximum(mass, FLOOR)
    inverse = reciprocal(density)
    vel_x, vel_y, vel_z = mom_x * inverse, mom_y * inverse, mom_z * inverse
    kinetic = 0.5 * density * (vel_x * vel_x + vel_y * vel_y + vel_z * vel_z)
    pressure = jnp.maximum((GAMMA - 1.0) * (energy - kinetic), FLOOR)
    return [density, vel_x, vel_y, vel_z, pressure]


def load_primitives(ref, base=0):
    return primitives(*[ref[pl.ds(base + ROWS * f, ROWS), :] for f in range(FIELDS)])


def minmod(p, q):
    return jnp.maximum(jnp.minimum(p, q), 0.0) + jnp.minimum(jnp.maximum(p, q), 0.0)


def slopes(table, base, low):
    cells = [table[base + j] for j in range(4)]
    halves = [roll_lanes(c, 64) for c in cells]
    for j in range(4):
        u = cells[j]
        up = jnp.where(low, halves[j], halves[min(j + 1, 3)])
        down = jnp.where(low, halves[max(j - 1, 0)], halves[j])
        table[base + 4 + j] = 0.25 * minmod(up - u, u - down)
        table[base + 8 + j] = 0.25 * minmod(roll_lanes(u, -8) - u, u - roll_lanes(u, 8))
        table[base + 12 + j] = 0.25 * minmod(roll_lanes(u, -1) - u, u - roll_lanes(u, 1))


def spread_fields(table, base, coarse_ref):
    for j in range(4):
        for f in range(FIELDS):
            table[base + j, f : f + 1, :] = coarse_ref[f * 4 + j]


def read_links(links_in, corner_in, coarse_in, start_in, pick_ref, table, corner_ref, own_ref, links_ref, coarse_ref, sems):
    copies = (links_in, links_ref), (corner_in, corner_ref), (coarse_in, coarse_ref), (start_in, own_ref)
    fetches = [pltpu.make_async_copy(src, dst, sems.at[i]) for i, (src, dst) in enumerate(copies)]
    for fetch in fetches:
        fetch.start()
    sub, lane = positions()
    y, z = (lane >> 3) & 7, lane & 7
    odd_segment = lax.axis_index("sfc") & 1
    for fetch in fetches:
        fetch.wait()
    spread_fields(table, 0, coarse_ref)
    slopes(table, 0, lane < 64)

    def choice(slot, face):
        link = links_ref[slot, face]
        offset = link >> 1
        below = jnp.where(offset == 0, 1, 0)
        block = jnp.where(offset == 1, 0, jnp.where(below == odd_segment, 1, 2))
        swapped = (link & 1) ^ slot
        return jnp.where(link < 0, 0, 1 + block * 2 + swapped)

    first = (sub & 1) == 0
    for direction in range(3):
        lower = (sub < 4) if direction == 0 else ((y if direction == 1 else z) < 4)
        minus = jnp.where(first, choice(0, 2 * direction), choice(1, 2 * direction))
        plus = jnp.where(first, choice(0, 2 * direction + 1), choice(1, 2 * direction + 1))
        pick_ref[pl.ds(direction * ROWS, ROWS), :] = jnp.where(lower, plus, minus)


def interpolate(corner_ref, own_table, *refs):
    coarse_refs, (ghost_ref, table, lines) = refs[:-3], refs[-3:]
    members = len(coarse_refs) + 1
    sub, lane = positions()
    low = lane < 64
    y, z = (lane >> 3) & 7, lane & 7
    me = lax.axis_index("sub")
    table[0:16] = own_table[...]
    for m, coarse_ref in enumerate(coarse_refs):
        spread_fields(table, (m + 1) * 16, coarse_ref)
        slopes(table, (m + 1) * 16, low)

    sign_x = jnp.where(low, -1.0, 1.0)
    sign_y = jnp.where((y & 1) == 0, -1.0, 1.0)
    sign_z = jnp.where((z & 1) == 0, -1.0, 1.0)
    spread = (y >> 1) * 8 + (z >> 1)

    def children(slot, face, j):
        direction, minus = face // 2, face % 2 == 0
        start = [corner_ref[slot, 1 + a, face] + (-1 if minus and a == direction else 1) for a in range(3)]
        owner = me - corner_ref[slot, 0, face]
        owner = jnp.where(owner < 0, owner + members, owner)
        along = start[0] + j
        index = (spread + ((along & 1) * 64 + start[1] * 8 + start[2])) & (LANES - 1)
        row = owner * 16 + (along >> 1)
        parts = [gather_lanes(table[row + 4 * q], index) for q in range(4)]
        return parts[0] + sign_x * parts[1] + sign_y * parts[2] + sign_z * parts[3]

    for direction in range(3):
        for slot in range(2):
            for j in range(4):
                minus, plus = 2 * direction, 2 * direction + 1
                if direction == 0:
                    value = children(slot, minus if j >= 2 else plus, j)
                else:
                    lower = (y if direction == 1 else z) < 4
                    value = jnp.where(lower, children(slot, plus, j), children(slot, minus, j))
                rows = pl.ds(direction * 40 + j * 2 + slot, FIELDS, stride=ROWS)
                lines[rows, :] = value[0:FIELDS, :]
        made = load_primitives(lines, direction * 40)
        for f in range(FIELDS):
            ghost_ref[pl.ds(direction * 40 + f * ROWS, ROWS), :] = made[f]


def weno(p):
    e = [p[k + 1] - p[k] for k in range(5)]
    d = [e[k + 1] - e[k] for k in range(4)]
    q = [(13.0 / 3.0) * (dk * dk) + EPS4 for dk in d]
    t1, t2, t3 = 3.0 * e[1], 3.0 * e[2], 3.0 * e[3]
    middle = 0.5 * (p[2] + p[3])

    def side(qa, sa, qb, sb, qc, sc, da, db, dc):
        a, b, c = qa + sa * sa, qb + sb * sb, qc + sc * sc
        bc, ac, ab = b * c, a * c, a * b
        wa, wb, wc = bc * bc, 6.0 * (ac * ac), 3.0 * (ab * ab)
        top = wa * (3.0 * db - 2.0 * da) + wb * db + wc * dc
        return middle - top * reciprocal(6.0 * (wa + wb + wc))

    left = side(q[0], t1 - e[0], q[1], e[1] + e[2], q[2], e[3] - t2, d[0], d[1], d[2])
    right = side(q[3], e[4] - t3, q[2], e[2] + e[3], q[1], t2 - e[1], d[3], d[2], d[1])
    return left, right


def hllc(left, right):
    rl, ul, vl, wl, pl_ = jnp.maximum(left[0], FLOOR), left[1], left[2], left[3], jnp.maximum(left[4], FLOOR)
    rr, ur, vr, wr, pr = jnp.maximum(right[0], FLOOR), right[1], right[2], right[3], jnp.maximum(right[4], FLOOR)
    gl, gr = GAMMA * pl_, GAMMA * pr
    cl, cr = gl * lax.rsqrt(gl * rl), gr * lax.rsqrt(gr * rr)
    speed_left = jnp.minimum(ul - cl, ur - cr)
    speed_right = jnp.maximum(ul + cl, ur + cr)
    ml, mr = rl * (speed_left - ul), rr * (speed_right - ur)
    contact = (pr - pl_ + ml * ul - mr * ur) * reciprocal(ml - mr)
    from_left = (speed_left >= 0.0) | (contact >= 0.0)
    r = jnp.where(from_left, rl, rr)
    u = jnp.where(from_left, ul, ur)
    v = jnp.where(from_left, vl, vr)
    w = jnp.where(from_left, wl, wr)
    p = jnp.where(from_left, pl_, pr)
    s = jnp.where(from_left, speed_left, speed_right)
    m = jnp.where(from_left, ml, mr)
    star = (speed_left < 0.0) & ((contact >= 0.0) | (speed_right >= 0.0))
    energy = p * (1.0 / (GAMMA - 1.0)) + 0.5 * r * (u * u + v * v + w * w)
    inverse = reciprocal(s - contact)
    star_p = p + m * (contact - u)
    star_e = ((s - u) * energy - p * u + star_p * contact) * inverse
    density = jnp.where(star, m * inverse, r)
    normal = jnp.where(star, contact, u)
    pressure = jnp.where(star, star_p, p)
    energy = jnp.where(star, star_e, energy)
    mass = density * normal
    return [mass, mass * normal + pressure, mass * v, mass * w, normal * (energy + pressure)]


def rate(own, blocks, ghost_ref, pick_ref):
    sub, lane = positions()
    low = lane < 64
    y, z = (lane >> 3) & 7, lane & 7
    half = lane & 64
    x = (sub >> 1) * 2 + (lane >> 6)
    even_row = (sub & 1) == 0

    candidates = []
    for block in blocks:
        candidates.append(block)
        candidates.append([jnp.where(even_row, roll_rows(v, -1), roll_rows(v, 1)) for v in block])
    ghosts = []
    for direction in range(3):
        pick = pick_ref[pl.ds(direction * ROWS, ROWS), :]
        wanted = [pick == c + 1 for c in range(len(candidates))]
        chosen = []
        for f in range(FIELDS):
            value = ghost_ref[pl.ds(direction * 40 + f * ROWS, ROWS), :]
            for c, candidate in enumerate(candidates):
                value = jnp.where(wanted[c], candidate[f], value)
            chosen.append(value)
        ghosts.append(chosen)

    def shifts_x(value):
        other = roll_lanes(value, 64)
        minus2, plus2 = roll_rows(other, 2), roll_rows(other, -2)
        return {
            -3: jnp.where(low, roll_rows(other, 4), minus2),
            -2: roll_rows(value, 2),
            -1: jnp.where(low, minus2, other),
            0: value,
            1: jnp.where(low, other, plus2),
            2: roll_rows(value, -2),
        }

    def index_along(direction, steps):
        if direction == 1:
            return half | (((y + steps) & 7) << 3) | z
        return half | (y << 3) | ((z + steps) & 7)

    ninth_x = low & (sub < 2)
    is_y = (lane >= 64) & (lane < 80)
    part, inner = ((lane >> 3) & 1) << 6, lane & 7

    def ninth_index(layer):
        return jnp.where(is_y, part | (layer << 3) | inner, part | (inner << 3) | layer)

    mains = [[], [], []]
    ninths = []
    for f in range(FIELDS):
        own_x, ghost_x = shifts_x(own[f]), shifts_x(ghosts[0][f])
        cells = []
        for k in range(6):
            s = k - 3
            outside = (x + s < 0) | (x + s > 7)
            cells.append(jnp.where(outside, ghost_x[s], own_x[s]) if s else own[f])
        mains[0].append(cells)
        for direction in (1, 2):
            place = y if direction == 1 else z
            cells = []
            for k in range(6):
                s = k - 3
                if s == 0:
                    cells.append(own[f])
                    continue
                outside = (place >= 8 + s) if s < 0 else (place < s)
                merged = jnp.where(outside, ghosts[direction][f], own[f])
                cells.append(gather_lanes(merged, index_along(direction, s)))
            mains[direction].append(cells)
        cells = []
        for k in range(6):
            if k < 3:
                beside = gather_lanes(own[f], ninth_index(5 + k))
                value = own_x[k - 3]
            else:
                index = ninth_index(k - 3)
                beside = jnp.where(is_y, gather_lanes(ghosts[1][f], index), gather_lanes(ghosts[2][f], index))
                value = ghost_x[k - 3]
            cells.append(jnp.where(ninth_x, value, beside))
        ninths.append(cells)

    orders = ((0, 1, 2, 3, 4), (0, 2, 1, 3, 4), (0, 3, 1, 2, 4))
    fluxes = []
    for direction in range(3):
        states = [weno(mains[direction][f]) for f in orders[direction]]
        fluxes.append(hllc([st[0] for st in states], [st[1] for st in states]))
    states = [weno(ninths[f]) for f in range(FIELDS)]
    is_z = lane >= 80

    def turned(side):
        values = [st[side] for st in states]
        normal = jnp.where(is_y, values[2], jnp.where(is_z, values[3], values[1]))
        one = jnp.where(is_y | is_z, values[1], values[2])
        two = jnp.where(is_z, values[2], values[3])
        return [values[0], normal, one, two, values[4]]

    last = hllc(turned(0), turned(1))

    back_index = (
        None,
        64 + ((lane >> 6) << 3) + z,
        80 + ((lane >> 6) << 3) + y,
    )
    backs = ((0, 1, 2, 3, 4), (0, 2, 1, 3, 4), (0, 2, 3, 1, 4))
    total = [None] * FIELDS
    for direction in range(3):
        for place in range(FIELDS):
            flux = fluxes[direction][place]
            if direction == 0:
                merged = roll_lanes(jnp.where(x == 0, last[place], flux), 64)
                after = jnp.where(low, merged, roll_rows(merged, -2))
            else:
                end = (y if direction == 1 else z) == 7
                after = jnp.where(
                    end,
                    gather_lanes(last[place], back_index[direction]),
                    gather_lanes(flux, index_along(direction, 1)),
                )
            change = flux - after
            f = backs[direction].index(place)
            total[f] = change if total[f] is None else total[f] + change
    return total


def first_stage(own_ref, odd_ref, even_ref, ghost_ref, pick_ref, out_ref):
    own = load_primitives(own_ref)
    change = rate(own, [own, load_primitives(even_ref), load_primitives(odd_ref)], ghost_ref, pick_ref)
    for f in range(FIELDS):
        rows = pl.ds(f * ROWS, ROWS)
        out_ref[rows, :] = own_ref[rows, :] + TIME_STEP * change[f]


def second_stage(start_ref, own_ref, odd_ref, even_ref, ghost_ref, pick_ref, count_ref, out_ref):
    own = load_primitives(own_ref)
    change = rate(own, [own, load_primitives(even_ref), load_primitives(odd_ref)], ghost_ref, pick_ref)
    sub, _ = positions()
    live = (sub & 1) < count_ref[0, 0]
    for f in range(FIELDS):
        rows = pl.ds(f * ROWS, ROWS)
        value = 0.5 * start_ref[rows, :] + 0.5 * (own_ref[rows, :] + TIME_STEP * change[f])
        out_ref[rows, :] = jnp.where(live, value, 0.0)


def vmem_spec():
    return pl.BlockSpec(memory_space=pltpu.VMEM)


def smem_spec():
    return pl.BlockSpec(memory_space=pltpu.SMEM)


def hbm_spec():
    return pl.BlockSpec(memory_space=pltpu.HBM)


def body(fine_state, coarse_old, box_count, fine_links, coarse_links):
    members = lax.axis_size("sub")
    tile_rows = FIELDS * ROWS
    start = to_tiles(fine_state)
    coarse = coarse_old.transpose(0, 2, 1, 3).reshape(FIELDS, 1, -1, LANES).transpose(0, 2, 1, 3)
    coarse = coarse.reshape(-1, 1, LANES)

    odd = exchange(start, odd_partner)
    group = [exchange(coarse, group_shift(r)) for r in range(1, members)]

    picks, table, corners, own = pl.pallas_call(
        read_links,
        out_shape=(
            pltpu.VMEM((3 * ROWS, LANES), jnp.int32),
            pltpu.VMEM((16, ROWS, LANES), jnp.float32),
            pltpu.SMEM((2, 4, 6), jnp.int32),
            pltpu.VMEM((tile_rows, LANES), jnp.float32),
        ),
        in_specs=[hbm_spec()] * 4,
        out_specs=(vmem_spec(), vmem_spec(), smem_spec(), vmem_spec()),
        scratch_shapes=[
            pltpu.SMEM((2, 6), jnp.int32),
            pltpu.VMEM((FIELDS * 4, 1, LANES), jnp.float32),
            pltpu.SemaphoreType.DMA((4,)),
        ],
        name="read_links",
    )(
        fine_links.reshape(2, 6),
        coarse_links.transpose(0, 1, 2, 4, 3).reshape(2, 4, 6),
        coarse,
        start,
    )
    even = exchange(start, even_partner)
    ghosts = pl.pallas_call(
        interpolate,
        out_shape=pltpu.VMEM((3 * tile_rows, LANES), jnp.float32),
        in_specs=[smem_spec()] + [vmem_spec()] * members,
        out_specs=vmem_spec(),
        scratch_shapes=[
            pltpu.VMEM((members * 16, ROWS, LANES), jnp.float32),
            pltpu.VMEM((3 * tile_rows, LANES), jnp.float32),
        ],
        name="interpolate",
        cost_estimate=pl.CostEstimate(flops=10000000000, bytes_accessed=10000000000, transcendentals=0),
    )(in_smem(corners), in_vmem(table), *[in_vmem(c) for c in group])

    middle = pl.pallas_call(
        first_stage,
        out_shape=pltpu.VMEM((tile_rows, LANES), jnp.float32),
        in_specs=[vmem_spec()] * 5,
        out_specs=vmem_spec(),
        name="first_stage",
    )(in_vmem(own), in_vmem(odd), in_vmem(even), in_vmem(ghosts), in_vmem(picks))

    even = exchange(middle, even_partner)
    odd = exchange(middle, odd_partner)
    result = pl.pallas_call(
        second_stage,
        out_shape=jax.ShapeDtypeStruct((tile_rows, LANES), jnp.float32),
        in_specs=[vmem_spec()] * 6 + [smem_spec()],
        out_specs=vmem_spec(),
        name="second_stage",
    )(
        in_vmem(own),
        in_vmem(middle),
        in_vmem(odd),
        in_vmem(even),
        in_vmem(ghosts),
        in_vmem(picks),
        box_count,
    )
    return from_tiles(result, fine_state.shape)


def solution(mesh):
    placed = (
        P("sfc", "sub", None, None, None),
        P("sfc", "sub", None, None),
        P("sfc", "sub"),
        P("sfc", "sub", None, None),
        P("sfc", "sub", None, None, None),
    )
    return jax.shard_map(
        body,
        mesh=mesh,
        in_specs=placed,
        out_specs=P("sfc", "sub", None, None, None),
        check_vma=False,
    )
```

```python
import jax
import jax.numpy as jnp
from jax import lax
from jax.experimental import pallas as pl
from jax.experimental.pallas import tpu as pltpu
from jax.sharding import PartitionSpec as P

FIELDS = 5
ROWS = 8
LANES = 128
GAMMA = 1.4
FLOOR = 0.1
EPS4 = 4e-06
TIME_STEP = 0.1
PARTS = ((0, 32), (32, 8))
HERE, EVEN, ODD = 1, 3, 5


def to_tiles(boxes):
    slots, fields = boxes.shape[2], boxes.shape[3]
    parts = boxes.reshape(slots, fields, -1, LANES)
    return parts.transpose(1, 2, 0, 3).reshape(-1, LANES)


def from_tiles(tiles, shape):
    slots, fields = shape[2], shape[3]
    parts = tiles.reshape(fields, -1, slots, LANES)
    return parts.transpose(2, 0, 1, 3).reshape(shape)


def in_vmem(value):
    return pltpu.with_memory_space_constraint(value, pltpu.VMEM)


def in_smem(value):
    return pltpu.with_memory_space_constraint(value, pltpu.SMEM)


def exchange(value, partner):
    count, members = lax.axis_size("sfc"), lax.axis_size("sub")
    pairs = []
    for segment in range(count):
        for member in range(members):
            other, other_member = partner(segment, member, count, members)
            pairs.append((segment * members + member, other * members + other_member))
    return lax.ppermute(value, ("sfc", "sub"), pairs)


def even_partner(segment, member, count, members):
    other = segment ^ 1
    return (other, member) if other < count else (segment, member)


def odd_partner(segment, member, count, members):
    other = ((segment - 1) ^ 1) + 1
    if 0 < segment and other < count:
        return (other, member)
    other_member = member ^ 1
    return (segment, other_member) if other_member < members else (segment, member)


def group_shift(steps):
    def partner(segment, member, count, members):
        return (segment, (member + steps) % members)

    return partner


def positions():
    sub = lax.broadcasted_iota(jnp.int32, (ROWS, LANES), 0)
    lane = lax.broadcasted_iota(jnp.int32, (ROWS, LANES), 1)
    return sub, lane


def gather_lanes(value, index):
    return jnp.take_along_axis(value, index, axis=1, mode="promise_in_bounds")


def gather_rows(value, index):
    return jnp.take_along_axis(value, index, axis=0, mode="promise_in_bounds")


def roll_lanes(value, steps):
    return pltpu.roll(value, steps % LANES, 1)


def roll_rows(value, steps):
    if steps % ROWS == 0:
        return value
    sub, _ = positions()
    return gather_rows(value, (sub - steps) & 7)


def reciprocal(value):
    return 1.0 / value


def primitives(mass, mom_x, mom_y, mom_z, energy):
    density = jnp.maximum(mass, FLOOR)
    inverse = reciprocal(density)
    vel_x, vel_y, vel_z = mom_x * inverse, mom_y * inverse, mom_z * inverse
    kinetic = 0.5 * density * (vel_x * vel_x + vel_y * vel_y + vel_z * vel_z)
    pressure = jnp.maximum((GAMMA - 1.0) * (energy - kinetic), FLOOR)
    return [density, vel_x, vel_y, vel_z, pressure]


def load_parts(refs):
    fields = []
    for ref, (_, rows) in zip(refs, PARTS):
        fields += [ref[pl.ds(at, ROWS), :] for at in range(0, rows, ROWS)]
    return fields


def store_parts(refs, fields):
    fields = list(fields)
    for ref, (_, rows) in zip(refs, PARTS):
        for at in range(0, rows, ROWS):
            ref[pl.ds(at, ROWS), :] = fields.pop(0)


def load_primitives(ref, base=0):
    return primitives(*[ref[pl.ds(base + ROWS * f, ROWS), :] for f in range(FIELDS)])


def minmod(p, q):
    return jnp.maximum(jnp.minimum(p, q), 0.0) + jnp.minimum(jnp.maximum(p, q), 0.0)


def slopes(table, base, low):
    cells = [table[base + j] for j in range(4)]
    halves = [roll_lanes(c, 64) for c in cells]
    for j in range(4):
        u = cells[j]
        up = jnp.where(low, halves[j], halves[min(j + 1, 3)])
        down = jnp.where(low, halves[max(j - 1, 0)], halves[j])
        table[base + 4 + j] = 0.25 * minmod(up - u, u - down)
        table[base + 8 + j] = 0.25 * minmod(roll_lanes(u, -8) - u, u - roll_lanes(u, 8))
        table[base + 12 + j] = 0.25 * minmod(roll_lanes(u, -1) - u, u - roll_lanes(u, 1))


def spread_fields(table, base, coarse_ref):
    for j in range(4):
        for f in range(FIELDS):
            table[base + j, f : f + 1, :] = coarse_ref[f * 4 + j]


def read_links(links_in, corner_in, coarse_in, start_in, pick_ref, table, corner_ref, code_ref, *refs):
    own_refs, (links_ref, coarse_ref, sems) = refs[:-3], refs[-3:]
    copies = [(links_in, links_ref), (corner_in, corner_ref), (coarse_in, coarse_ref)]
    for own_ref, (first, rows) in zip(own_refs, PARTS):
        copies.append((start_in.at[pl.ds(first, rows), :], own_ref))
    fetches = [pltpu.make_async_copy(src, dst, sems.at[i]) for i, (src, dst) in enumerate(copies)]
    for fetch in fetches:
        fetch.start()
    sub, lane = positions()
    y, z = (lane >> 3) & 7, lane & 7
    odd_segment = lax.axis_index("sfc") & 1
    for fetch in fetches:
        fetch.wait()
    spread_fields(table, 0, coarse_ref)
    slopes(table, 0, lane < 64)

    def choice(slot, face):
        link = links_ref[slot, face]
        offset = link >> 1
        below = jnp.where(offset == 0, 1, 0)
        block = jnp.where(offset == 1, 0, jnp.where(below == odd_segment, 1, 2))
        swapped = (link & 1) ^ slot
        return jnp.where(link < 0, 0, 1 + block * 2 + swapped)

    codes = [[choice(slot, face) for face in range(6)] for slot in range(2)]
    waits = jnp.int32(0)
    for code in codes[0] + codes[1]:
        waits = jnp.maximum(waits, jnp.where(code >= ODD, 1, 0))
    code_ref[0, 0] = waits

    first = (sub & 1) == 0
    for direction in range(3):
        lower = (sub < 4) if direction == 0 else ((y if direction == 1 else z) < 4)
        minus = jnp.where(first, codes[0][2 * direction], codes[1][2 * direction])
        plus = jnp.where(first, codes[0][2 * direction + 1], codes[1][2 * direction + 1])
        pick_ref[pl.ds(direction * ROWS, ROWS), :] = jnp.where(lower, plus, minus)


def interpolate(corner_ref, own_table, *refs):
    coarse_refs, (ghost_ref, table, lines) = refs[:-3], refs[-3:]
    members = len(coarse_refs) + 1
    sub, lane = positions()
    low = lane < 64
    y, z = (lane >> 3) & 7, lane & 7
    me = lax.axis_index("sub")
    table[0:16] = own_table[...]
    for m, coarse_ref in enumerate(coarse_refs):
        spread_fields(table, (m + 1) * 16, coarse_ref)
        slopes(table, (m + 1) * 16, low)

    sign_x = jnp.where(low, -1.0, 1.0)
    sign_y = jnp.where((y & 1) == 0, -1.0, 1.0)
    sign_z = jnp.where((z & 1) == 0, -1.0, 1.0)
    spread = (y >> 1) * 8 + (z >> 1)

    def children(slot, face, j):
        direction, minus = face // 2, face % 2 == 0
        start = [corner_ref[slot, 1 + a, face] + (-1 if minus and a == direction else 1) for a in range(3)]
        owner = me - corner_ref[slot, 0, face]
        owner = jnp.where(owner < 0, owner + members, owner)
        along = start[0] + j
        index = (spread + ((along & 1) * 64 + start[1] * 8 + start[2])) & (LANES - 1)
        row = owner * 16 + (along >> 1)
        parts = [gather_lanes(table[row + 4 * q], index) for q in range(4)]
        return parts[0] + sign_x * parts[1] + sign_y * parts[2] + sign_z * parts[3]

    for direction in range(3):
        for slot in range(2):
            for j in range(4):
                minus, plus = 2 * direction, 2 * direction + 1
                if direction == 0:
                    value = children(slot, minus if j >= 2 else plus, j)
                else:
                    lower = (y if direction == 1 else z) < 4
                    value = jnp.where(lower, children(slot, plus, j), children(slot, minus, j))
                rows = pl.ds(direction * 40 + j * 2 + slot, FIELDS, stride=ROWS)
                lines[rows, :] = value[0:FIELDS, :]
        made = load_primitives(lines, direction * 40)
        for f in range(FIELDS):
            ghost_ref[pl.ds(direction * 40 + f * ROWS, ROWS), :] = made[f]


def weno(cells):
    centre = cells[2]
    e0, e1, e2, e3 = [cells[k + 1] - cells[k] for k in range(4)]
    d1, d2, d3 = e1 - e0, e2 - e1, e3 - e2
    below, above, across = 3.0 * e1 - e0, 3.0 * e2 - e3, e1 + e2
    a = ((13.0 / 3.0) * (d1 * d1) + EPS4) + below * below
    b = ((13.0 / 3.0) * (d2 * d2) + EPS4) + across * across
    c = ((13.0 / 3.0) * (d3 * d3) + EPS4) + above * above
    bc, ac, ab = b * c, a * c, a * b
    bc, ac, ab = bc * bc, 6.0 * (ac * ac), ab * ab
    bc3, ab3 = 3.0 * bc, 3.0 * ab
    up = bc * (2.0 * below - e1) + ac * (across + e2) + ab3 * (above + e2)
    down = ab * (2.0 * above - e2) + ac * (across + e1) + bc3 * (below + e1)
    upper = centre + up * ((1.0 / 6.0) * reciprocal(bc + ac + ab3))
    lower = centre - down * ((1.0 / 6.0) * reciprocal(ab + ac + bc3))
    return upper, lower


def hllc(left, right):
    rl, ul, vl, wl, pl_ = jnp.maximum(left[0], FLOOR), left[1], left[2], left[3], jnp.maximum(left[4], FLOOR)
    rr, ur, vr, wr, pr = jnp.maximum(right[0], FLOOR), right[1], right[2], right[3], jnp.maximum(right[4], FLOOR)
    gl, gr = GAMMA * pl_, GAMMA * pr
    cl, cr = gl * lax.rsqrt(gl * rl), gr * lax.rsqrt(gr * rr)
    speed_left = jnp.minimum(ul - cl, ur - cr)
    speed_right = jnp.maximum(ul + cl, ur + cr)
    ml, mr = rl * (speed_left - ul), rr * (speed_right - ur)
    contact = (pr - pl_ + ml * ul - mr * ur) * reciprocal(ml - mr)
    from_left = (speed_left >= 0.0) | (contact >= 0.0)
    r = jnp.where(from_left, rl, rr)
    u = jnp.where(from_left, ul, ur)
    v = jnp.where(from_left, vl, vr)
    w = jnp.where(from_left, wl, wr)
    p = jnp.where(from_left, pl_, pr)
    s = jnp.where(from_left, speed_left, speed_right)
    m = jnp.where(from_left, ml, mr)
    star = (speed_left < 0.0) & ((contact >= 0.0) | (speed_right >= 0.0))
    energy = p * (1.0 / (GAMMA - 1.0)) + 0.5 * r * (u * u + v * v + w * w)
    inverse = reciprocal(s - contact)
    star_p = p + m * (contact - u)
    star_e = ((s - u) * energy - p * u + star_p * contact) * inverse
    density = jnp.where(star, m * inverse, r)
    normal = jnp.where(star, contact, u)
    pressure = jnp.where(star, star_p, p)
    energy = jnp.where(star, star_e, energy)
    mass = density * normal
    return [mass, mass * normal + pressure, mass * v, mass * w, normal * (energy + pressure)]


class Turns:
    def __init__(self):
        sub, lane = positions()
        self.sub = sub
        y, z = (lane >> 3) & 7, lane & 7
        high = lane >> 6
        self.steps = (
            (sub ^ high, lane ^ ((sub & 1) << 6), sub ^ high),
            ((sub - y) & 7, (lane & 71) | (((sub - y) & 7) << 3), (sub + y) & 7),
            ((sub - z) & 7, (lane & 120) | ((sub - z) & 7), (sub + z) & 7),
        )

    def __call__(self, direction, value):
        before, across, after = self.steps[direction]
        return gather_rows(gather_lanes(gather_rows(value, before), across), after)


def swapped_slots(value, sub):
    return gather_rows(value, sub ^ 1)


OWN, GHOST, READY = 0, 15, 30


def make_ready(ghost_ref, pick_ref, *refs):
    own_refs, ready_ref = refs[:-1], refs[-1]
    turn = Turns()
    own = primitives(*load_parts(own_refs))
    candidates = [own, [swapped_slots(v, turn.sub) for v in own]]
    for direction in range(3):
        pick = pick_ref[pl.ds(direction * ROWS, ROWS), :]
        wanted = [pick == c + 1 for c in range(len(candidates))]
        remote = pick > len(candidates)
        for f in range(FIELDS):
            value = ghost_ref[pl.ds((direction * FIELDS + f) * ROWS, ROWS), :]
            for c, candidate in enumerate(candidates):
                value = jnp.where(wanted[c], candidate[f], value)
            value = jnp.where(remote, 0.0, value)
            tile = direction * FIELDS + f
            ready_ref[pl.ds((GHOST + tile) * ROWS, ROWS), :] = turn(direction, value)
            ready_ref[pl.ds((OWN + tile) * ROWS, ROWS), :] = turn(direction, own[f])


def rate(blocks, ready_ref, pick_ref):
    turn = Turns()
    sub = turn.sub
    first_row = sub == 0
    candidates = []
    for block in blocks:
        candidates += [block, [swapped_slots(v, sub) for v in block]]

    def line(direction, f):
        pick = pick_ref[pl.ds(direction * ROWS, ROWS), :]
        tile = direction * FIELDS + f
        remote = jnp.zeros((ROWS, LANES), jnp.float32)
        for c, candidate in enumerate(candidates):
            remote = jnp.where(pick == EVEN + c, candidate[f], remote)
        ghost = ready_ref[pl.ds((GHOST + tile) * ROWS, ROWS), :] + turn(direction, remote)
        return ready_ref[pl.ds((OWN + tile) * ROWS, ROWS), :], ghost

    is_x, is_y = (sub == 7) | first_row, (sub == 1) | (sub == 2)
    places = (0, 2, 4)
    sides = [[], [], []]
    outer = []
    for f in range(FIELDS):
        beside = []
        for direction in range(3):
            own, ghost = line(direction, f)
            cells, around = [], []
            for s in range(-2, 3):
                if s == 0:
                    cells.append(own)
                    around.append(ghost)
                    continue
                own_s, ghost_s = roll_rows(own, -s), roll_rows(ghost, -s)
                outside = (sub + s < 0) | (sub + s > 7)
                cells.append(jnp.where(outside, ghost_s, own_s))
                at_first, at_last = (own_s, ghost_s) if s < 0 else (ghost_s, own_s)
                around.append(jnp.where(first_row, at_first, at_last))
            sides[direction].append(weno(cells))
            beside.append(around)
        outer.append(
            weno(
                [
                    jnp.where(is_x, vx, jnp.where(is_y, roll_rows(vy, 2), roll_rows(vz, 4)))
                    for vx, vy, vz in zip(*beside)
                ]
            )
        )

    ended = []
    fluxes = []
    orders = ((0, 1, 2, 3, 4), (0, 2, 1, 3, 4), (0, 3, 1, 2, 4))
    for direction in range(3):
        rolled = [roll_rows(side[0], 1) for side in sides[direction]]
        ended.append([roll_rows(v, places[direction]) for v in rolled])
        lefts = [jnp.where(first_row, roll_rows(o[0], 1 - places[direction]), v) for o, v in zip(outer, rolled)]
        rights = [side[1] for side in sides[direction]]
        order = orders[direction]
        fluxes.append(hllc([lefts[f] for f in order], [rights[f] for f in order]))

    at_y, at_z = sub == 2, sub == 4

    def turned(values):
        normal = jnp.where(at_y, values[2], jnp.where(at_z, values[3], values[1]))
        one = jnp.where(at_y | at_z, values[1], values[2])
        two = jnp.where(at_z, values[2], values[3])
        return [values[0], normal, one, two, values[4]]

    left_end = [jnp.where(at_y, ended[1][f], jnp.where(at_z, ended[2][f], ended[0][f])) for f in range(FIELDS)]
    last = hllc(turned(left_end), turned([o[1] for o in outer]))

    total = [None] * FIELDS
    for direction in range(3):
        for place, f in enumerate(orders[direction]):
            flux = fluxes[direction][place]
            merged = jnp.where(first_row, roll_rows(last[place], -places[direction]), flux)
            change = turn(direction, flux - roll_rows(merged, -1))
            total[f] = change if total[f] is None else total[f] + change
    return total


def even_and_odd(even_refs, odd_refs):
    blocks = [primitives(*load_parts(even_refs))]
    return blocks + [load_primitives(ref) for ref in odd_refs]


def middle_of(own_refs, even_refs, odd_refs, ready_ref, pick_ref, out_ref, part_refs):
    own = load_parts(own_refs)
    change = rate(even_and_odd(even_refs, odd_refs), ready_ref, pick_ref)
    middle = [own[f] + TIME_STEP * change[f] for f in range(FIELDS)]
    store_parts(part_refs, middle)
    for f in range(FIELDS):
        out_ref[pl.ds(f * ROWS, ROWS), :] = middle[f]


def first_stage(waits_ref, ready_ref, pick_ref, *refs):
    n = len(PARTS)
    own_refs, even_refs, out_ref, part_refs = refs[:n], refs[n : 2 * n], refs[2 * n], refs[2 * n + 1 :]

    @pl.when(waits_ref[0, 0] == 0)
    def _():
        middle_of(own_refs, even_refs, [], ready_ref, pick_ref, out_ref, part_refs)


def first_stage_odd(waits_ref, ready_ref, pick_ref, *refs):
    n = len(PARTS)
    own_refs, even_refs, odd_ref, made = refs[:n], refs[n : 2 * n], refs[2 * n], refs[3 * n + 2 :]

    @pl.when(waits_ref[0, 0] != 0)
    def _():
        middle_of(own_refs, even_refs, [odd_ref], ready_ref, pick_ref, made[0], made[1:])


def advanced_of(start_refs, own_refs, even_refs, odd_refs, ready_ref, pick_ref, count_ref, out_ref, made_ref, sem):
    start, own = load_parts(start_refs), load_parts(own_refs)
    change = rate(even_and_odd(even_refs, odd_refs), ready_ref, pick_ref)
    sub, _ = positions()
    live = (sub & 1) < count_ref[0, 0]
    for f in range(FIELDS):
        value = 0.5 * start[f] + 0.5 * (own[f] + TIME_STEP * change[f])
        made_ref[pl.ds(f * ROWS, ROWS), :] = jnp.where(live, value, 0.0)
    copy = pltpu.make_async_copy(made_ref, out_ref, sem)
    copy.start()
    copy.wait()


def second_stage(waits_ref, count_ref, ready_ref, pick_ref, *refs):
    n = len(PARTS)
    start_refs, own_refs, even_refs, (out_ref, made_ref, sem) = refs[:n], refs[n : 2 * n], refs[2 * n : 3 * n], refs[3 * n :]

    @pl.when(waits_ref[0, 0] == 0)
    def _():
        advanced_of(start_refs, own_refs, even_refs, [], ready_ref, pick_ref, count_ref, out_ref, made_ref, sem)


def second_stage_odd(waits_ref, count_ref, ready_ref, pick_ref, *refs):
    n = len(PARTS)
    start_refs, own_refs, even_refs = refs[:n], refs[n : 2 * n], refs[2 * n : 3 * n]
    odd_ref, _, out_ref, made_ref, sem = refs[3 * n :]

    @pl.when(waits_ref[0, 0] != 0)
    def _():
        advanced_of(start_refs, own_refs, even_refs, [odd_ref], ready_ref, pick_ref, count_ref, out_ref, made_ref, sem)


def vmem_spec():
    return pl.BlockSpec(memory_space=pltpu.VMEM)


def smem_spec():
    return pl.BlockSpec(memory_space=pltpu.SMEM)


def hbm_spec():
    return pl.BlockSpec(memory_space=pltpu.HBM)


def body(fine_state, coarse_old, box_count, fine_links, coarse_links):
    members = lax.axis_size("sub")
    tile_rows = FIELDS * ROWS
    start = to_tiles(fine_state)
    coarse = coarse_old.transpose(0, 2, 1, 3).reshape(FIELDS, 1, -1, LANES).transpose(0, 2, 1, 3)
    coarse = coarse.reshape(-1, 1, LANES)

    odd = exchange(start, odd_partner)
    group = [exchange(coarse, group_shift(r)) for r in range(1, members)]

    picks, table, corners, waits, *own = pl.pallas_call(
        read_links,
        out_shape=(
            pltpu.VMEM((3 * ROWS, LANES), jnp.int32),
            pltpu.VMEM((16, ROWS, LANES), jnp.float32),
            pltpu.SMEM((2, 4, 6), jnp.int32),
            pltpu.SMEM((2, 6), jnp.int32),
            *[pltpu.VMEM((rows, LANES), jnp.float32) for _, rows in PARTS],
        ),
        in_specs=[hbm_spec()] * 4,
        out_specs=(vmem_spec(), vmem_spec(), smem_spec(), smem_spec()) + (vmem_spec(),) * len(PARTS),
        scratch_shapes=[
            pltpu.SMEM((2, 6), jnp.int32),
            pltpu.VMEM((FIELDS * 4, 1, LANES), jnp.float32),
            pltpu.SemaphoreType.DMA((3 + len(PARTS),)),
        ],
        name="read_links",
    )(
        fine_links.reshape(2, 6),
        coarse_links.transpose(0, 1, 2, 4, 3).reshape(2, 4, 6),
        coarse,
        start,
    )
    even = [in_vmem(exchange(part, even_partner)) for part in own]
    ghosts = pl.pallas_call(
        interpolate,
        out_shape=pltpu.VMEM((3 * tile_rows, LANES), jnp.float32),
        in_specs=[smem_spec()] + [vmem_spec()] * members,
        out_specs=vmem_spec(),
        scratch_shapes=[
            pltpu.VMEM((members * 16, ROWS, LANES), jnp.float32),
            pltpu.VMEM((3 * tile_rows, LANES), jnp.float32),
        ],
        name="interpolate",
        cost_estimate=pl.CostEstimate(flops=10000000000, bytes_accessed=10000000000, transcendentals=0),
    )(in_smem(corners), in_vmem(table), *[in_vmem(c) for c in group])

    count = len(PARTS)
    tiles = (tile_rows, LANES)
    waits, picks, ghosts = in_smem(waits), in_vmem(picks), in_vmem(ghosts)
    own = [in_vmem(part) for part in own]

    def fold(parts):
        ready = pl.pallas_call(
            make_ready,
            out_shape=pltpu.VMEM((READY * ROWS, LANES), jnp.float32),
            in_specs=[vmem_spec()] * (2 + count),
            out_specs=vmem_spec(),
            name="fold",
        )(ghosts, picks, *parts)
        return in_vmem(ready)

    made = (pltpu.VMEM(tiles, jnp.float32),) + tuple(pltpu.VMEM((rows, LANES), jnp.float32) for _, rows in PARTS)
    ready = fold(own)
    middle = pl.pallas_call(
        first_stage,
        out_shape=made,
        in_specs=[smem_spec()] + [vmem_spec()] * (2 + 2 * count),
        out_specs=(vmem_spec(),) * len(made),
        name="first_stage",
    )(waits, ready, picks, *own, *even)
    middle, *parts = pl.pallas_call(
        first_stage_odd,
        out_shape=made,
        in_specs=[smem_spec()] + [vmem_spec()] * (4 + 3 * count),
        out_specs=(vmem_spec(),) * len(made),
        input_output_aliases={4 + 2 * count + k: k for k in range(len(made))},
        name="first_stage_odd",
    )(waits, ready, picks, *own, *even, in_vmem(odd), *[in_vmem(m) for m in middle])

    odd = exchange(middle, odd_partner)
    even = [in_vmem(exchange(part, even_partner)) for part in parts]
    parts = [in_vmem(part) for part in parts]
    ready = fold(parts)
    scratch = [pltpu.VMEM(tiles, jnp.float32), pltpu.SemaphoreType.DMA(())]
    result = pl.pallas_call(
        second_stage,
        out_shape=jax.ShapeDtypeStruct(tiles, jnp.float32),
        in_specs=[smem_spec()] * 2 + [vmem_spec()] * (2 + 3 * count),
        out_specs=hbm_spec(),
        scratch_shapes=scratch,
        name="second_stage",
    )(waits, box_count, ready, picks, *own, *parts, *even)
    result = pl.pallas_call(
        second_stage_odd,
        out_shape=jax.ShapeDtypeStruct(tiles, jnp.float32),
        in_specs=[smem_spec()] * 2 + [vmem_spec()] * (3 + 3 * count) + [hbm_spec()],
        out_specs=hbm_spec(),
        scratch_shapes=scratch,
        input_output_aliases={5 + 3 * count: 0},
        name="second_stage_odd",
    )(waits, box_count, ready, picks, *own, *parts, *even, in_vmem(odd), result)
    return from_tiles(result, fine_state.shape)


def solution(mesh):
    placed = (
        P("sfc", "sub", None, None, None),
        P("sfc", "sub", None, None),
        P("sfc", "sub"),
        P("sfc", "sub", None, None),
        P("sfc", "sub", None, None, None),
    )
    return jax.shard_map(
        body,
        mesh=mesh,
        in_specs=placed,
        out_specs=P("sfc", "sub", None, None, None),
        check_vma=False,
    )
```

```python
import jax
import jax.numpy as jnp
from jax import lax
from jax.experimental import pallas as pl
from jax.experimental.pallas import tpu as pltpu
from jax.sharding import PartitionSpec as P

FIELDS = 5
ROWS = 8
LANES = 128
GAMMA = 1.4
FLOOR = 0.1
EPS4 = 4e-06
TIME_STEP = 0.1
PARTS = ((0, 32), (32, 8))
HERE, EVEN, ODD = 1, 3, 5


def to_tiles(boxes):
    slots, fields = boxes.shape[2], boxes.shape[3]
    parts = boxes.reshape(slots, fields, -1, LANES)
    return parts.transpose(1, 2, 0, 3).reshape(-1, LANES)


def from_tiles(tiles, shape):
    slots, fields = shape[2], shape[3]
    parts = tiles.reshape(fields, -1, slots, LANES)
    return parts.transpose(2, 0, 1, 3).reshape(shape)


def in_vmem(value):
    return pltpu.with_memory_space_constraint(value, pltpu.VMEM)


def in_smem(value):
    return pltpu.with_memory_space_constraint(value, pltpu.SMEM)


def exchange(value, partner):
    count, members = lax.axis_size("sfc"), lax.axis_size("sub")
    pairs = []
    for segment in range(count):
        for member in range(members):
            other, other_member = partner(segment, member, count, members)
            pairs.append((segment * members + member, other * members + other_member))
    return lax.ppermute(value, ("sfc", "sub"), pairs)


def even_partner(segment, member, count, members):
    other = segment ^ 1
    return (other, member) if other < count else (segment, member)


def odd_partner(segment, member, count, members):
    other = ((segment - 1) ^ 1) + 1
    if 0 < segment and other < count:
        return (other, member)
    other_member = member ^ 1
    return (segment, other_member) if other_member < members else (segment, member)


def group_shift(steps):
    def partner(segment, member, count, members):
        return (segment, (member + steps) % members)

    return partner


def positions():
    sub = lax.broadcasted_iota(jnp.int32, (ROWS, LANES), 0)
    lane = lax.broadcasted_iota(jnp.int32, (ROWS, LANES), 1)
    return sub, lane


def gather_lanes(value, index):
    return jnp.take_along_axis(value, index, axis=1, mode="promise_in_bounds")


def gather_rows(value, index):
    return jnp.take_along_axis(value, index, axis=0, mode="promise_in_bounds")


def roll_lanes(value, steps):
    return pltpu.roll(value, steps % LANES, 1)


def roll_rows(value, steps):
    if steps % ROWS == 0:
        return value
    sub, _ = positions()
    return gather_rows(value, (sub - steps) & 7)


def reciprocal(value):
    return 1.0 / value


def primitives(mass, mom_x, mom_y, mom_z, energy):
    density = jnp.maximum(mass, FLOOR)
    inverse = reciprocal(density)
    vel_x, vel_y, vel_z = mom_x * inverse, mom_y * inverse, mom_z * inverse
    kinetic = 0.5 * density * (vel_x * vel_x + vel_y * vel_y + vel_z * vel_z)
    pressure = jnp.maximum((GAMMA - 1.0) * (energy - kinetic), FLOOR)
    return [density, vel_x, vel_y, vel_z, pressure]


def load_parts(refs):
    fields = []
    for ref, (_, rows) in zip(refs, PARTS):
        fields += [ref[pl.ds(at, ROWS), :] for at in range(0, rows, ROWS)]
    return fields


def store_parts(refs, fields):
    fields = list(fields)
    for ref, (_, rows) in zip(refs, PARTS):
        for at in range(0, rows, ROWS):
            ref[pl.ds(at, ROWS), :] = fields.pop(0)


def load_primitives(ref, base=0):
    return primitives(*[ref[pl.ds(base + ROWS * f, ROWS), :] for f in range(FIELDS)])


def minmod(p, q):
    return jnp.maximum(jnp.minimum(p, q), 0.0) + jnp.minimum(jnp.maximum(p, q), 0.0)


def build_table(coarse_ref, raw, table, base):
    sub, lane = positions()
    low = lane < 64
    for j in range(4):
        for f in range(FIELDS):
            raw[j, f : f + 1, :] = coarse_ref[f * 4 + j]
    cells = [raw[j] for j in range(4)]
    halves = [roll_lanes(c, 64) for c in cells]
    for j in range(4):
        u = cells[j]
        up = jnp.where(low, halves[j], halves[min(j + 1, 3)])
        down = jnp.where(low, halves[max(j - 1, 0)], halves[j])
        slopes = (
            0.25 * minmod(up - u, u - down),
            0.25 * minmod(roll_lanes(u, -8) - u, u - roll_lanes(u, 8)),
            0.25 * minmod(roll_lanes(u, -1) - u, u - roll_lanes(u, 1)),
        )
        along_x, along_y, along_z = slopes
        swapped_x, swapped_y, swapped_z = [roll_lanes(v, 64) for v in slopes]
        for x in (2 * j, 2 * j + 1):
            if x in (0, 7):
                continue
            if x % 2 == 0:
                value, slope = jnp.where(low, u, halves[j]), jnp.where(low, along_x, swapped_x)
                sides = jnp.where(low, along_y, swapped_z)
            else:
                value, slope = jnp.where(low, halves[j], u), jnp.where(low, swapped_x, along_x)
                sides = jnp.where(low, swapped_y, along_z)
            value = jnp.where(low, value - slope, value + slope)
            table[base + x] = jnp.where(sub < FIELDS, value, gather_rows(sides, (sub + 3) & 7))
            table[base + 8 + x] = jnp.where(sub < FIELDS, sides, gather_rows(sides, (sub + 6) & 7))


def fetch(links_in, corner_in, coarse_in, start_in, links_ref, corner_ref, coarse_ref, *refs):
    own_refs, sems = refs[:-1], refs[-1]
    copies = [(links_in, links_ref), (corner_in, corner_ref), (coarse_in, coarse_ref)]
    for own_ref, (first, rows) in zip(own_refs, PARTS):
        copies.append((start_in.at[pl.ds(first, rows), :], own_ref))
    fetches = [pltpu.make_async_copy(src, dst, sems.at[i]) for i, (src, dst) in enumerate(copies)]
    for copy in fetches:
        copy.start()
    for copy in fetches:
        copy.wait()


def read_links(links_ref, coarse_ref, pick_ref, table, code_ref, raw):
    sub, lane = positions()
    y, z = (lane >> 3) & 7, lane & 7
    odd_segment = lax.axis_index("sfc") & 1
    build_table(coarse_ref, raw, table, 0)

    def choice(slot, face):
        link = links_ref[slot, face]
        offset = link >> 1
        below = jnp.where(offset == 0, 1, 0)
        block = jnp.where(offset == 1, 0, jnp.where(below == odd_segment, 1, 2))
        swapped = (link & 1) ^ slot
        return jnp.where(link < 0, 0, 1 + block * 2 + swapped)

    codes = [[choice(slot, face) for face in range(6)] for slot in range(2)]
    waits = jnp.int32(0)
    for code in codes[0] + codes[1]:
        waits = jnp.maximum(waits, jnp.where(code >= ODD, 1, 0))
    code_ref[0, 0] = waits

    first = (sub & 1) == 0
    for direction in range(3):
        lower = (sub < 4) if direction == 0 else ((y if direction == 1 else z) < 4)
        minus = jnp.where(first, codes[0][2 * direction], codes[1][2 * direction])
        plus = jnp.where(first, codes[0][2 * direction + 1], codes[1][2 * direction + 1])
        pick_ref[pl.ds(direction * ROWS, ROWS), :] = jnp.where(lower, plus, minus)


def interpolate(corner_ref, own_table, *refs):
    coarse_refs, (ghost_ref, table, raw, lines) = refs[:-4], refs[-4:]
    members = len(coarse_refs) + 1
    sub, lane = positions()
    y, z = (lane >> 3) & 7, lane & 7
    me = lax.axis_index("sub")
    table[0:16] = own_table[...]
    for m, coarse_ref in enumerate(coarse_refs):
        build_table(coarse_ref, raw, table, (m + 1) * 16)

    sign_y = jnp.where((y & 1) == 0, -1.0, 1.0)
    sign_z = jnp.where((z & 1) == 0, -1.0, 1.0)
    spread = (y >> 1) * 8 + (z >> 1)
    upper, whole = jnp.where(sub < FIELDS, lane & 64, 0), jnp.where(sub < FIELDS, 64, 0)

    def finder(slot, face):
        direction, minus = face // 2, face % 2 == 0
        start = [corner_ref[slot, 1 + a, face] + (-1 if minus and a == direction else 1) for a in range(3)]
        owner = me - corner_ref[slot, 0, face]
        owner = jnp.where(owner < 0, owner + members, owner)
        index = (spread + (start[1] * 8 + start[2])) & 63
        first, second, row = index | upper, index | whole, owner * 16 + start[0]

        def find(j):
            return gather_lanes(table[row + j], first), gather_lanes(table[row + 8 + j], second)

        return find

    for direction in range(3):
        for slot in range(2):
            minus, plus = finder(slot, 2 * direction), finder(slot, 2 * direction + 1)
            for j in range(4):
                if direction == 0:
                    value, sides = (minus if j >= 2 else plus)(j)
                else:
                    lower = (y if direction == 1 else z) < 4
                    value, sides = [jnp.where(lower, p, m) for p, m in zip(plus(j), minus(j))]
                along_y = jnp.where(sub < 3, gather_rows(value, (sub + 5) & 7), gather_rows(sides, (sub + 2) & 7))
                value = value + sign_y * along_y + sign_z * sides
                rows = pl.ds(direction * 40 + j * 2 + slot, FIELDS, stride=ROWS)
                lines[rows, :] = value[0:FIELDS, :]
        made = load_primitives(lines, direction * 40)
        for f in range(FIELDS):
            ghost_ref[pl.ds(direction * 40 + f * ROWS, ROWS), :] = made[f]


def weno(cells):
    centre = cells[2]
    e0, e1, e2, e3 = [cells[k + 1] - cells[k] for k in range(4)]
    d1, d2, d3 = e1 - e0, e2 - e1, e3 - e2
    below, above, across = 3.0 * e1 - e0, 3.0 * e2 - e3, e1 + e2
    a = ((13.0 / 3.0) * (d1 * d1) + EPS4) + below * below
    b = ((13.0 / 3.0) * (d2 * d2) + EPS4) + across * across
    c = ((13.0 / 3.0) * (d3 * d3) + EPS4) + above * above
    bc, ac, ab = b * c, a * c, a * b
    bc, ac, ab = bc * bc, 6.0 * (ac * ac), ab * ab
    bc3, ab3 = 3.0 * bc, 3.0 * ab
    up = bc * (2.0 * below - e1) + ac * (across + e2) + ab3 * (above + e2)
    down = ab * (2.0 * above - e2) + ac * (across + e1) + bc3 * (below + e1)
    upper = centre + up * ((1.0 / 6.0) * reciprocal(bc + ac + ab3))
    lower = centre - down * ((1.0 / 6.0) * reciprocal(ab + ac + bc3))
    return upper, lower


def hllc(left, right):
    rl, ul, vl, wl, pl_ = jnp.maximum(left[0], FLOOR), left[1], left[2], left[3], jnp.maximum(left[4], FLOOR)
    rr, ur, vr, wr, pr = jnp.maximum(right[0], FLOOR), right[1], right[2], right[3], jnp.maximum(right[4], FLOOR)
    gl, gr = GAMMA * pl_, GAMMA * pr
    cl, cr = gl * lax.rsqrt(gl * rl), gr * lax.rsqrt(gr * rr)
    speed_left = jnp.minimum(ul - cl, ur - cr)
    speed_right = jnp.maximum(ul + cl, ur + cr)
    ml, mr = rl * (speed_left - ul), rr * (speed_right - ur)
    contact = (pr - pl_ + ml * ul - mr * ur) * reciprocal(ml - mr)
    from_left = (speed_left >= 0.0) | (contact >= 0.0)
    r = jnp.where(from_left, rl, rr)
    u = jnp.where(from_left, ul, ur)
    v = jnp.where(from_left, vl, vr)
    w = jnp.where(from_left, wl, wr)
    p = jnp.where(from_left, pl_, pr)
    s = jnp.where(from_left, speed_left, speed_right)
    m = jnp.where(from_left, ml, mr)
    star = (speed_left < 0.0) & ((contact >= 0.0) | (speed_right >= 0.0))
    energy = p * (1.0 / (GAMMA - 1.0)) + 0.5 * r * (u * u + v * v + w * w)
    inverse = reciprocal(s - contact)
    star_p = p + m * (contact - u)
    star_e = ((s - u) * energy - p * u + star_p * contact) * inverse
    density = jnp.where(star, m * inverse, r)
    normal = jnp.where(star, contact, u)
    pressure = jnp.where(star, star_p, p)
    energy = jnp.where(star, star_e, energy)
    mass = density * normal
    return [mass, mass * normal + pressure, mass * v, mass * w, normal * (energy + pressure)]


class Turns:
    def __init__(self):
        sub, lane = positions()
        self.sub = sub
        y, z = (lane >> 3) & 7, lane & 7
        high = lane >> 6
        self.steps = (
            (sub ^ high, lane ^ ((sub & 1) << 6), sub ^ high),
            ((sub - y) & 7, (lane & 71) | (((sub - y) & 7) << 3), (sub + y) & 7),
            ((sub - z) & 7, (lane & 120) | ((sub - z) & 7), (sub + z) & 7),
        )

    def __call__(self, direction, value):
        before, across, after = self.steps[direction]
        return gather_rows(gather_lanes(gather_rows(value, before), across), after)


def swapped_slots(value, sub):
    return gather_rows(value, sub ^ 1)


OWN, GHOST, READY = 0, 15, 30


def make_ready(ghost_ref, pick_ref, *refs):
    own_refs, ready_ref = refs[:-1], refs[-1]
    turn = Turns()
    own = primitives(*load_parts(own_refs))
    candidates = [own, [swapped_slots(v, turn.sub) for v in own]]
    for direction in range(3):
        pick = pick_ref[pl.ds(direction * ROWS, ROWS), :]
        wanted = [pick == c + 1 for c in range(len(candidates))]
        remote = pick > len(candidates)
        for f in range(FIELDS):
            value = ghost_ref[pl.ds((direction * FIELDS + f) * ROWS, ROWS), :]
            for c, candidate in enumerate(candidates):
                value = jnp.where(wanted[c], candidate[f], value)
            value = jnp.where(remote, 0.0, value)
            tile = direction * FIELDS + f
            ready_ref[pl.ds((GHOST + tile) * ROWS, ROWS), :] = turn(direction, value)
            ready_ref[pl.ds((OWN + tile) * ROWS, ROWS), :] = turn(direction, own[f])


def rate(blocks, ready_ref, pick_ref):
    turn = Turns()
    sub = turn.sub
    first_row = sub == 0
    candidates = []
    for block in blocks:
        candidates += [block, [swapped_slots(v, sub) for v in block]]

    def line(direction, f):
        pick = pick_ref[pl.ds(direction * ROWS, ROWS), :]
        tile = direction * FIELDS + f
        remote = jnp.zeros((ROWS, LANES), jnp.float32)
        for c, candidate in enumerate(candidates):
            remote = jnp.where(pick == EVEN + c, candidate[f], remote)
        ghost = ready_ref[pl.ds((GHOST + tile) * ROWS, ROWS), :] + turn(direction, remote)
        return ready_ref[pl.ds((OWN + tile) * ROWS, ROWS), :], ghost

    is_x, is_y = (sub == 7) | first_row, (sub == 1) | (sub == 2)
    places = (0, 2, 4)
    sides = [[], [], []]
    outer = []
    for f in range(FIELDS):
        beside = []
        for direction in range(3):
            own, ghost = line(direction, f)
            cells, around = [], []
            for s in range(-2, 3):
                if s == 0:
                    cells.append(own)
                    around.append(ghost)
                    continue
                own_s, ghost_s = roll_rows(own, -s), roll_rows(ghost, -s)
                outside = (sub + s < 0) | (sub + s > 7)
                cells.append(jnp.where(outside, ghost_s, own_s))
                at_first, at_last = (own_s, ghost_s) if s < 0 else (ghost_s, own_s)
                around.append(jnp.where(first_row, at_first, at_last))
            sides[direction].append(weno(cells))
            beside.append(around)
        outer.append(
            weno(
                [
                    jnp.where(is_x, vx, jnp.where(is_y, roll_rows(vy, 2), roll_rows(vz, 4)))
                    for vx, vy, vz in zip(*beside)
                ]
            )
        )

    ended = []
    fluxes = []
    orders = ((0, 1, 2, 3, 4), (0, 2, 1, 3, 4), (0, 3, 1, 2, 4))
    for direction in range(3):
        rolled = [roll_rows(side[0], 1) for side in sides[direction]]
        ended.append([roll_rows(v, places[direction]) for v in rolled])
        lefts = [jnp.where(first_row, roll_rows(o[0], 1 - places[direction]), v) for o, v in zip(outer, rolled)]
        rights = [side[1] for side in sides[direction]]
        order = orders[direction]
        fluxes.append(hllc([lefts[f] for f in order], [rights[f] for f in order]))

    at_y, at_z = sub == 2, sub == 4

    def turned(values):
        normal = jnp.where(at_y, values[2], jnp.where(at_z, values[3], values[1]))
        one = jnp.where(at_y | at_z, values[1], values[2])
        two = jnp.where(at_z, values[2], values[3])
        return [values[0], normal, one, two, values[4]]

    left_end = [jnp.where(at_y, ended[1][f], jnp.where(at_z, ended[2][f], ended[0][f])) for f in range(FIELDS)]
    last = hllc(turned(left_end), turned([o[1] for o in outer]))

    total = [None] * FIELDS
    for direction in range(3):
        for place, f in enumerate(orders[direction]):
            flux = fluxes[direction][place]
            merged = jnp.where(first_row, roll_rows(last[place], -places[direction]), flux)
            change = turn(direction, flux - roll_rows(merged, -1))
            total[f] = change if total[f] is None else total[f] + change
    return total


def even_and_odd(even_refs, odd_refs):
    blocks = [primitives(*load_parts(even_refs))]
    return blocks + [load_primitives(ref) for ref in odd_refs]


def middle_of(own_refs, even_refs, odd_refs, ready_ref, pick_ref, out_ref, part_refs):
    own = load_parts(own_refs)
    change = rate(even_and_odd(even_refs, odd_refs), ready_ref, pick_ref)
    middle = [own[f] + TIME_STEP * change[f] for f in range(FIELDS)]
    store_parts(part_refs, middle)
    for f in range(FIELDS):
        out_ref[pl.ds(f * ROWS, ROWS), :] = middle[f]


def first_stage(waits_ref, ready_ref, pick_ref, *refs):
    n = len(PARTS)
    own_refs, even_refs, out_ref, part_refs = refs[:n], refs[n : 2 * n], refs[2 * n], refs[2 * n + 1 :]

    @pl.when(waits_ref[0, 0] == 0)
    def _():
        middle_of(own_refs, even_refs, [], ready_ref, pick_ref, out_ref, part_refs)


def first_stage_odd(waits_ref, ready_ref, pick_ref, *refs):
    n = len(PARTS)
    own_refs, even_refs, odd_ref, made = refs[:n], refs[n : 2 * n], refs[2 * n], refs[3 * n + 2 :]

    @pl.when(waits_ref[0, 0] != 0)
    def _():
        middle_of(own_refs, even_refs, [odd_ref], ready_ref, pick_ref, made[0], made[1:])


def advanced_of(start_refs, own_refs, even_refs, odd_refs, ready_ref, pick_ref, count_ref, out_ref, made_ref, sem):
    start, own = load_parts(start_refs), load_parts(own_refs)
    change = rate(even_and_odd(even_refs, odd_refs), ready_ref, pick_ref)
    sub, _ = positions()
    live = (sub & 1) < count_ref[0, 0]
    for f in range(FIELDS):
        value = 0.5 * start[f] + 0.5 * (own[f] + TIME_STEP * change[f])
        made_ref[pl.ds(f * ROWS, ROWS), :] = jnp.where(live, value, 0.0)
    copy = pltpu.make_async_copy(made_ref, out_ref, sem)
    copy.start()
    copy.wait()


def second_stage(waits_ref, count_ref, ready_ref, pick_ref, *refs):
    n = len(PARTS)
    start_refs, own_refs, even_refs, (out_ref, made_ref, sem) = refs[:n], refs[n : 2 * n], refs[2 * n : 3 * n], refs[3 * n :]

    @pl.when(waits_ref[0, 0] == 0)
    def _():
        advanced_of(start_refs, own_refs, even_refs, [], ready_ref, pick_ref, count_ref, out_ref, made_ref, sem)


def second_stage_odd(waits_ref, count_ref, ready_ref, pick_ref, *refs):
    n = len(PARTS)
    start_refs, own_refs, even_refs = refs[:n], refs[n : 2 * n], refs[2 * n : 3 * n]
    odd_ref, _, out_ref, made_ref, sem = refs[3 * n :]

    @pl.when(waits_ref[0, 0] != 0)
    def _():
        advanced_of(start_refs, own_refs, even_refs, [odd_ref], ready_ref, pick_ref, count_ref, out_ref, made_ref, sem)


def vmem_spec():
    return pl.BlockSpec(memory_space=pltpu.VMEM)


def smem_spec():
    return pl.BlockSpec(memory_space=pltpu.SMEM)


def hbm_spec():
    return pl.BlockSpec(memory_space=pltpu.HBM)


def body(fine_state, coarse_old, box_count, fine_links, coarse_links):
    members = lax.axis_size("sub")
    tile_rows = FIELDS * ROWS
    start = to_tiles(fine_state)
    coarse = coarse_old.transpose(0, 2, 1, 3).reshape(FIELDS, 1, -1, LANES).transpose(0, 2, 1, 3)
    coarse = coarse.reshape(-1, 1, LANES)

    odd = exchange(start, odd_partner)
    group = [in_vmem(exchange(coarse, group_shift(r))) for r in range(1, members)]

    links, corners, own_coarse, *own = pl.pallas_call(
        fetch,
        out_shape=(
            pltpu.SMEM((2, 6), jnp.int32),
            pltpu.SMEM((2, 4, 6), jnp.int32),
            pltpu.VMEM((FIELDS * 4, 1, LANES), jnp.float32),
            *[pltpu.VMEM((rows, LANES), jnp.float32) for _, rows in PARTS],
        ),
        in_specs=[hbm_spec()] * 4,
        out_specs=(smem_spec(), smem_spec(), vmem_spec()) + (vmem_spec(),) * len(PARTS),
        scratch_shapes=[pltpu.SemaphoreType.DMA((3 + len(PARTS),))],
        name="fetch",
    )(
        fine_links.reshape(2, 6),
        coarse_links.transpose(0, 1, 2, 4, 3).reshape(2, 4, 6),
        coarse,
        start,
    )
    even = [in_vmem(exchange(part, even_partner)) for part in own]
    raw = pltpu.VMEM((4, ROWS, LANES), jnp.float32)
    picks, table, waits = pl.pallas_call(
        read_links,
        out_shape=(
            pltpu.VMEM((3 * ROWS, LANES), jnp.int32),
            pltpu.VMEM((16, ROWS, LANES), jnp.float32),
            pltpu.SMEM((2, 6), jnp.int32),
        ),
        in_specs=[smem_spec(), vmem_spec()],
        out_specs=(vmem_spec(), vmem_spec(), smem_spec()),
        scratch_shapes=[raw],
        name="read_links",
    )(in_smem(links), in_vmem(own_coarse))

    ghosts = pl.pallas_call(
        interpolate,
        out_shape=pltpu.VMEM((3 * tile_rows, LANES), jnp.float32),
        in_specs=[smem_spec()] + [vmem_spec()] * members,
        out_specs=vmem_spec(),
        scratch_shapes=[
            pltpu.VMEM((members * 16, ROWS, LANES), jnp.float32),
            raw,
            pltpu.VMEM((3 * tile_rows, LANES), jnp.float32),
        ],
        cost_estimate=pl.CostEstimate(flops=10**10, bytes_accessed=10**10, transcendentals=0),
        name="interpolate",
    )(in_smem(corners), in_vmem(table), *group)

    count = len(PARTS)
    tiles = (tile_rows, LANES)
    waits, picks, ghosts = in_smem(waits), in_vmem(picks), in_vmem(ghosts)
    own = [in_vmem(part) for part in own]

    def fold(parts):
        ready = pl.pallas_call(
            make_ready,
            out_shape=pltpu.VMEM((READY * ROWS, LANES), jnp.float32),
            in_specs=[vmem_spec()] * (2 + count),
            out_specs=vmem_spec(),
            name="fold",
        )(ghosts, picks, *parts)
        return in_vmem(ready)

    made = (pltpu.VMEM(tiles, jnp.float32),) + tuple(pltpu.VMEM((rows, LANES), jnp.float32) for _, rows in PARTS)
    ready = fold(own)
    middle = pl.pallas_call(
        first_stage,
        out_shape=made,
        in_specs=[smem_spec()] + [vmem_spec()] * (2 + 2 * count),
        out_specs=(vmem_spec(),) * len(made),
        name="first_stage",
    )(waits, ready, picks, *own, *even)
    middle, *parts = pl.pallas_call(
        first_stage_odd,
        out_shape=made,
        in_specs=[smem_spec()] + [vmem_spec()] * (4 + 3 * count),
        out_specs=(vmem_spec(),) * len(made),
        input_output_aliases={4 + 2 * count + k: k for k in range(len(made))},
        name="first_stage_odd",
    )(waits, ready, picks, *own, *even, in_vmem(odd), *[in_vmem(m) for m in middle])

    odd = exchange(middle, odd_partner)
    even = [in_vmem(exchange(part, even_partner)) for part in parts]
    parts = [in_vmem(part) for part in parts]
    ready = fold(parts)
    scratch = [pltpu.VMEM(tiles, jnp.float32), pltpu.SemaphoreType.DMA(())]
    result = pl.pallas_call(
        second_stage,
        out_shape=jax.ShapeDtypeStruct(tiles, jnp.float32),
        in_specs=[smem_spec()] * 2 + [vmem_spec()] * (2 + 3 * count),
        out_specs=hbm_spec(),
        scratch_shapes=scratch,
        name="second_stage",
    )(waits, box_count, ready, picks, *own, *parts, *even)
    result = pl.pallas_call(
        second_stage_odd,
        out_shape=jax.ShapeDtypeStruct(tiles, jnp.float32),
        in_specs=[smem_spec()] * 2 + [vmem_spec()] * (3 + 3 * count) + [hbm_spec()],
        out_specs=hbm_spec(),
        scratch_shapes=scratch,
        input_output_aliases={5 + 3 * count: 0},
        name="second_stage_odd",
    )(waits, box_count, ready, picks, *own, *parts, *even, in_vmem(odd), result)
    return from_tiles(result, fine_state.shape)


def solution(mesh):
    placed = (
        P("sfc", "sub", None, None, None),
        P("sfc", "sub", None, None),
        P("sfc", "sub"),
        P("sfc", "sub", None, None),
        P("sfc", "sub", None, None, None),
    )
    return jax.shard_map(
        body,
        mesh=mesh,
        in_specs=placed,
        out_specs=P("sfc", "sub", None, None, None),
        check_vma=False,
    )
```

```python
import jax
import jax.numpy as jnp
from jax import lax
from jax.experimental import pallas as pl
from jax.experimental.pallas import tpu as pltpu
from jax.sharding import PartitionSpec as P

FIELDS = 5
ROWS = 8
LANES = 128
GAMMA = 1.4
FLOOR = 0.1
EPS4 = 4e-06
TIME_STEP = 0.1
PARTS = ((0, 32), (32, 8))
HERE, EVEN, ODD = 1, 3, 5


def to_tiles(boxes):
    slots, fields = boxes.shape[2], boxes.shape[3]
    parts = boxes.reshape(slots, fields, -1, LANES)
    return parts.transpose(1, 2, 0, 3).reshape(-1, LANES)


def from_tiles(tiles, shape):
    slots, fields = shape[2], shape[3]
    parts = tiles.reshape(fields, -1, slots, LANES)
    return parts.transpose(2, 0, 1, 3).reshape(shape)


def in_vmem(value):
    return pltpu.with_memory_space_constraint(value, pltpu.VMEM)


def in_smem(value):
    return pltpu.with_memory_space_constraint(value, pltpu.SMEM)


def exchange(value, partner):
    count, members = lax.axis_size("sfc"), lax.axis_size("sub")
    pairs = []
    for segment in range(count):
        for member in range(members):
            other, other_member = partner(segment, member, count, members)
            pairs.append((segment * members + member, other * members + other_member))
    return lax.ppermute(value, ("sfc", "sub"), pairs)


def even_partner(segment, member, count, members):
    other = segment ^ 1
    return (other, member) if other < count else (segment, member)


def odd_partner(segment, member, count, members):
    other = ((segment - 1) ^ 1) + 1
    if 0 < segment and other < count:
        return (other, member)
    other_member = member ^ 1
    return (segment, other_member) if other_member < members else (segment, member)


def group_shift(steps):
    def partner(segment, member, count, members):
        return (segment, (member + steps) % members)

    return partner


def positions():
    sub = lax.broadcasted_iota(jnp.int32, (ROWS, LANES), 0)
    lane = lax.broadcasted_iota(jnp.int32, (ROWS, LANES), 1)
    return sub, lane


def gather_lanes(value, index):
    return jnp.take_along_axis(value, index, axis=1, mode="promise_in_bounds")


def gather_rows(value, index):
    return jnp.take_along_axis(value, index, axis=0, mode="promise_in_bounds")


def roll_lanes(value, steps):
    return pltpu.roll(value, steps % LANES, 1)


def roll_rows(value, steps):
    if steps % ROWS == 0:
        return value
    sub, _ = positions()
    return gather_rows(value, (sub - steps) & 7)


def reciprocal(value):
    return 1.0 / value


def primitives(mass, mom_x, mom_y, mom_z, energy):
    density = jnp.maximum(mass, FLOOR)
    inverse = reciprocal(density)
    vel_x, vel_y, vel_z = mom_x * inverse, mom_y * inverse, mom_z * inverse
    kinetic = 0.5 * density * (vel_x * vel_x + vel_y * vel_y + vel_z * vel_z)
    pressure = jnp.maximum((GAMMA - 1.0) * (energy - kinetic), FLOOR)
    return [density, vel_x, vel_y, vel_z, pressure]


def load_parts(refs):
    return [ref[pl.ds(at, ROWS), :] for ref in refs for at in range(0, ref.shape[0], ROWS)]


def store_parts(refs, fields):
    fields = list(fields)
    for ref, (_, rows) in zip(refs, PARTS):
        for at in range(0, rows, ROWS):
            ref[pl.ds(at, ROWS), :] = fields.pop(0)


def load_primitives(ref, base=0):
    return primitives(*[ref[pl.ds(base + ROWS * f, ROWS), :] for f in range(FIELDS)])


def minmod(p, q):
    return jnp.maximum(jnp.minimum(p, q), 0.0) + jnp.minimum(jnp.maximum(p, q), 0.0)


def build_table(coarse_ref, raw, table, base):
    sub, lane = positions()
    low = lane < 64
    for j in range(4):
        for f in range(FIELDS):
            raw[j, f : f + 1, :] = coarse_ref[f * 4 + j]
    cells = [raw[j] for j in range(4)]
    halves = [roll_lanes(c, 64) for c in cells]
    for j in range(4):
        u = cells[j]
        up = jnp.where(low, halves[j], halves[min(j + 1, 3)])
        down = jnp.where(low, halves[max(j - 1, 0)], halves[j])
        slopes = (
            0.25 * minmod(up - u, u - down),
            0.25 * minmod(roll_lanes(u, -8) - u, u - roll_lanes(u, 8)),
            0.25 * minmod(roll_lanes(u, -1) - u, u - roll_lanes(u, 1)),
        )
        along_x, along_y, along_z = slopes
        swapped_x, swapped_y, swapped_z = [roll_lanes(v, 64) for v in slopes]
        for x in (2 * j, 2 * j + 1):
            if x in (0, 7):
                continue
            if x % 2 == 0:
                value, slope = jnp.where(low, u, halves[j]), jnp.where(low, along_x, swapped_x)
                sides = jnp.where(low, along_y, swapped_z)
            else:
                value, slope = jnp.where(low, halves[j], u), jnp.where(low, swapped_x, along_x)
                sides = jnp.where(low, swapped_y, along_z)
            value = jnp.where(low, value - slope, value + slope)
            table[base + x] = jnp.where(sub < FIELDS, value, gather_rows(sides, (sub + 3) & 7))
            table[base + 8 + x] = jnp.where(sub < FIELDS, sides, gather_rows(sides, (sub + 6) & 7))


def fetch(links_in, corner_in, coarse_in, start_in, links_ref, corner_ref, coarse_ref, own_ref, sems):
    copies = [(links_in, links_ref), (corner_in, corner_ref), (coarse_in, coarse_ref), (start_in, own_ref)]
    fetches = [pltpu.make_async_copy(src, dst, sems.at[i]) for i, (src, dst) in enumerate(copies)]
    for copy in fetches:
        copy.start()
    for copy in fetches:
        copy.wait()


def read_links(links_ref, coarse_ref, pick_ref, table, code_ref, raw):
    sub, lane = positions()
    y, z = (lane >> 3) & 7, lane & 7
    odd_segment = lax.axis_index("sfc") & 1
    build_table(coarse_ref, raw, table, 0)

    def choice(slot, face):
        link = links_ref[slot, face]
        offset = link >> 1
        below = jnp.where(offset == 0, 1, 0)
        block = jnp.where(offset == 1, 0, jnp.where(below == odd_segment, 1, 2))
        swapped = (link & 1) ^ slot
        return jnp.where(link < 0, 0, 1 + block * 2 + swapped)

    codes = [[choice(slot, face) for face in range(6)] for slot in range(2)]
    waits = jnp.int32(0)
    for code in codes[0] + codes[1]:
        waits = jnp.maximum(waits, jnp.where(code >= ODD, 1, 0))
    code_ref[0, 0] = waits

    first = (sub & 1) == 0
    for direction in range(3):
        lower = (sub < 4) if direction == 0 else ((y if direction == 1 else z) < 4)
        minus = jnp.where(first, codes[0][2 * direction], codes[1][2 * direction])
        plus = jnp.where(first, codes[0][2 * direction + 1], codes[1][2 * direction + 1])
        pick_ref[pl.ds(direction * ROWS, ROWS), :] = jnp.where(lower, plus, minus)


def interpolate(corner_ref, own_table, *refs):
    coarse_refs, (ghost_ref, table, raw, lines) = refs[:-4], refs[-4:]
    members = len(coarse_refs) + 1
    sub, lane = positions()
    y, z = (lane >> 3) & 7, lane & 7
    me = lax.axis_index("sub")
    table[0:16] = own_table[...]
    for m, coarse_ref in enumerate(coarse_refs):
        build_table(coarse_ref, raw, table, (m + 1) * 16)

    sign_y = jnp.where((y & 1) == 0, -1.0, 1.0)
    sign_z = jnp.where((z & 1) == 0, -1.0, 1.0)
    spread = (y >> 1) * 8 + (z >> 1)
    upper, whole = jnp.where(sub < FIELDS, lane & 64, 0), jnp.where(sub < FIELDS, 64, 0)

    def finder(slot, face):
        direction, minus = face // 2, face % 2 == 0
        start = [corner_ref[slot, 1 + a, face] + (-1 if minus and a == direction else 1) for a in range(3)]
        owner = me - corner_ref[slot, 0, face]
        owner = jnp.where(owner < 0, owner + members, owner)
        index = (spread + (start[1] * 8 + start[2])) & 63
        first, second, row = index | upper, index | whole, owner * 16 + start[0]

        def find(j):
            return gather_lanes(table[row + j], first), gather_lanes(table[row + 8 + j], second)

        return find

    for direction in range(3):
        for slot in range(2):
            minus, plus = finder(slot, 2 * direction), finder(slot, 2 * direction + 1)
            for j in range(4):
                if direction == 0:
                    value, sides = (minus if j >= 2 else plus)(j)
                else:
                    lower = (y if direction == 1 else z) < 4
                    value, sides = [jnp.where(lower, p, m) for p, m in zip(plus(j), minus(j))]
                along_y = jnp.where(sub < 3, gather_rows(value, (sub + 5) & 7), gather_rows(sides, (sub + 2) & 7))
                value = value + sign_y * along_y + sign_z * sides
                rows = pl.ds(direction * 40 + j * 2 + slot, FIELDS, stride=ROWS)
                lines[rows, :] = value[0:FIELDS, :]
        made = load_primitives(lines, direction * 40)
        for f in range(FIELDS):
            ghost_ref[pl.ds(direction * 40 + f * ROWS, ROWS), :] = made[f]


def weno(cells):
    centre = cells[2]
    e0, e1, e2, e3 = [cells[k + 1] - cells[k] for k in range(4)]
    d1, d2, d3 = e1 - e0, e2 - e1, e3 - e2
    below, above, across = 3.0 * e1 - e0, 3.0 * e2 - e3, e1 + e2
    a = ((13.0 / 3.0) * (d1 * d1) + EPS4) + below * below
    b = ((13.0 / 3.0) * (d2 * d2) + EPS4) + across * across
    c = ((13.0 / 3.0) * (d3 * d3) + EPS4) + above * above
    bc, ac, ab = b * c, a * c, a * b
    bc, ac, ab = bc * bc, 6.0 * (ac * ac), ab * ab
    bc3, ab3 = 3.0 * bc, 3.0 * ab
    up = bc * (2.0 * below - e1) + ac * (across + e2) + ab3 * (above + e2)
    down = ab * (2.0 * above - e2) + ac * (across + e1) + bc3 * (below + e1)
    upper = centre + up * ((1.0 / 6.0) * reciprocal(bc + ac + ab3))
    lower = centre - down * ((1.0 / 6.0) * reciprocal(ab + ac + bc3))
    return upper, lower


def hllc(left, right):
    rl, ul, vl, wl, pl_ = jnp.maximum(left[0], FLOOR), left[1], left[2], left[3], jnp.maximum(left[4], FLOOR)
    rr, ur, vr, wr, pr = jnp.maximum(right[0], FLOOR), right[1], right[2], right[3], jnp.maximum(right[4], FLOOR)
    gl, gr = GAMMA * pl_, GAMMA * pr
    cl, cr = gl * lax.rsqrt(gl * rl), gr * lax.rsqrt(gr * rr)
    speed_left = jnp.minimum(ul - cl, ur - cr)
    speed_right = jnp.maximum(ul + cl, ur + cr)
    ml, mr = rl * (speed_left - ul), rr * (speed_right - ur)
    contact = (pr - pl_ + ml * ul - mr * ur) * reciprocal(ml - mr)
    from_left = (speed_left >= 0.0) | (contact >= 0.0)
    r = jnp.where(from_left, rl, rr)
    u = jnp.where(from_left, ul, ur)
    v = jnp.where(from_left, vl, vr)
    w = jnp.where(from_left, wl, wr)
    p = jnp.where(from_left, pl_, pr)
    s = jnp.where(from_left, speed_left, speed_right)
    m = jnp.where(from_left, ml, mr)
    star = (speed_left < 0.0) & ((contact >= 0.0) | (speed_right >= 0.0))
    energy = p * (1.0 / (GAMMA - 1.0)) + 0.5 * r * (u * u + v * v + w * w)
    inverse = reciprocal(s - contact)
    star_p = p + m * (contact - u)
    star_e = ((s - u) * energy - p * u + star_p * contact) * inverse
    density = jnp.where(star, m * inverse, r)
    normal = jnp.where(star, contact, u)
    pressure = jnp.where(star, star_p, p)
    energy = jnp.where(star, star_e, energy)
    mass = density * normal
    return [mass, mass * normal + pressure, mass * v, mass * w, normal * (energy + pressure)]


class Turns:
    def __init__(self):
        sub, lane = positions()
        self.sub = sub
        y, z = (lane >> 3) & 7, lane & 7
        high = lane >> 6
        self.steps = (
            (sub ^ high, lane ^ ((sub & 1) << 6), sub ^ high),
            ((sub - y) & 7, (lane & 71) | (((sub - y) & 7) << 3), (sub + y) & 7),
            ((sub - z) & 7, (lane & 120) | ((sub - z) & 7), (sub + z) & 7),
        )

    def __call__(self, direction, value):
        before, across, after = self.steps[direction]
        return gather_rows(gather_lanes(gather_rows(value, before), across), after)


def swapped_slots(value, sub):
    return gather_rows(value, sub ^ 1)


OWN, GHOST, READY = 0, 15, 30


def make_ready(ghost_ref, pick_ref, *refs):
    own_refs, ready_ref = refs[:-1], refs[-1]
    turn = Turns()
    own = primitives(*load_parts(own_refs))
    candidates = [own, [swapped_slots(v, turn.sub) for v in own]]
    for direction in range(3):
        pick = pick_ref[pl.ds(direction * ROWS, ROWS), :]
        wanted = [pick == c + 1 for c in range(len(candidates))]
        remote = pick > len(candidates)
        for f in range(FIELDS):
            value = ghost_ref[pl.ds((direction * FIELDS + f) * ROWS, ROWS), :]
            for c, candidate in enumerate(candidates):
                value = jnp.where(wanted[c], candidate[f], value)
            value = jnp.where(remote, 0.0, value)
            tile = direction * FIELDS + f
            ready_ref[pl.ds((GHOST + tile) * ROWS, ROWS), :] = turn(direction, value)
            ready_ref[pl.ds((OWN + tile) * ROWS, ROWS), :] = turn(direction, own[f])


def rate(blocks, ready_ref, pick_ref):
    turn = Turns()
    sub = turn.sub
    first_row = sub == 0
    candidates = []
    for block in blocks:
        candidates += [block, [swapped_slots(v, sub) for v in block]]

    def line(direction, f):
        pick = pick_ref[pl.ds(direction * ROWS, ROWS), :]
        tile = direction * FIELDS + f
        remote = jnp.zeros((ROWS, LANES), jnp.float32)
        for c, candidate in enumerate(candidates):
            remote = jnp.where(pick == EVEN + c, candidate[f], remote)
        ghost = ready_ref[pl.ds((GHOST + tile) * ROWS, ROWS), :] + turn(direction, remote)
        return ready_ref[pl.ds((OWN + tile) * ROWS, ROWS), :], ghost

    is_x, is_y = (sub == 7) | first_row, (sub == 1) | (sub == 2)
    places = (0, 2, 4)
    sides = [[], [], []]
    outer = []
    for f in range(FIELDS):
        beside = []
        for direction in range(3):
            own, ghost = line(direction, f)
            cells, around = [], []
            for s in range(-2, 3):
                if s == 0:
                    cells.append(own)
                    around.append(ghost)
                    continue
                own_s, ghost_s = roll_rows(own, -s), roll_rows(ghost, -s)
                outside = (sub + s < 0) | (sub + s > 7)
                cells.append(jnp.where(outside, ghost_s, own_s))
                at_first, at_last = (own_s, ghost_s) if s < 0 else (ghost_s, own_s)
                around.append(jnp.where(first_row, at_first, at_last))
            sides[direction].append(weno(cells))
            beside.append(around)
        outer.append(
            weno(
                [
                    jnp.where(is_x, vx, jnp.where(is_y, roll_rows(vy, 2), roll_rows(vz, 4)))
                    for vx, vy, vz in zip(*beside)
                ]
            )
        )

    ended = []
    fluxes = []
    orders = ((0, 1, 2, 3, 4), (0, 2, 1, 3, 4), (0, 3, 1, 2, 4))
    for direction in range(3):
        rolled = [roll_rows(side[0], 1) for side in sides[direction]]
        ended.append([roll_rows(v, places[direction]) for v in rolled])
        lefts = [jnp.where(first_row, roll_rows(o[0], 1 - places[direction]), v) for o, v in zip(outer, rolled)]
        rights = [side[1] for side in sides[direction]]
        order = orders[direction]
        fluxes.append(hllc([lefts[f] for f in order], [rights[f] for f in order]))

    at_y, at_z = sub == 2, sub == 4

    def turned(values):
        normal = jnp.where(at_y, values[2], jnp.where(at_z, values[3], values[1]))
        one = jnp.where(at_y | at_z, values[1], values[2])
        two = jnp.where(at_z, values[2], values[3])
        return [values[0], normal, one, two, values[4]]

    left_end = [jnp.where(at_y, ended[1][f], jnp.where(at_z, ended[2][f], ended[0][f])) for f in range(FIELDS)]
    last = hllc(turned(left_end), turned([o[1] for o in outer]))

    total = [None] * FIELDS
    for direction in range(3):
        for place, f in enumerate(orders[direction]):
            flux = fluxes[direction][place]
            merged = jnp.where(first_row, roll_rows(last[place], -places[direction]), flux)
            change = turn(direction, flux - roll_rows(merged, -1))
            total[f] = change if total[f] is None else total[f] + change
    return total


def even_and_odd(even_refs, odd_refs):
    blocks = [primitives(*load_parts(even_refs))]
    return blocks + [load_primitives(ref) for ref in odd_refs]


def middle_of(own_refs, even_refs, odd_refs, ready_ref, pick_ref, out_ref, part_refs):
    own = load_parts(own_refs)
    change = rate(even_and_odd(even_refs, odd_refs), ready_ref, pick_ref)
    middle = [own[f] + TIME_STEP * change[f] for f in range(FIELDS)]
    store_parts(part_refs, middle)
    for f in range(FIELDS):
        out_ref[pl.ds(f * ROWS, ROWS), :] = middle[f]


def first_stage(waits_ref, ready_ref, pick_ref, own_ref, even_ref, *made):
    @pl.when(waits_ref[0, 0] == 0)
    def _():
        middle_of([own_ref], [even_ref], [], ready_ref, pick_ref, made[0], made[1:])


def first_stage_odd(waits_ref, ready_ref, pick_ref, own_ref, even_ref, odd_ref, *refs):
    made = refs[len(refs) // 2 :]

    @pl.when(waits_ref[0, 0] != 0)
    def _():
        middle_of([own_ref], [even_ref], [odd_ref], ready_ref, pick_ref, made[0], made[1:])


def advanced_of(start_refs, own_refs, even_refs, odd_refs, ready_ref, pick_ref, count_ref, out_ref, made_ref, sem):
    start, own = load_parts(start_refs), load_parts(own_refs)
    change = rate(even_and_odd(even_refs, odd_refs), ready_ref, pick_ref)
    sub, _ = positions()
    live = (sub & 1) < count_ref[0, 0]
    for f in range(FIELDS):
        value = 0.5 * start[f] + 0.5 * (own[f] + TIME_STEP * change[f])
        made_ref[pl.ds(f * ROWS, ROWS), :] = jnp.where(live, value, 0.0)
    copy = pltpu.make_async_copy(made_ref, out_ref, sem)
    copy.start()
    copy.wait()


def second_stage(waits_ref, count_ref, ready_ref, pick_ref, start_ref, *refs):
    n = len(PARTS)
    own_refs, even_refs, (out_ref, made_ref, sem) = refs[:n], refs[n : 2 * n], refs[2 * n :]

    @pl.when(waits_ref[0, 0] == 0)
    def _():
        advanced_of([start_ref], own_refs, even_refs, [], ready_ref, pick_ref, count_ref, out_ref, made_ref, sem)


def second_stage_odd(waits_ref, count_ref, ready_ref, pick_ref, start_ref, *refs):
    n = len(PARTS)
    own_refs, even_refs, (odd_ref, _, out_ref, made_ref, sem) = refs[:n], refs[n : 2 * n], refs[2 * n :]

    @pl.when(waits_ref[0, 0] != 0)
    def _():
        advanced_of([start_ref], own_refs, even_refs, [odd_ref], ready_ref, pick_ref, count_ref, out_ref, made_ref, sem)


def vmem_spec():
    return pl.BlockSpec(memory_space=pltpu.VMEM)


def smem_spec():
    return pl.BlockSpec(memory_space=pltpu.SMEM)


def hbm_spec():
    return pl.BlockSpec(memory_space=pltpu.HBM)


def body(fine_state, coarse_old, box_count, fine_links, coarse_links):
    members = lax.axis_size("sub")
    tile_rows = FIELDS * ROWS
    start = to_tiles(fine_state)
    coarse = coarse_old.transpose(0, 2, 1, 3).reshape(FIELDS, 1, -1, LANES).transpose(0, 2, 1, 3)
    coarse = coarse.reshape(-1, 1, LANES)

    odd = exchange(start, odd_partner)
    group = [in_vmem(exchange(coarse, group_shift(r))) for r in range(1, members)]

    links, corners, own_coarse, own = pl.pallas_call(
        fetch,
        out_shape=(
            pltpu.SMEM((2, 6), jnp.int32),
            pltpu.SMEM((2, 4, 6), jnp.int32),
            pltpu.VMEM((FIELDS * 4, 1, LANES), jnp.float32),
            pltpu.VMEM((tile_rows, LANES), jnp.float32),
        ),
        in_specs=[hbm_spec()] * 4,
        out_specs=(smem_spec(), smem_spec(), vmem_spec(), vmem_spec()),
        scratch_shapes=[pltpu.SemaphoreType.DMA((4,))],
        name="fetch",
    )(
        fine_links.reshape(2, 6),
        coarse_links.transpose(0, 1, 2, 4, 3).reshape(2, 4, 6),
        coarse,
        start,
    )
    even = in_vmem(exchange(own, even_partner))
    raw = pltpu.VMEM((4, ROWS, LANES), jnp.float32)
    picks, table, waits = pl.pallas_call(
        read_links,
        out_shape=(
            pltpu.VMEM((3 * ROWS, LANES), jnp.int32),
            pltpu.VMEM((16, ROWS, LANES), jnp.float32),
            pltpu.SMEM((2, 6), jnp.int32),
        ),
        in_specs=[smem_spec(), vmem_spec()],
        out_specs=(vmem_spec(), vmem_spec(), smem_spec()),
        scratch_shapes=[raw],
        name="read_links",
    )(in_smem(links), in_vmem(own_coarse))

    ghosts = pl.pallas_call(
        interpolate,
        out_shape=pltpu.VMEM((3 * tile_rows, LANES), jnp.float32),
        in_specs=[smem_spec()] + [vmem_spec()] * members,
        out_specs=vmem_spec(),
        scratch_shapes=[
            pltpu.VMEM((members * 16, ROWS, LANES), jnp.float32),
            raw,
            pltpu.VMEM((3 * tile_rows, LANES), jnp.float32),
        ],
        cost_estimate=pl.CostEstimate(flops=10**10, bytes_accessed=10**10, transcendentals=0),
        name="interpolate",
    )(in_smem(corners), in_vmem(table), *group)

    count = len(PARTS)
    tiles = (tile_rows, LANES)
    waits, picks, ghosts = in_smem(waits), in_vmem(picks), in_vmem(ghosts)
    own = in_vmem(own)

    def fold(parts):
        ready = pl.pallas_call(
            make_ready,
            out_shape=pltpu.VMEM((READY * ROWS, LANES), jnp.float32),
            in_specs=[vmem_spec()] * (2 + len(parts)),
            out_specs=vmem_spec(),
            name="fold",
        )(ghosts, picks, *parts)
        return in_vmem(ready)

    made = (pltpu.VMEM(tiles, jnp.float32),) + tuple(pltpu.VMEM((rows, LANES), jnp.float32) for _, rows in PARTS)
    ready = fold([own])
    middle = pl.pallas_call(
        first_stage,
        out_shape=made,
        in_specs=[smem_spec()] + [vmem_spec()] * 4,
        out_specs=(vmem_spec(),) * len(made),
        name="first_stage",
    )(waits, ready, picks, own, even)
    middle, *parts = pl.pallas_call(
        first_stage_odd,
        out_shape=made,
        in_specs=[smem_spec()] + [vmem_spec()] * (5 + len(made)),
        out_specs=(vmem_spec(),) * len(made),
        input_output_aliases={6 + k: k for k in range(len(made))},
        name="first_stage_odd",
    )(waits, ready, picks, own, even, in_vmem(odd), *[in_vmem(m) for m in middle])

    odd = exchange(middle, odd_partner)
    even = [in_vmem(exchange(part, even_partner)) for part in parts]
    parts = [in_vmem(part) for part in parts]
    ready = fold(parts)
    scratch = [pltpu.VMEM(tiles, jnp.float32), pltpu.SemaphoreType.DMA(())]
    result = pl.pallas_call(
        second_stage,
        out_shape=jax.ShapeDtypeStruct(tiles, jnp.float32),
        in_specs=[smem_spec()] * 2 + [vmem_spec()] * (3 + 2 * count),
        out_specs=hbm_spec(),
        scratch_shapes=scratch,
        name="second_stage",
    )(waits, box_count, ready, picks, own, *parts, *even)
    result = pl.pallas_call(
        second_stage_odd,
        out_shape=jax.ShapeDtypeStruct(tiles, jnp.float32),
        in_specs=[smem_spec()] * 2 + [vmem_spec()] * (4 + 2 * count) + [hbm_spec()],
        out_specs=hbm_spec(),
        scratch_shapes=scratch,
        input_output_aliases={6 + 2 * count: 0},
        name="second_stage_odd",
    )(waits, box_count, ready, picks, own, *parts, *even, in_vmem(odd), result)
    return from_tiles(result, fine_state.shape)


def solution(mesh):
    placed = (
        P("sfc", "sub", None, None, None),
        P("sfc", "sub", None, None),
        P("sfc", "sub"),
        P("sfc", "sub", None, None),
        P("sfc", "sub", None, None, None),
    )
    return jax.shard_map(
        body,
        mesh=mesh,
        in_specs=placed,
        out_specs=P("sfc", "sub", None, None, None),
        check_vma=False,
    )
```

```python
import jax
import jax.numpy as jnp
from jax import lax
from jax.experimental import pallas as pl
from jax.experimental.pallas import tpu as pltpu
from jax.sharding import PartitionSpec as P

FIELDS = 5
ROWS = 8
LANES = 128
GAMMA = 1.4
FLOOR = 0.1
WENO_EPS = 1e-06
TIME_STEP = 0.1
PARTS = ((0, 32), (32, 8))
HERE, EVEN, ODD = 1, 3, 5


def to_tiles(boxes):
    slots, fields = boxes.shape[2], boxes.shape[3]
    parts = boxes.reshape(slots, fields, -1, LANES)
    return parts.transpose(1, 2, 0, 3).reshape(-1, LANES)


def from_tiles(tiles, shape):
    slots, fields = shape[2], shape[3]
    parts = tiles.reshape(fields, -1, slots, LANES)
    return parts.transpose(2, 0, 1, 3).reshape(shape)


def in_vmem(value):
    return pltpu.with_memory_space_constraint(value, pltpu.VMEM)


def in_smem(value):
    return pltpu.with_memory_space_constraint(value, pltpu.SMEM)


def exchange(value, partner):
    count, members = lax.axis_size("sfc"), lax.axis_size("sub")
    pairs = []
    for segment in range(count):
        for member in range(members):
            other, other_member = partner(segment, member, count, members)
            pairs.append((segment * members + member, other * members + other_member))
    return lax.ppermute(value, ("sfc", "sub"), pairs)


def even_partner(segment, member, count, members):
    other = segment ^ 1
    return (other, member) if other < count else (segment, member)


def odd_partner(segment, member, count, members):
    other = ((segment - 1) ^ 1) + 1
    if 0 < segment and other < count:
        return (other, member)
    other_member = member ^ 1
    return (segment, other_member) if other_member < members else (segment, member)


def group_shift(steps):
    def partner(segment, member, count, members):
        return (segment, (member + steps) % members)

    return partner


def positions():
    sub = lax.broadcasted_iota(jnp.int32, (ROWS, LANES), 0)
    lane = lax.broadcasted_iota(jnp.int32, (ROWS, LANES), 1)
    return sub, lane


def gather_lanes(value, index):
    return jnp.take_along_axis(value, index, axis=1, mode="promise_in_bounds")


def gather_rows(value, index):
    return jnp.take_along_axis(value, index, axis=0, mode="promise_in_bounds")


def roll_lanes(value, steps):
    return pltpu.roll(value, steps % LANES, 1)


def roll_rows(value, steps):
    if steps % ROWS == 0:
        return value
    sub, _ = positions()
    return gather_rows(value, (sub - steps) & 7)


def reciprocal(value):
    return 1.0 / value


def primitives(mass, mom_x, mom_y, mom_z, energy):
    density = jnp.maximum(mass, FLOOR)
    inverse = reciprocal(density)
    vel_x, vel_y, vel_z = mom_x * inverse, mom_y * inverse, mom_z * inverse
    kinetic = 0.5 * density * (vel_x * vel_x + vel_y * vel_y + vel_z * vel_z)
    pressure = jnp.maximum((GAMMA - 1.0) * (energy - kinetic), FLOOR)
    return [density, vel_x, vel_y, vel_z, pressure]


def load_parts(refs):
    return [ref[pl.ds(at, ROWS), :] for ref in refs for at in range(0, ref.shape[0], ROWS)]


def store_parts(refs, fields):
    fields = list(fields)
    for ref, (_, rows) in zip(refs, PARTS):
        for at in range(0, rows, ROWS):
            ref[pl.ds(at, ROWS), :] = fields.pop(0)


def load_primitives(ref, base=0):
    return primitives(*[ref[pl.ds(base + ROWS * f, ROWS), :] for f in range(FIELDS)])


def minmod(p, q):
    return jnp.maximum(jnp.minimum(p, q), 0.0) + jnp.minimum(jnp.maximum(p, q), 0.0)


def build_table(coarse_ref, raw, table, base):
    sub, lane = positions()
    low = lane < 64
    for j in range(4):
        for f in range(FIELDS):
            raw[j, f : f + 1, :] = coarse_ref[f * 4 + j]
    cells = [raw[j] for j in range(4)]
    halves = [roll_lanes(c, 64) for c in cells]
    for j in range(4):
        u = cells[j]
        up = jnp.where(low, halves[j], halves[min(j + 1, 3)])
        down = jnp.where(low, halves[max(j - 1, 0)], halves[j])
        slopes = (
            0.25 * minmod(up - u, u - down),
            0.25 * minmod(roll_lanes(u, -8) - u, u - roll_lanes(u, 8)),
            0.25 * minmod(roll_lanes(u, -1) - u, u - roll_lanes(u, 1)),
        )
        along_x, along_y, along_z = slopes
        swapped_x, swapped_y, swapped_z = [roll_lanes(v, 64) for v in slopes]
        for x in (2 * j, 2 * j + 1):
            if x in (0, 7):
                continue
            if x % 2 == 0:
                value, slope = jnp.where(low, u, halves[j]), jnp.where(low, along_x, swapped_x)
                sides = jnp.where(low, along_y, swapped_z)
            else:
                value, slope = jnp.where(low, halves[j], u), jnp.where(low, swapped_x, along_x)
                sides = jnp.where(low, swapped_y, along_z)
            value = jnp.where(low, value - slope, value + slope)
            table[base + x] = jnp.where(sub < FIELDS, value, gather_rows(sides, (sub + 3) & 7))
            table[base + 8 + x] = jnp.where(sub < FIELDS, sides, gather_rows(sides, (sub + 6) & 7))


def fetch(links_in, corner_in, coarse_in, start_in, links_ref, corner_ref, coarse_ref, own_ref, sems):
    copies = [(links_in, links_ref), (corner_in, corner_ref), (coarse_in, coarse_ref), (start_in, own_ref)]
    fetches = [pltpu.make_async_copy(src, dst, sems.at[i]) for i, (src, dst) in enumerate(copies)]
    for copy in fetches:
        copy.start()
    for copy in fetches:
        copy.wait()


def read_links(links_ref, coarse_ref, pick_ref, table, code_ref, raw):
    sub, lane = positions()
    y, z = (lane >> 3) & 7, lane & 7
    odd_segment = lax.axis_index("sfc") & 1
    build_table(coarse_ref, raw, table, 0)

    def choice(slot, face):
        link = links_ref[slot, face]
        offset = link >> 1
        below = jnp.where(offset == 0, 1, 0)
        block = jnp.where(offset == 1, 0, jnp.where(below == odd_segment, 1, 2))
        swapped = (link & 1) ^ slot
        return jnp.where(link < 0, 0, 1 + block * 2 + swapped)

    codes = [[choice(slot, face) for face in range(6)] for slot in range(2)]
    waits = jnp.int32(0)
    for code in codes[0] + codes[1]:
        waits = jnp.maximum(waits, jnp.where(code >= ODD, 1, 0))
    code_ref[0, 0] = waits

    first = (sub & 1) == 0
    for direction in range(3):
        lower = (sub < 4) if direction == 0 else ((y if direction == 1 else z) < 4)
        minus = jnp.where(first, codes[0][2 * direction], codes[1][2 * direction])
        plus = jnp.where(first, codes[0][2 * direction + 1], codes[1][2 * direction + 1])
        pick_ref[pl.ds(direction * ROWS, ROWS), :] = jnp.where(lower, plus, minus)


def interpolate(corner_ref, own_table, *refs):
    coarse_refs, (ghost_ref, table, raw, lines) = refs[:-4], refs[-4:]
    members = len(coarse_refs) + 1
    sub, lane = positions()
    y, z = (lane >> 3) & 7, lane & 7
    me = lax.axis_index("sub")
    table[0:16] = own_table[...]
    for m, coarse_ref in enumerate(coarse_refs):
        build_table(coarse_ref, raw, table, (m + 1) * 16)

    sign_y = jnp.where((y & 1) == 0, -1.0, 1.0)
    sign_z = jnp.where((z & 1) == 0, -1.0, 1.0)
    spread = (y >> 1) * 8 + (z >> 1)
    upper, whole = jnp.where(sub < FIELDS, lane & 64, 0), jnp.where(sub < FIELDS, 64, 0)

    def finder(slot, face):
        direction, minus = face // 2, face % 2 == 0
        start = [corner_ref[slot, 1 + a, face] + (-1 if minus and a == direction else 1) for a in range(3)]
        owner = me - corner_ref[slot, 0, face]
        owner = jnp.where(owner < 0, owner + members, owner)
        index = (spread + (start[1] * 8 + start[2])) & 63
        first, second, row = index | upper, index | whole, owner * 16 + start[0]

        def find(j):
            return gather_lanes(table[row + j], first), gather_lanes(table[row + 8 + j], second)

        return find

    for direction in range(3):
        for slot in range(2):
            minus, plus = finder(slot, 2 * direction), finder(slot, 2 * direction + 1)
            for j in range(4):
                if direction == 0:
                    value, sides = (minus if j >= 2 else plus)(j)
                else:
                    lower = (y if direction == 1 else z) < 4
                    value, sides = [jnp.where(lower, p, m) for p, m in zip(plus(j), minus(j))]
                along_y = jnp.where(sub < 3, gather_rows(value, (sub + 5) & 7), gather_rows(sides, (sub + 2) & 7))
                value = value + sign_y * along_y + sign_z * sides
                rows = pl.ds(direction * 40 + j * 2 + slot, FIELDS, stride=ROWS)
                lines[rows, :] = value[0:FIELDS, :]
        made = load_primitives(lines, direction * 40)
        for f in range(FIELDS):
            ghost_ref[pl.ds(direction * 40 + f * ROWS, ROWS), :] = made[f]


def weno(cells, both=True):
    centre = cells[2]
    e0, e1, e2, e3 = [cells[k + 1] - cells[k] for k in range(4)]
    d1, d2, d3 = e1 - e0, e2 - e1, e3 - e2
    a = ((4.0 / 3.0) * (d1 * d1) + WENO_EPS) + e1 * (e1 + d1)
    b = ((4.0 / 3.0) * (d2 * d2) + WENO_EPS) + e1 * e2
    c = ((4.0 / 3.0) * (d3 * d3) + WENO_EPS) + e2 * (e2 - d3)
    bc, ac, ab = b * c, a * c, a * b
    bc, ac, ab = bc * bc, 6.0 * (ac * ac), ab * ab
    with_ab, with_bc = 3.0 * ab + ac, 3.0 * bc + ac
    low, high = bc * d1, ab * d3
    twice = 2.0 * (high - low)
    up = with_bc * d2 + (twice + high)
    upper = (centre + 0.5 * e2) - up * ((1.0 / 6.0) * reciprocal(bc + with_ab))
    if not both:
        return upper
    down = with_ab * d2 + (low - twice)
    lower = (centre - 0.5 * e1) - down * ((1.0 / 6.0) * reciprocal(ab + with_bc))
    return upper, lower


def hllc(left, right):
    rl, ul, vl, wl, pl_ = jnp.maximum(left[0], FLOOR), left[1], left[2], left[3], jnp.maximum(left[4], FLOOR)
    rr, ur, vr, wr, pr = jnp.maximum(right[0], FLOOR), right[1], right[2], right[3], jnp.maximum(right[4], FLOOR)
    gl, gr = GAMMA * pl_, GAMMA * pr
    cl, cr = gl * lax.rsqrt(gl * rl), gr * lax.rsqrt(gr * rr)
    speed_left = jnp.minimum(ul - cl, ur - cr)
    speed_right = jnp.maximum(ul + cl, ur + cr)
    ml, mr = rl * (speed_left - ul), rr * (speed_right - ur)
    contact = (pr - pl_ + ml * ul - mr * ur) * reciprocal(ml - mr)
    from_left = (speed_left >= 0.0) | (contact >= 0.0)
    r = jnp.where(from_left, rl, rr)
    u = jnp.where(from_left, ul, ur)
    v = jnp.where(from_left, vl, vr)
    w = jnp.where(from_left, wl, wr)
    p = jnp.where(from_left, pl_, pr)
    s = jnp.where(from_left, speed_left, speed_right)
    m = jnp.where(from_left, ml, mr)
    star = (speed_left < 0.0) & ((contact >= 0.0) | (speed_right >= 0.0))
    energy = p * (1.0 / (GAMMA - 1.0)) + 0.5 * r * (u * u + v * v + w * w)
    inverse = reciprocal(s - contact)
    star_p = p + m * (contact - u)
    star_e = ((s - u) * energy - p * u + star_p * contact) * inverse
    density = jnp.where(star, m * inverse, r)
    normal = jnp.where(star, contact, u)
    pressure = jnp.where(star, star_p, p)
    energy = jnp.where(star, star_e, energy)
    mass = density * normal
    return [mass, mass * normal + pressure, mass * v, mass * w, normal * (energy + pressure)]


class Turns:
    def __init__(self):
        sub, lane = positions()
        self.sub = sub
        y, z = (lane >> 3) & 7, lane & 7
        high = lane >> 6
        self.steps = (
            (sub ^ high, lane ^ ((sub & 1) << 6), sub ^ high),
            ((sub - y) & 7, (lane & 71) | (((sub - y) & 7) << 3), (sub + y) & 7),
            ((sub - z) & 7, (lane & 120) | ((sub - z) & 7), (sub + z) & 7),
        )

    def __call__(self, direction, value):
        before, across, after = self.steps[direction]
        return gather_rows(gather_lanes(gather_rows(value, before), across), after)


def swapped_slots(value, sub):
    return gather_rows(value, sub ^ 1)


OWN, GHOST, SHIFTED, READY = 0, 15, 30, 90
SHIFTS = (-2, -1, 1, 2)


def make_ready(ghost_ref, pick_ref, *refs):
    own_refs, ready_ref = refs[:-1], refs[-1]
    turn = Turns()
    own = primitives(*load_parts(own_refs))
    candidates = [own, [swapped_slots(v, turn.sub) for v in own]]
    for direction in range(3):
        pick = pick_ref[pl.ds(direction * ROWS, ROWS), :]
        wanted = [pick == c + 1 for c in range(len(candidates))]
        remote = pick > len(candidates)
        for f in range(FIELDS):
            value = ghost_ref[pl.ds((direction * FIELDS + f) * ROWS, ROWS), :]
            for c, candidate in enumerate(candidates):
                value = jnp.where(wanted[c], candidate[f], value)
            value = jnp.where(remote, 0.0, value)
            tile = direction * FIELDS + f
            ready_ref[pl.ds((GHOST + tile) * ROWS, ROWS), :] = turn(direction, value)
            cells = turn(direction, own[f])
            ready_ref[pl.ds((OWN + tile) * ROWS, ROWS), :] = cells
            for k, s in enumerate(SHIFTS):
                ready_ref[pl.ds((SHIFTED + tile * len(SHIFTS) + k) * ROWS, ROWS), :] = roll_rows(cells, -s)


def rate(blocks, ready_ref, pick_ref):
    turn = Turns()
    sub = turn.sub
    first_row = sub == 0
    candidates = []
    for block in blocks:
        candidates += [block, [swapped_slots(v, sub) for v in block]]

    def line(direction, f):
        pick = pick_ref[pl.ds(direction * ROWS, ROWS), :]
        tile = direction * FIELDS + f
        remote = jnp.zeros((ROWS, LANES), jnp.float32)
        for c, candidate in enumerate(candidates):
            remote = jnp.where(pick == EVEN + c, candidate[f], remote)
        ghost = ready_ref[pl.ds((GHOST + tile) * ROWS, ROWS), :] + turn(direction, remote)
        return ready_ref[pl.ds((OWN + tile) * ROWS, ROWS), :], ghost

    is_x, is_y = (sub == 7) | first_row, (sub == 1) | (sub == 2)
    places = (0, 2, 4)
    sides = [[], [], []]
    outer = []
    for f in range(FIELDS):
        beside = []
        for direction in range(3):
            own, ghost = line(direction, f)
            cells, around = [], []
            rolled_own, rolled_ghost = {}, {}
            for s in range(-2, 3):
                if s == 0:
                    cells.append(own)
                    continue
                shifted = SHIFTED + (direction * FIELDS + f) * len(SHIFTS) + SHIFTS.index(s)
                own_s, ghost_s = ready_ref[pl.ds(shifted * ROWS, ROWS), :], roll_rows(ghost, -s)
                outside = (sub + s < 0) | (sub + s > 7)
                cells.append(jnp.where(outside, ghost_s, own_s))
                rolled_own[s], rolled_ghost[s] = own_s, ghost_s
            for s in range(-2, 3):
                if s == 0:
                    around.append(ghost)
                elif s < 0:
                    around.append(jnp.where(first_row, rolled_ghost[-s], rolled_ghost[s]))
                else:
                    around.append(jnp.where(first_row, rolled_own[-s], rolled_own[s]))
            sides[direction].append(weno(cells))
            beside.append(around)
        outer.append(
            weno(
                [
                    jnp.where(is_x, vx, jnp.where(is_y, roll_rows(vy, 2), roll_rows(vz, 4)))
                    for vx, vy, vz in zip(*beside)
                ],
                both=False,
            )
        )

    ended = []
    fluxes = []
    orders = ((0, 1, 2, 3, 4), (0, 2, 1, 3, 4), (0, 3, 1, 2, 4))
    for direction in range(3):
        rolled = [roll_rows(side[0], 1) for side in sides[direction]]
        ended.append([roll_rows(v, places[direction]) for v in rolled])
        lefts = [jnp.where(first_row, roll_rows(o, 1 - places[direction]), v) for o, v in zip(outer, rolled)]
        rights = [side[1] for side in sides[direction]]
        order = orders[direction]
        fluxes.append(hllc([lefts[f] for f in order], [rights[f] for f in order]))

    at_y, at_z = sub == 2, sub == 4

    def turned(values):
        normal = jnp.where(at_y, values[2], jnp.where(at_z, values[3], values[1]))
        one = jnp.where(at_y | at_z, values[1], values[2])
        two = jnp.where(at_z, values[2], values[3])
        return [values[0], normal, one, two, values[4]]

    left_end = [jnp.where(at_y, ended[1][f], jnp.where(at_z, ended[2][f], ended[0][f])) for f in range(FIELDS)]
    last = hllc(turned(left_end), turned(outer))

    total = [None] * FIELDS
    for direction in range(3):
        for place, f in enumerate(orders[direction]):
            flux = fluxes[direction][place]
            merged = jnp.where(first_row, roll_rows(last[place], -places[direction]), flux)
            change = turn(direction, flux - roll_rows(merged, -1))
            total[f] = change if total[f] is None else total[f] + change
    return total


def even_and_odd(even_refs, odd_refs):
    blocks = [primitives(*load_parts(even_refs))]
    return blocks + [load_primitives(ref) for ref in odd_refs]


def middle_of(own_refs, even_refs, odd_refs, ready_ref, pick_ref, out_ref, part_refs):
    own = load_parts(own_refs)
    change = rate(even_and_odd(even_refs, odd_refs), ready_ref, pick_ref)
    middle = [own[f] + TIME_STEP * change[f] for f in range(FIELDS)]
    store_parts(part_refs, middle)
    for f in range(FIELDS):
        out_ref[pl.ds(f * ROWS, ROWS), :] = middle[f]


def first_stage(waits_ref, ready_ref, pick_ref, own_ref, even_ref, *made):
    @pl.when(waits_ref[0, 0] == 0)
    def _():
        middle_of([own_ref], [even_ref], [], ready_ref, pick_ref, made[0], made[1:])


def first_stage_odd(waits_ref, ready_ref, pick_ref, own_ref, even_ref, odd_ref, *refs):
    made = refs[len(refs) // 2 :]

    @pl.when(waits_ref[0, 0] != 0)
    def _():
        middle_of([own_ref], [even_ref], [odd_ref], ready_ref, pick_ref, made[0], made[1:])


def advanced_of(start_refs, own_refs, even_refs, odd_refs, ready_ref, pick_ref, count_ref, out_ref, made_ref, sem):
    start, own = load_parts(start_refs), load_parts(own_refs)
    change = rate(even_and_odd(even_refs, odd_refs), ready_ref, pick_ref)
    sub, _ = positions()
    live = (sub & 1) < count_ref[0, 0]
    for f in range(FIELDS):
        value = 0.5 * start[f] + 0.5 * (own[f] + TIME_STEP * change[f])
        made_ref[pl.ds(f * ROWS, ROWS), :] = jnp.where(live, value, 0.0)
    copy = pltpu.make_async_copy(made_ref, out_ref, sem)
    copy.start()
    copy.wait()


def second_stage(waits_ref, count_ref, ready_ref, pick_ref, start_ref, *refs):
    n = len(PARTS)
    own_refs, even_refs, (out_ref, made_ref, sem) = refs[:n], refs[n : 2 * n], refs[2 * n :]

    @pl.when(waits_ref[0, 0] == 0)
    def _():
        advanced_of([start_ref], own_refs, even_refs, [], ready_ref, pick_ref, count_ref, out_ref, made_ref, sem)


def second_stage_odd(waits_ref, count_ref, ready_ref, pick_ref, start_ref, *refs):
    n = len(PARTS)
    own_refs, even_refs, (odd_ref, _, out_ref, made_ref, sem) = refs[:n], refs[n : 2 * n], refs[2 * n :]

    @pl.when(waits_ref[0, 0] != 0)
    def _():
        advanced_of([start_ref], own_refs, even_refs, [odd_ref], ready_ref, pick_ref, count_ref, out_ref, made_ref, sem)


def vmem_spec():
    return pl.BlockSpec(memory_space=pltpu.VMEM)


def smem_spec():
    return pl.BlockSpec(memory_space=pltpu.SMEM)


def hbm_spec():
    return pl.BlockSpec(memory_space=pltpu.HBM)


def body(fine_state, coarse_old, box_count, fine_links, coarse_links):
    members = lax.axis_size("sub")
    tile_rows = FIELDS * ROWS
    start = to_tiles(fine_state)
    coarse = coarse_old.transpose(0, 2, 1, 3).reshape(FIELDS, 1, -1, LANES).transpose(0, 2, 1, 3)
    coarse = coarse.reshape(-1, 1, LANES)

    odd = exchange(start, odd_partner)
    group = [in_vmem(exchange(coarse, group_shift(r))) for r in range(1, members)]

    links, corners, own_coarse, own = pl.pallas_call(
        fetch,
        out_shape=(
            pltpu.SMEM((2, 6), jnp.int32),
            pltpu.SMEM((2, 4, 6), jnp.int32),
            pltpu.VMEM((FIELDS * 4, 1, LANES), jnp.float32),
            pltpu.VMEM((tile_rows, LANES), jnp.float32),
        ),
        in_specs=[hbm_spec()] * 4,
        out_specs=(smem_spec(), smem_spec(), vmem_spec(), vmem_spec()),
        scratch_shapes=[pltpu.SemaphoreType.DMA((4,))],
        name="fetch",
    )(
        fine_links.reshape(2, 6),
        coarse_links.transpose(0, 1, 2, 4, 3).reshape(2, 4, 6),
        coarse,
        start,
    )
    even = in_vmem(exchange(own, even_partner))
    raw = pltpu.VMEM((4, ROWS, LANES), jnp.float32)
    picks, table, waits = pl.pallas_call(
        read_links,
        out_shape=(
            pltpu.VMEM((3 * ROWS, LANES), jnp.int32),
            pltpu.VMEM((16, ROWS, LANES), jnp.float32),
            pltpu.SMEM((2, 6), jnp.int32),
        ),
        in_specs=[smem_spec(), vmem_spec()],
        out_specs=(vmem_spec(), vmem_spec(), smem_spec()),
        scratch_shapes=[raw],
        name="read_links",
    )(in_smem(links), in_vmem(own_coarse))

    ghosts = pl.pallas_call(
        interpolate,
        out_shape=pltpu.VMEM((3 * tile_rows, LANES), jnp.float32),
        in_specs=[smem_spec()] + [vmem_spec()] * members,
        out_specs=vmem_spec(),
        scratch_shapes=[
            pltpu.VMEM((members * 16, ROWS, LANES), jnp.float32),
            raw,
            pltpu.VMEM((3 * tile_rows, LANES), jnp.float32),
        ],
        cost_estimate=pl.CostEstimate(flops=10**10, bytes_accessed=10**10, transcendentals=0),
        name="interpolate",
    )(in_smem(corners), in_vmem(table), *group)

    count = len(PARTS)
    tiles = (tile_rows, LANES)
    waits, picks, ghosts = in_smem(waits), in_vmem(picks), in_vmem(ghosts)
    own = in_vmem(own)

    def fold(parts):
        ready = pl.pallas_call(
            make_ready,
            out_shape=pltpu.VMEM((READY * ROWS, LANES), jnp.float32),
            in_specs=[vmem_spec()] * (2 + len(parts)),
            out_specs=vmem_spec(),
            name="fold",
        )(ghosts, picks, *parts)
        return in_vmem(ready)

    made = (pltpu.VMEM(tiles, jnp.float32),) + tuple(pltpu.VMEM((rows, LANES), jnp.float32) for _, rows in PARTS)
    ready = fold([own])
    middle = pl.pallas_call(
        first_stage,
        out_shape=made,
        in_specs=[smem_spec()] + [vmem_spec()] * 4,
        out_specs=(vmem_spec(),) * len(made),
        name="first_stage",
    )(waits, ready, picks, own, even)
    middle, *parts = pl.pallas_call(
        first_stage_odd,
        out_shape=made,
        in_specs=[smem_spec()] + [vmem_spec()] * (5 + len(made)),
        out_specs=(vmem_spec(),) * len(made),
        input_output_aliases={6 + k: k for k in range(len(made))},
        name="first_stage_odd",
    )(waits, ready, picks, own, even, in_vmem(odd), *[in_vmem(m) for m in middle])

    odd = exchange(middle, odd_partner)
    even = [in_vmem(exchange(part, even_partner)) for part in parts]
    parts = [in_vmem(part) for part in parts]
    ready = fold(parts)
    scratch = [pltpu.VMEM(tiles, jnp.float32), pltpu.SemaphoreType.DMA(())]
    result = pl.pallas_call(
        second_stage,
        out_shape=jax.ShapeDtypeStruct(tiles, jnp.float32),
        in_specs=[smem_spec()] * 2 + [vmem_spec()] * (3 + 2 * count),
        out_specs=hbm_spec(),
        scratch_shapes=scratch,
        name="second_stage",
    )(waits, box_count, ready, picks, own, *parts, *even)
    result = pl.pallas_call(
        second_stage_odd,
        out_shape=jax.ShapeDtypeStruct(tiles, jnp.float32),
        in_specs=[smem_spec()] * 2 + [vmem_spec()] * (4 + 2 * count) + [hbm_spec()],
        out_specs=hbm_spec(),
        scratch_shapes=scratch,
        input_output_aliases={6 + 2 * count: 0},
        name="second_stage_odd",
    )(waits, box_count, ready, picks, own, *parts, *even, in_vmem(odd), result)
    return from_tiles(result, fine_state.shape)


def solution(mesh):
    placed = (
        P("sfc", "sub", None, None, None),
        P("sfc", "sub", None, None),
        P("sfc", "sub"),
        P("sfc", "sub", None, None),
        P("sfc", "sub", None, None, None),
    )
    return jax.shard_map(
        body,
        mesh=mesh,
        in_specs=placed,
        out_specs=P("sfc", "sub", None, None, None),
        check_vma=False,
    )
```

```python
import jax
import jax.numpy as jnp
from jax import lax
from jax.experimental import pallas as pl
from jax.experimental.pallas import tpu as pltpu
from jax.sharding import PartitionSpec as P

FIELDS = 5
ROWS = 8
LANES = 128
GAMMA = 1.4
FLOOR = 0.1
WENO_EPS = 1e-06
TIME_STEP = 0.1
PARTS = ((0, 32), (32, 8))
HERE, EVEN, ODD = 1, 3, 5


def to_tiles(boxes):
    slots, fields = boxes.shape[2], boxes.shape[3]
    parts = boxes.reshape(slots, fields, -1, LANES)
    return parts.transpose(1, 2, 0, 3).reshape(-1, LANES)


def from_tiles(tiles, shape):
    slots, fields = shape[2], shape[3]
    parts = tiles.reshape(fields, -1, slots, LANES)
    return parts.transpose(2, 0, 1, 3).reshape(shape)


def in_vmem(value):
    return pltpu.with_memory_space_constraint(value, pltpu.VMEM)


def in_smem(value):
    return pltpu.with_memory_space_constraint(value, pltpu.SMEM)


def exchange(value, partner):
    count, members = lax.axis_size("sfc"), lax.axis_size("sub")
    pairs = []
    for segment in range(count):
        for member in range(members):
            other, other_member = partner(segment, member, count, members)
            pairs.append((segment * members + member, other * members + other_member))
    return lax.ppermute(value, ("sfc", "sub"), pairs)


def even_partner(segment, member, count, members):
    other = segment ^ 1
    return (other, member) if other < count else (segment, member)


def odd_partner(segment, member, count, members):
    other = ((segment - 1) ^ 1) + 1
    if 0 < segment and other < count:
        return (other, member)
    other_member = member ^ 1
    return (segment, other_member) if other_member < members else (segment, member)


def group_shift(steps):
    def partner(segment, member, count, members):
        return (segment, (member + steps) % members)

    return partner


def positions():
    sub = lax.broadcasted_iota(jnp.int32, (ROWS, LANES), 0)
    lane = lax.broadcasted_iota(jnp.int32, (ROWS, LANES), 1)
    return sub, lane


def gather_lanes(value, index):
    return jnp.take_along_axis(value, index, axis=1, mode="promise_in_bounds")


def gather_rows(value, index):
    return jnp.take_along_axis(value, index, axis=0, mode="promise_in_bounds")


def roll_lanes(value, steps):
    return pltpu.roll(value, steps % LANES, 1)


def roll_rows(value, steps):
    if steps % ROWS == 0:
        return value
    sub, _ = positions()
    return gather_rows(value, (sub - steps) & 7)


def reciprocal(value):
    return 1.0 / value


def primitives(mass, mom_x, mom_y, mom_z, energy):
    density = jnp.maximum(mass, FLOOR)
    inverse = reciprocal(density)
    vel_x, vel_y, vel_z = mom_x * inverse, mom_y * inverse, mom_z * inverse
    kinetic = 0.5 * density * (vel_x * vel_x + vel_y * vel_y + vel_z * vel_z)
    pressure = jnp.maximum((GAMMA - 1.0) * (energy - kinetic), FLOOR)
    return [density, vel_x, vel_y, vel_z, pressure]


def load_parts(refs):
    return [ref[pl.ds(at, ROWS), :] for ref in refs for at in range(0, ref.shape[0], ROWS)]


def store_parts(refs, fields):
    fields = list(fields)
    for ref, (_, rows) in zip(refs, PARTS):
        for at in range(0, rows, ROWS):
            ref[pl.ds(at, ROWS), :] = fields.pop(0)


def load_primitives(ref, base=0):
    return primitives(*[ref[pl.ds(base + ROWS * f, ROWS), :] for f in range(FIELDS)])


def minmod(p, q):
    return jnp.maximum(jnp.minimum(p, q), 0.0) + jnp.minimum(jnp.maximum(p, q), 0.0)


def build_table(coarse_ref, raw, table, base):
    sub, lane = positions()
    low = lane < 64
    for j in range(4):
        for f in range(FIELDS):
            raw[j, f : f + 1, :] = coarse_ref[f * 4 + j]
    cells = [raw[j] for j in range(4)]
    halves = [roll_lanes(c, 64) for c in cells]
    for j in range(4):
        u, other, after, before = cells[j], halves[j], min(j + 1, 3), max(j - 1, 0)

        def slope_of(up, value, down):
            return 0.25 * minmod(up - value, value - down)

        along_x = slope_of(jnp.where(low, other, halves[after]), u, jnp.where(low, halves[before], other))
        swapped_x = slope_of(jnp.where(low, cells[after], u), other, jnp.where(low, u, cells[before]))
        along_y, along_z = [slope_of(roll_lanes(u, -n), u, roll_lanes(u, n)) for n in (8, 1)]
        swapped_y, swapped_z = [slope_of(roll_lanes(u, 64 - n), other, roll_lanes(u, 64 + n)) for n in (8, 1)]
        for x in (2 * j, 2 * j + 1):
            if x in (0, 7):
                continue
            if x % 2 == 0:
                value, slope = jnp.where(low, u, halves[j]), jnp.where(low, along_x, swapped_x)
                sides = jnp.where(low, along_y, swapped_z)
            else:
                value, slope = jnp.where(low, halves[j], u), jnp.where(low, swapped_x, along_x)
                sides = jnp.where(low, swapped_y, along_z)
            value = jnp.where(low, value - slope, value + slope)
            table[base + x] = jnp.where(sub < FIELDS, value, gather_rows(sides, (sub + 3) & 7))
            table[base + 8 + x] = jnp.where(sub < FIELDS, sides, gather_rows(sides, (sub + 6) & 7))


def fetch(links_in, corner_in, coarse_in, start_in, links_ref, corner_ref, coarse_ref, own_ref, sems):
    copies = [(links_in, links_ref), (corner_in, corner_ref), (coarse_in, coarse_ref), (start_in, own_ref)]
    fetches = [pltpu.make_async_copy(src, dst, sems.at[i]) for i, (src, dst) in enumerate(copies)]
    for copy in fetches:
        copy.start()
    for copy in fetches:
        copy.wait()


def read_links(links_ref, coarse_ref, pick_ref, table, code_ref, raw):
    sub, lane = positions()
    y, z = (lane >> 3) & 7, lane & 7
    odd_segment = lax.axis_index("sfc") & 1
    build_table(coarse_ref, raw, table, 0)

    def choice(slot, face):
        link = links_ref[slot, face]
        offset = link >> 1
        below = jnp.where(offset == 0, 1, 0)
        block = jnp.where(offset == 1, 0, jnp.where(below == odd_segment, 1, 2))
        swapped = (link & 1) ^ slot
        return jnp.where(link < 0, 0, 1 + block * 2 + swapped)

    codes = [[choice(slot, face) for face in range(6)] for slot in range(2)]
    waits = jnp.int32(0)
    for code in codes[0] + codes[1]:
        waits = jnp.maximum(waits, jnp.where(code >= ODD, 1, 0))
    code_ref[0, 0] = waits

    first = (sub & 1) == 0
    for direction in range(3):
        lower = (sub < 4) if direction == 0 else ((y if direction == 1 else z) < 4)
        minus = jnp.where(first, codes[0][2 * direction], codes[1][2 * direction])
        plus = jnp.where(first, codes[0][2 * direction + 1], codes[1][2 * direction + 1])
        pick_ref[pl.ds(direction * ROWS, ROWS), :] = jnp.where(lower, plus, minus)


def interpolate(corner_ref, own_table, *refs):
    coarse_refs, (ghost_ref, table, raw, lines) = refs[:-4], refs[-4:]
    members = len(coarse_refs) + 1
    sub, lane = positions()
    y, z = (lane >> 3) & 7, lane & 7
    me = lax.axis_index("sub")
    table[0:16] = own_table[...]
    for m, coarse_ref in enumerate(coarse_refs):
        build_table(coarse_ref, raw, table, (m + 1) * 16)

    sign_y = jnp.where((y & 1) == 0, -1.0, 1.0)
    sign_z = jnp.where((z & 1) == 0, -1.0, 1.0)
    spread = (y >> 1) * 8 + (z >> 1)
    upper, whole = jnp.where(sub < FIELDS, lane & 64, 0), jnp.where(sub < FIELDS, 64, 0)

    def finder(slot, face):
        direction, minus = face // 2, face % 2 == 0
        start = [corner_ref[slot, 1 + a, face] + (-1 if minus and a == direction else 1) for a in range(3)]
        owner = me - corner_ref[slot, 0, face]
        owner = jnp.where(owner < 0, owner + members, owner)
        index = (spread + (start[1] * 8 + start[2])) & 63
        first, second, row = index | upper, index | whole, owner * 16 + start[0]

        def find(j):
            return gather_lanes(table[row + j], first), gather_lanes(table[row + 8 + j], second)

        return find

    for direction in range(3):
        for slot in range(2):
            minus, plus = finder(slot, 2 * direction), finder(slot, 2 * direction + 1)
            for j in range(4):
                if direction == 0:
                    value, sides = (minus if j >= 2 else plus)(j)
                else:
                    lower = (y if direction == 1 else z) < 4
                    value, sides = [jnp.where(lower, p, m) for p, m in zip(plus(j), minus(j))]
                along_y = jnp.where(sub < 3, gather_rows(value, (sub + 5) & 7), gather_rows(sides, (sub + 2) & 7))
                value = value + sign_y * along_y + sign_z * sides
                rows = pl.ds(direction * 40 + j * 2 + slot, FIELDS, stride=ROWS)
                lines[rows, :] = value[0:FIELDS, :]
        made = load_primitives(lines, direction * 40)
        for f in range(FIELDS):
            ghost_ref[pl.ds(direction * 40 + f * ROWS, ROWS), :] = made[f]


def weno(cells, both=True):
    centre = cells[2]
    e0, e1, e2, e3 = [cells[k + 1] - cells[k] for k in range(4)]
    d1, d2, d3 = e1 - e0, e2 - e1, e3 - e2
    a = ((4.0 / 3.0) * (d1 * d1) + WENO_EPS) + e1 * (e1 + d1)
    b = ((4.0 / 3.0) * (d2 * d2) + WENO_EPS) + e1 * e2
    c = ((4.0 / 3.0) * (d3 * d3) + WENO_EPS) + e2 * (e2 - d3)
    bc, ac, ab = b * c, a * c, a * b
    bc, ac, ab = bc * bc, 6.0 * (ac * ac), ab * ab
    with_ab, with_bc = 3.0 * ab + ac, 3.0 * bc + ac
    low, high = bc * d1, ab * d3
    twice = 2.0 * (high - low)
    up = with_bc * d2 + (twice + high)
    upper = (centre + 0.5 * e2) - up * ((1.0 / 6.0) * reciprocal(bc + with_ab))
    if not both:
        return upper
    down = with_ab * d2 + (low - twice)
    lower = (centre - 0.5 * e1) - down * ((1.0 / 6.0) * reciprocal(ab + with_bc))
    return upper, lower


def hllc(left, right):
    rl, ul, vl, wl, pl_ = jnp.maximum(left[0], FLOOR), left[1], left[2], left[3], jnp.maximum(left[4], FLOOR)
    rr, ur, vr, wr, pr = jnp.maximum(right[0], FLOOR), right[1], right[2], right[3], jnp.maximum(right[4], FLOOR)
    gl, gr = GAMMA * pl_, GAMMA * pr
    cl, cr = gl * lax.rsqrt(gl * rl), gr * lax.rsqrt(gr * rr)
    speed_left = jnp.minimum(ul - cl, ur - cr)
    speed_right = jnp.maximum(ul + cl, ur + cr)
    ml, mr = rl * (speed_left - ul), rr * (speed_right - ur)
    contact = (pr - pl_ + ml * ul - mr * ur) * reciprocal(ml - mr)
    from_left = (speed_left >= 0.0) | (contact >= 0.0)
    r = jnp.where(from_left, rl, rr)
    u = jnp.where(from_left, ul, ur)
    v = jnp.where(from_left, vl, vr)
    w = jnp.where(from_left, wl, wr)
    p = jnp.where(from_left, pl_, pr)
    s = jnp.where(from_left, speed_left, speed_right)
    m = jnp.where(from_left, ml, mr)
    star = (speed_left < 0.0) & ((contact >= 0.0) | (speed_right >= 0.0))
    energy = p * (1.0 / (GAMMA - 1.0)) + 0.5 * r * (u * u + v * v + w * w)
    inverse = reciprocal(s - contact)
    star_p = p + m * (contact - u)
    star_e = ((s - u) * energy - p * u + star_p * contact) * inverse
    density = jnp.where(star, m * inverse, r)
    normal = jnp.where(star, contact, u)
    pressure = jnp.where(star, star_p, p)
    energy = jnp.where(star, star_e, energy)
    mass = density * normal
    return [mass, mass * normal + pressure, mass * v, mass * w, normal * (energy + pressure)]


class Turns:
    def __init__(self):
        sub, lane = positions()
        self.sub = sub
        y, z = (lane >> 3) & 7, lane & 7
        high = lane >> 6
        self.steps = (
            (sub ^ high, lane ^ ((sub & 1) << 6), sub ^ high),
            ((sub - y) & 7, (lane & 71) | (((sub - y) & 7) << 3), (sub + y) & 7),
            ((sub - z) & 7, (lane & 120) | ((sub - z) & 7), (sub + z) & 7),
        )

    def __call__(self, direction, value):
        before, across, after = self.steps[direction]
        return gather_rows(gather_lanes(gather_rows(value, before), across), after)


def swapped_slots(value, sub):
    return gather_rows(value, sub ^ 1)


OWN, GHOST, SHIFTED, READY = 0, 15, 30, 90
SHIFTS = (-2, -1, 1, 2)


def make_ready(ghost_ref, pick_ref, *refs):
    own_refs, ready_ref = refs[:-1], refs[-1]
    turn = Turns()
    own = primitives(*load_parts(own_refs))
    candidates = [own, [swapped_slots(v, turn.sub) for v in own]]
    for direction in range(3):
        pick = pick_ref[pl.ds(direction * ROWS, ROWS), :]
        wanted = [pick == c + 1 for c in range(len(candidates))]
        remote = pick > len(candidates)
        for f in range(FIELDS):
            value = ghost_ref[pl.ds((direction * FIELDS + f) * ROWS, ROWS), :]
            for c, candidate in enumerate(candidates):
                value = jnp.where(wanted[c], candidate[f], value)
            value = jnp.where(remote, 0.0, value)
            tile = direction * FIELDS + f
            ready_ref[pl.ds((GHOST + tile) * ROWS, ROWS), :] = turn(direction, value)
            cells = turn(direction, own[f])
            ready_ref[pl.ds((OWN + tile) * ROWS, ROWS), :] = cells
            for k, s in enumerate(SHIFTS):
                ready_ref[pl.ds((SHIFTED + tile * len(SHIFTS) + k) * ROWS, ROWS), :] = roll_rows(cells, -s)


def rate(blocks, ready_ref, pick_ref):
    turn = Turns()
    sub = turn.sub
    first_row = sub == 0
    candidates = []
    for block in blocks:
        candidates += [block, [swapped_slots(v, sub) for v in block]]

    def line(direction, f):
        pick = pick_ref[pl.ds(direction * ROWS, ROWS), :]
        tile = direction * FIELDS + f
        remote = jnp.zeros((ROWS, LANES), jnp.float32)
        for c, candidate in enumerate(candidates):
            remote = jnp.where(pick == EVEN + c, candidate[f], remote)
        ghost = ready_ref[pl.ds((GHOST + tile) * ROWS, ROWS), :] + turn(direction, remote)
        return ready_ref[pl.ds((OWN + tile) * ROWS, ROWS), :], ghost

    is_x, is_y = (sub == 7) | first_row, (sub == 1) | (sub == 2)
    places = (0, 2, 4)
    sides = [[], [], []]
    outer = []
    for f in range(FIELDS):
        beside = []
        for direction in range(3):
            own, ghost = line(direction, f)
            cells, around = [], []
            rolled_own, rolled_ghost = {}, {}
            for s in range(-2, 3):
                if s == 0:
                    cells.append(own)
                    continue
                shifted = SHIFTED + (direction * FIELDS + f) * len(SHIFTS) + SHIFTS.index(s)
                own_s, ghost_s = ready_ref[pl.ds(shifted * ROWS, ROWS), :], roll_rows(ghost, -s)
                outside = (sub < -s) if s < 0 else (sub > 7 - s)
                cells.append(jnp.where(outside, ghost_s, own_s))
                rolled_own[s], rolled_ghost[s] = own_s, ghost_s
            for s in range(-2, 3):
                if s == 0:
                    around.append(ghost)
                elif s < 0:
                    around.append(jnp.where(first_row, rolled_ghost[-s], rolled_ghost[s]))
                else:
                    around.append(jnp.where(first_row, rolled_own[-s], rolled_own[s]))
            sides[direction].append(weno(cells))
            beside.append(around)
        outer.append(
            weno(
                [
                    jnp.where(is_x, vx, jnp.where(is_y, roll_rows(vy, 2), roll_rows(vz, 4)))
                    for vx, vy, vz in zip(*beside)
                ],
                both=False,
            )
        )

    ended = []
    fluxes = []
    orders = ((0, 1, 2, 3, 4), (0, 2, 1, 3, 4), (0, 3, 1, 2, 4))
    for direction in range(3):
        rolled = [roll_rows(side[0], 1) for side in sides[direction]]
        ended.append([roll_rows(v, places[direction]) for v in rolled])
        lefts = [jnp.where(first_row, roll_rows(o, 1 - places[direction]), v) for o, v in zip(outer, rolled)]
        rights = [side[1] for side in sides[direction]]
        order = orders[direction]
        fluxes.append(hllc([lefts[f] for f in order], [rights[f] for f in order]))

    at_y, at_z = sub == 2, sub == 4

    def turned(values):
        normal = jnp.where(at_y, values[2], jnp.where(at_z, values[3], values[1]))
        one = jnp.where(at_y | at_z, values[1], values[2])
        two = jnp.where(at_z, values[2], values[3])
        return [values[0], normal, one, two, values[4]]

    left_end = [jnp.where(at_y, ended[1][f], jnp.where(at_z, ended[2][f], ended[0][f])) for f in range(FIELDS)]
    last = hllc(turned(left_end), turned(outer))

    total = [None] * FIELDS
    for direction in range(3):
        for place, f in enumerate(orders[direction]):
            flux = fluxes[direction][place]
            merged = jnp.where(first_row, roll_rows(last[place], -places[direction]), flux)
            change = turn(direction, flux - roll_rows(merged, -1))
            total[f] = change if total[f] is None else total[f] + change
    return total


def even_and_odd(even_refs, odd_refs):
    blocks = [primitives(*load_parts(even_refs))]
    return blocks + [load_primitives(ref) for ref in odd_refs]


def middle_of(own_refs, even_refs, odd_refs, ready_ref, pick_ref, out_ref, part_refs):
    own = load_parts(own_refs)
    change = rate(even_and_odd(even_refs, odd_refs), ready_ref, pick_ref)
    middle = [own[f] + TIME_STEP * change[f] for f in range(FIELDS)]
    store_parts(part_refs, middle)
    for f in range(FIELDS):
        out_ref[pl.ds(f * ROWS, ROWS), :] = middle[f]


def first_stage(waits_ref, ready_ref, pick_ref, own_ref, even_ref, *made):
    @pl.when(waits_ref[0, 0] == 0)
    def _():
        middle_of([own_ref], [even_ref], [], ready_ref, pick_ref, made[0], made[1:])


def first_stage_odd(waits_ref, ready_ref, pick_ref, own_ref, even_ref, odd_ref, *refs):
    made = refs[len(refs) // 2 :]

    @pl.when(waits_ref[0, 0] != 0)
    def _():
        middle_of([own_ref], [even_ref], [odd_ref], ready_ref, pick_ref, made[0], made[1:])


def advanced_of(start_refs, own_refs, even_refs, odd_refs, ready_ref, pick_ref, count_ref, out_ref, made_ref, sem):
    start, own = load_parts(start_refs), load_parts(own_refs)
    change = rate(even_and_odd(even_refs, odd_refs), ready_ref, pick_ref)
    sub, _ = positions()
    live = (sub & 1) < count_ref[0, 0]
    for f in range(FIELDS):
        value = 0.5 * start[f] + 0.5 * (own[f] + TIME_STEP * change[f])
        made_ref[pl.ds(f * ROWS, ROWS), :] = jnp.where(live, value, 0.0)
    copy = pltpu.make_async_copy(made_ref, out_ref, sem)
    copy.start()
    copy.wait()


def second_stage(waits_ref, count_ref, ready_ref, pick_ref, start_ref, *refs):
    n = len(PARTS)
    own_refs, even_refs, (out_ref, made_ref, sem) = refs[:n], refs[n : 2 * n], refs[2 * n :]

    @pl.when(waits_ref[0, 0] == 0)
    def _():
        advanced_of([start_ref], own_refs, even_refs, [], ready_ref, pick_ref, count_ref, out_ref, made_ref, sem)


def second_stage_odd(waits_ref, count_ref, ready_ref, pick_ref, start_ref, *refs):
    n = len(PARTS)
    own_refs, even_refs, (odd_ref, _, out_ref, made_ref, sem) = refs[:n], refs[n : 2 * n], refs[2 * n :]

    @pl.when(waits_ref[0, 0] != 0)
    def _():
        advanced_of([start_ref], own_refs, even_refs, [odd_ref], ready_ref, pick_ref, count_ref, out_ref, made_ref, sem)


def vmem_spec():
    return pl.BlockSpec(memory_space=pltpu.VMEM)


def smem_spec():
    return pl.BlockSpec(memory_space=pltpu.SMEM)


def hbm_spec():
    return pl.BlockSpec(memory_space=pltpu.HBM)


def body(fine_state, coarse_old, box_count, fine_links, coarse_links):
    members = lax.axis_size("sub")
    tile_rows = FIELDS * ROWS
    start = to_tiles(fine_state)
    coarse = coarse_old.transpose(0, 2, 1, 3).reshape(FIELDS, 1, -1, LANES).transpose(0, 2, 1, 3)
    coarse = coarse.reshape(-1, 1, LANES)

    odd = exchange(start, odd_partner)
    group = [in_vmem(exchange(coarse, group_shift(r))) for r in range(1, members)]

    links, corners, own_coarse, own = pl.pallas_call(
        fetch,
        out_shape=(
            pltpu.SMEM((2, 6), jnp.int32),
            pltpu.SMEM((2, 4, 6), jnp.int32),
            pltpu.VMEM((FIELDS * 4, 1, LANES), jnp.float32),
            pltpu.VMEM((tile_rows, LANES), jnp.float32),
        ),
        in_specs=[hbm_spec()] * 4,
        out_specs=(smem_spec(), smem_spec(), vmem_spec(), vmem_spec()),
        scratch_shapes=[pltpu.SemaphoreType.DMA((4,))],
        name="fetch",
    )(
        fine_links.reshape(2, 6),
        coarse_links.transpose(0, 1, 2, 4, 3).reshape(2, 4, 6),
        coarse,
        start,
    )
    even = in_vmem(exchange(own, even_partner))
    raw = pltpu.VMEM((4, ROWS, LANES), jnp.float32)
    picks, table, waits = pl.pallas_call(
        read_links,
        out_shape=(
            pltpu.VMEM((3 * ROWS, LANES), jnp.int32),
            pltpu.VMEM((16, ROWS, LANES), jnp.float32),
            pltpu.SMEM((2, 6), jnp.int32),
        ),
        in_specs=[smem_spec(), vmem_spec()],
        out_specs=(vmem_spec(), vmem_spec(), smem_spec()),
        scratch_shapes=[raw],
        name="read_links",
    )(in_smem(links), in_vmem(own_coarse))

    ghosts = pl.pallas_call(
        interpolate,
        out_shape=pltpu.VMEM((3 * tile_rows, LANES), jnp.float32),
        in_specs=[smem_spec()] + [vmem_spec()] * members,
        out_specs=vmem_spec(),
        scratch_shapes=[
            pltpu.VMEM((members * 16, ROWS, LANES), jnp.float32),
            raw,
            pltpu.VMEM((3 * tile_rows, LANES), jnp.float32),
        ],
        cost_estimate=pl.CostEstimate(flops=10**10, bytes_accessed=10**10, transcendentals=0),
        name="interpolate",
    )(in_smem(corners), in_vmem(table), *group)

    count = len(PARTS)
    tiles = (tile_rows, LANES)
    waits, picks, ghosts = in_smem(waits), in_vmem(picks), in_vmem(ghosts)
    own = in_vmem(own)

    def fold(parts):
        ready = pl.pallas_call(
            make_ready,
            out_shape=pltpu.VMEM((READY * ROWS, LANES), jnp.float32),
            in_specs=[vmem_spec()] * (2 + len(parts)),
            out_specs=vmem_spec(),
            name="fold",
        )(ghosts, picks, *parts)
        return in_vmem(ready)

    made = (pltpu.VMEM(tiles, jnp.float32),) + tuple(pltpu.VMEM((rows, LANES), jnp.float32) for _, rows in PARTS)
    ready = fold([own])
    middle = pl.pallas_call(
        first_stage,
        out_shape=made,
        in_specs=[smem_spec()] + [vmem_spec()] * 4,
        out_specs=(vmem_spec(),) * len(made),
        name="first_stage",
    )(waits, ready, picks, own, even)
    middle, *parts = pl.pallas_call(
        first_stage_odd,
        out_shape=made,
        in_specs=[smem_spec()] + [vmem_spec()] * (5 + len(made)),
        out_specs=(vmem_spec(),) * len(made),
        input_output_aliases={6 + k: k for k in range(len(made))},
        name="first_stage_odd",
    )(waits, ready, picks, own, even, in_vmem(odd), *[in_vmem(m) for m in middle])

    odd = exchange(middle, odd_partner)
    even = [in_vmem(exchange(part, even_partner)) for part in parts]
    parts = [in_vmem(part) for part in parts]
    ready = fold(parts)
    scratch = [pltpu.VMEM(tiles, jnp.float32), pltpu.SemaphoreType.DMA(())]
    result = pl.pallas_call(
        second_stage,
        out_shape=jax.ShapeDtypeStruct(tiles, jnp.float32),
        in_specs=[smem_spec()] * 2 + [vmem_spec()] * (3 + 2 * count),
        out_specs=hbm_spec(),
        scratch_shapes=scratch,
        name="second_stage",
    )(waits, box_count, ready, picks, own, *parts, *even)
    result = pl.pallas_call(
        second_stage_odd,
        out_shape=jax.ShapeDtypeStruct(tiles, jnp.float32),
        in_specs=[smem_spec()] * 2 + [vmem_spec()] * (4 + 2 * count) + [hbm_spec()],
        out_specs=hbm_spec(),
        scratch_shapes=scratch,
        input_output_aliases={6 + 2 * count: 0},
        name="second_stage_odd",
    )(waits, box_count, ready, picks, own, *parts, *even, in_vmem(odd), result)
    return from_tiles(result, fine_state.shape)


def solution(mesh):
    placed = (
        P("sfc", "sub", None, None, None),
        P("sfc", "sub", None, None),
        P("sfc", "sub"),
        P("sfc", "sub", None, None),
        P("sfc", "sub", None, None, None),
    )
    return jax.shard_map(
        body,
        mesh=mesh,
        in_specs=placed,
        out_specs=P("sfc", "sub", None, None, None),
        check_vma=False,
    )
```

```python
import jax
import jax.numpy as jnp
from jax import lax
from jax.experimental import pallas as pl
from jax.experimental.pallas import tpu as pltpu
from jax.sharding import PartitionSpec as P

FIELDS = 5
ROWS = 8
LANES = 128
GAMMA = 1.4
FLOOR = 0.1
WENO_EPS = 1e-06
TIME_STEP = 0.1
PARTS = ((0, 32), (32, 8))
HERE, EVEN, ODD = 1, 3, 5


def to_tiles(boxes):
    slots, fields = boxes.shape[2], boxes.shape[3]
    parts = boxes.reshape(slots, fields, -1, LANES)
    return parts.transpose(1, 2, 0, 3).reshape(-1, LANES)


def from_tiles(tiles, shape):
    slots, fields = shape[2], shape[3]
    parts = tiles.reshape(fields, -1, slots, LANES)
    return parts.transpose(2, 0, 1, 3).reshape(shape)


def in_vmem(value):
    return pltpu.with_memory_space_constraint(value, pltpu.VMEM)


def in_smem(value):
    return pltpu.with_memory_space_constraint(value, pltpu.SMEM)


def exchange(value, partner):
    count, members = lax.axis_size("sfc"), lax.axis_size("sub")
    pairs = []
    for segment in range(count):
        for member in range(members):
            other, other_member = partner(segment, member, count, members)
            pairs.append((segment * members + member, other * members + other_member))
    return lax.ppermute(value, ("sfc", "sub"), pairs)


def even_partner(segment, member, count, members):
    other = segment ^ 1
    return (other, member) if other < count else (segment, member)


def odd_partner(segment, member, count, members):
    other = ((segment - 1) ^ 1) + 1
    if 0 < segment and other < count:
        return (other, member)
    other_member = member ^ 1
    return (segment, other_member) if other_member < members else (segment, member)


def group_shift(steps):
    def partner(segment, member, count, members):
        return (segment, (member + steps) % members)

    return partner


def positions():
    sub = lax.broadcasted_iota(jnp.int32, (ROWS, LANES), 0)
    lane = lax.broadcasted_iota(jnp.int32, (ROWS, LANES), 1)
    return sub, lane


def gather_lanes(value, index):
    return jnp.take_along_axis(value, index, axis=1, mode="promise_in_bounds")


def gather_rows(value, index):
    return jnp.take_along_axis(value, index, axis=0, mode="promise_in_bounds")


def roll_lanes(value, steps):
    return pltpu.roll(value, steps % LANES, 1)


def roll_rows(value, steps):
    return pltpu.roll(value, steps % ROWS, 0) if steps % ROWS else value


def reciprocal(value):
    return 1.0 / value


def primitives(mass, mom_x, mom_y, mom_z, energy):
    density = jnp.maximum(mass, FLOOR)
    inverse = reciprocal(density)
    vel_x, vel_y, vel_z = mom_x * inverse, mom_y * inverse, mom_z * inverse
    kinetic = 0.5 * density * (vel_x * vel_x + vel_y * vel_y + vel_z * vel_z)
    pressure = jnp.maximum((GAMMA - 1.0) * (energy - kinetic), FLOOR)
    return [density, vel_x, vel_y, vel_z, pressure]


def load_parts(refs):
    return [ref[pl.ds(at, ROWS), :] for ref in refs for at in range(0, ref.shape[0], ROWS)]


def store_parts(refs, fields):
    fields = list(fields)
    for ref, (_, rows) in zip(refs, PARTS):
        for at in range(0, rows, ROWS):
            ref[pl.ds(at, ROWS), :] = fields.pop(0)


def load_primitives(ref, base=0):
    return primitives(*[ref[pl.ds(base + ROWS * f, ROWS), :] for f in range(FIELDS)])


def minmod(p, q):
    return jnp.maximum(jnp.minimum(p, q), 0.0) + jnp.minimum(jnp.maximum(p, q), 0.0)


def build_table(coarse_ref, raw, table, base):
    sub, lane = positions()
    low = lane < 64
    for j in range(4):
        for f in range(FIELDS):
            raw[j, f : f + 1, :] = coarse_ref[f * 4 + j]
    cells = [raw[j] for j in range(4)]
    halves = [roll_lanes(c, 64) for c in cells]
    for j in range(4):
        u, other, after, before = cells[j], halves[j], min(j + 1, 3), max(j - 1, 0)

        def slope_of(up, value, down):
            return 0.25 * minmod(up - value, value - down)

        along_x = slope_of(jnp.where(low, other, halves[after]), u, jnp.where(low, halves[before], other))
        swapped_x = slope_of(jnp.where(low, cells[after], u), other, jnp.where(low, u, cells[before]))
        along_y, along_z = [slope_of(roll_lanes(u, -n), u, roll_lanes(u, n)) for n in (8, 1)]
        swapped_y, swapped_z = [slope_of(roll_lanes(u, 64 - n), other, roll_lanes(u, 64 + n)) for n in (8, 1)]
        for x in (2 * j, 2 * j + 1):
            if x in (0, 7):
                continue
            if x % 2 == 0:
                value, slope = jnp.where(low, u, halves[j]), jnp.where(low, along_x, swapped_x)
                sides = jnp.where(low, along_y, swapped_z)
            else:
                value, slope = jnp.where(low, halves[j], u), jnp.where(low, swapped_x, along_x)
                sides = jnp.where(low, swapped_y, along_z)
            value = jnp.where(low, value - slope, value + slope)
            table[base + x] = jnp.where(sub < FIELDS, value, gather_rows(sides, (sub + 3) & 7))
            table[base + 8 + x] = jnp.where(sub < FIELDS, sides, gather_rows(sides, (sub + 6) & 7))


def fetch(links_in, corner_in, coarse_in, start_in, links_ref, corner_ref, coarse_ref, own_ref, sems):
    copies = [(links_in, links_ref), (corner_in, corner_ref), (coarse_in, coarse_ref), (start_in, own_ref)]
    fetches = [pltpu.make_async_copy(src, dst, sems.at[i]) for i, (src, dst) in enumerate(copies)]
    for copy in fetches:
        copy.start()
    for copy in fetches:
        copy.wait()


def read_links(links_ref, coarse_ref, pick_ref, table, code_ref, raw):
    sub, lane = positions()
    y, z = (lane >> 3) & 7, lane & 7
    odd_segment = lax.axis_index("sfc") & 1
    build_table(coarse_ref, raw, table, 0)

    def choice(slot, face):
        link = links_ref[slot, face]
        offset = link >> 1
        below = jnp.where(offset == 0, 1, 0)
        block = jnp.where(offset == 1, 0, jnp.where(below == odd_segment, 1, 2))
        swapped = (link & 1) ^ slot
        return jnp.where(link < 0, 0, 1 + block * 2 + swapped)

    codes = [[choice(slot, face) for face in range(6)] for slot in range(2)]
    waits = jnp.int32(0)
    for code in codes[0] + codes[1]:
        waits = jnp.maximum(waits, jnp.where(code >= ODD, 1, 0))
    code_ref[0, 0] = waits

    first = (sub & 1) == 0
    for direction in range(3):
        lower = (sub < 4) if direction == 0 else ((y if direction == 1 else z) < 4)
        minus = jnp.where(first, codes[0][2 * direction], codes[1][2 * direction])
        plus = jnp.where(first, codes[0][2 * direction + 1], codes[1][2 * direction + 1])
        pick_ref[pl.ds(direction * ROWS, ROWS), :] = jnp.where(lower, plus, minus)


def interpolate(corner_ref, own_table, *refs):
    coarse_refs, (ghost_ref, table, raw, lines) = refs[:-4], refs[-4:]
    members = len(coarse_refs) + 1
    sub, lane = positions()
    y, z = (lane >> 3) & 7, lane & 7
    me = lax.axis_index("sub")
    table[0:16] = own_table[...]
    for m, coarse_ref in enumerate(coarse_refs):
        build_table(coarse_ref, raw, table, (m + 1) * 16)

    sign_y = jnp.where((y & 1) == 0, -1.0, 1.0)
    sign_z = jnp.where((z & 1) == 0, -1.0, 1.0)
    spread = (y >> 1) * 8 + (z >> 1)
    upper, whole = jnp.where(sub < FIELDS, lane & 64, 0), jnp.where(sub < FIELDS, 64, 0)

    def finder(slot, face):
        direction, minus = face // 2, face % 2 == 0
        start = [corner_ref[slot, 1 + a, face] + (-1 if minus and a == direction else 1) for a in range(3)]
        owner = me - corner_ref[slot, 0, face]
        owner = jnp.where(owner < 0, owner + members, owner)
        index = (spread + (start[1] * 8 + start[2])) & 63
        first, second, row = index | upper, index | whole, owner * 16 + start[0]

        def find(j):
            return gather_lanes(table[row + j], first), gather_lanes(table[row + 8 + j], second)

        return find

    for direction in range(3):
        for slot in range(2):
            minus, plus = finder(slot, 2 * direction), finder(slot, 2 * direction + 1)
            for j in range(4):
                if direction == 0:
                    value, sides = (minus if j >= 2 else plus)(j)
                else:
                    lower = (y if direction == 1 else z) < 4
                    value, sides = [jnp.where(lower, p, m) for p, m in zip(plus(j), minus(j))]
                along_y = jnp.where(sub < 3, gather_rows(value, (sub + 5) & 7), gather_rows(sides, (sub + 2) & 7))
                value = value + sign_y * along_y + sign_z * sides
                rows = pl.ds(direction * 40 + j * 2 + slot, FIELDS, stride=ROWS)
                lines[rows, :] = value[0:FIELDS, :]
        made = load_primitives(lines, direction * 40)
        for f in range(FIELDS):
            ghost_ref[pl.ds(direction * 40 + f * ROWS, ROWS), :] = made[f]


def weno(cells, both=True):
    centre = cells[2]
    e0, e1, e2, e3 = [cells[k + 1] - cells[k] for k in range(4)]
    d1, d2, d3 = e1 - e0, e2 - e1, e3 - e2
    a = ((4.0 / 3.0) * (d1 * d1) + WENO_EPS) + e1 * (e1 + d1)
    b = ((4.0 / 3.0) * (d2 * d2) + WENO_EPS) + e1 * e2
    c = ((4.0 / 3.0) * (d3 * d3) + WENO_EPS) + e2 * (e2 - d3)
    bc, ac, ab = b * c, a * c, a * b
    bc, ac, ab = bc * bc, 6.0 * (ac * ac), ab * ab
    with_ab, with_bc = 3.0 * ab + ac, 3.0 * bc + ac
    low, high = bc * d1, ab * d3
    twice = 2.0 * (high - low)
    up = with_bc * d2 + (twice + high)
    upper = (centre + 0.5 * e2) - up * ((1.0 / 6.0) * reciprocal(bc + with_ab))
    if not both:
        return upper
    down = with_ab * d2 + (low - twice)
    lower = (centre - 0.5 * e1) - down * ((1.0 / 6.0) * reciprocal(ab + with_bc))
    return upper, lower


def hllc(left, right):
    rl, ul, vl, wl, pl_ = jnp.maximum(left[0], FLOOR), left[1], left[2], left[3], jnp.maximum(left[4], FLOOR)
    rr, ur, vr, wr, pr = jnp.maximum(right[0], FLOOR), right[1], right[2], right[3], jnp.maximum(right[4], FLOOR)
    gl, gr = GAMMA * pl_, GAMMA * pr
    cl, cr = gl * lax.rsqrt(gl * rl), gr * lax.rsqrt(gr * rr)
    speed_left = jnp.minimum(ul - cl, ur - cr)
    speed_right = jnp.maximum(ul + cl, ur + cr)
    ml, mr = rl * (speed_left - ul), rr * (speed_right - ur)
    contact = (pr - pl_ + ml * ul - mr * ur) * reciprocal(ml - mr)
    from_left = (speed_left >= 0.0) | (contact >= 0.0)
    r = jnp.where(from_left, rl, rr)
    u = jnp.where(from_left, ul, ur)
    v = jnp.where(from_left, vl, vr)
    w = jnp.where(from_left, wl, wr)
    p = jnp.where(from_left, pl_, pr)
    s = jnp.where(from_left, speed_left, speed_right)
    m = jnp.where(from_left, ml, mr)
    star = (speed_left < 0.0) & ((contact >= 0.0) | (speed_right >= 0.0))
    energy = p * (1.0 / (GAMMA - 1.0)) + 0.5 * r * (u * u + v * v + w * w)
    inverse = reciprocal(s - contact)
    star_p = p + m * (contact - u)
    star_e = ((s - u) * energy - p * u + star_p * contact) * inverse
    density = jnp.where(star, m * inverse, r)
    normal = jnp.where(star, contact, u)
    pressure = jnp.where(star, star_p, p)
    energy = jnp.where(star, star_e, energy)
    mass = density * normal
    return [mass, mass * normal + pressure, mass * v, mass * w, normal * (energy + pressure)]


class Turns:
    def __init__(self):
        sub, lane = positions()
        self.sub = sub
        y, z = (lane >> 3) & 7, lane & 7
        high = lane >> 6
        self.steps = (
            (sub ^ high, lane ^ ((sub & 1) << 6), sub ^ high),
            ((sub - y) & 7, (lane & 71) | (((sub - y) & 7) << 3), (sub + y) & 7),
            ((sub - z) & 7, (lane & 120) | ((sub - z) & 7), (sub + z) & 7),
        )

    def __call__(self, direction, value):
        before, across, after = self.steps[direction]
        return gather_rows(gather_lanes(gather_rows(value, before), across), after)


def swapped_slots(value, sub):
    return gather_rows(value, sub ^ 1)


OWN, GHOST, SHIFTED, READY = 0, 15, 30, 90
SHIFTS = (-2, -1, 1, 2)


def make_ready(ghost_ref, pick_ref, *refs):
    own_refs, ready_ref = refs[:-1], refs[-1]
    turn = Turns()
    own = primitives(*load_parts(own_refs))
    candidates = [own, [swapped_slots(v, turn.sub) for v in own]]
    for direction in range(3):
        pick = pick_ref[pl.ds(direction * ROWS, ROWS), :]
        wanted = [pick == c + 1 for c in range(len(candidates))]
        remote = pick > len(candidates)
        for f in range(FIELDS):
            value = ghost_ref[pl.ds((direction * FIELDS + f) * ROWS, ROWS), :]
            for c, candidate in enumerate(candidates):
                value = jnp.where(wanted[c], candidate[f], value)
            value = jnp.where(remote, 0.0, value)
            tile = direction * FIELDS + f
            ready_ref[pl.ds((GHOST + tile) * ROWS, ROWS), :] = turn(direction, value)
            cells = turn(direction, own[f])
            ready_ref[pl.ds((OWN + tile) * ROWS, ROWS), :] = cells
            for k, s in enumerate(SHIFTS):
                ready_ref[pl.ds((SHIFTED + tile * len(SHIFTS) + k) * ROWS, ROWS), :] = roll_rows(cells, -s)


def rate(blocks, ready_ref, pick_ref):
    turn = Turns()
    sub = turn.sub
    first_row = sub == 0
    candidates = []
    for block in blocks:
        candidates += [block, [swapped_slots(v, sub) for v in block]]

    def line(direction, f):
        pick = pick_ref[pl.ds(direction * ROWS, ROWS), :]
        tile = direction * FIELDS + f
        remote = jnp.zeros((ROWS, LANES), jnp.float32)
        for c, candidate in enumerate(candidates):
            remote = jnp.where(pick == EVEN + c, candidate[f], remote)
        ghost = ready_ref[pl.ds((GHOST + tile) * ROWS, ROWS), :] + turn(direction, remote)
        return ready_ref[pl.ds((OWN + tile) * ROWS, ROWS), :], ghost

    is_x, is_y = (sub == 7) | first_row, (sub == 1) | (sub == 2)
    places = (0, 2, 4)
    sides = [[], [], []]
    outer = []
    for f in range(FIELDS):
        beside = []
        for direction in range(3):
            own, ghost = line(direction, f)
            cells, around = [], []
            rolled_own, rolled_ghost = {}, {}
            for s in range(-2, 3):
                if s == 0:
                    cells.append(own)
                    continue
                shifted = SHIFTED + (direction * FIELDS + f) * len(SHIFTS) + SHIFTS.index(s)
                own_s, ghost_s = ready_ref[pl.ds(shifted * ROWS, ROWS), :], roll_rows(ghost, -s)
                outside = (sub < -s) if s < 0 else (sub > 7 - s)
                cells.append(jnp.where(outside, ghost_s, own_s))
                rolled_own[s], rolled_ghost[s] = own_s, ghost_s
            for s in range(-2, 3):
                if s == 0:
                    around.append(ghost)
                elif s < 0:
                    around.append(jnp.where(first_row, rolled_ghost[-s], rolled_ghost[s]))
                else:
                    around.append(jnp.where(first_row, rolled_own[-s], rolled_own[s]))
            sides[direction].append(weno(cells))
            beside.append(around)
        outer.append(
            weno(
                [
                    jnp.where(is_x, vx, jnp.where(is_y, roll_rows(vy, 2), roll_rows(vz, 4)))
                    for vx, vy, vz in zip(*beside)
                ],
                both=False,
            )
        )

    ended = []
    fluxes = []
    orders = ((0, 1, 2, 3, 4), (0, 2, 1, 3, 4), (0, 3, 1, 2, 4))
    for direction in range(3):
        rolled = [roll_rows(side[0], 1) for side in sides[direction]]
        ended.append([roll_rows(v, places[direction]) for v in rolled])
        lefts = [jnp.where(first_row, roll_rows(o, 1 - places[direction]), v) for o, v in zip(outer, rolled)]
        rights = [side[1] for side in sides[direction]]
        order = orders[direction]
        fluxes.append(hllc([lefts[f] for f in order], [rights[f] for f in order]))

    at_y, at_z = sub == 2, sub == 4

    def turned(values):
        normal = jnp.where(at_y, values[2], jnp.where(at_z, values[3], values[1]))
        one = jnp.where(at_y | at_z, values[1], values[2])
        two = jnp.where(at_z, values[2], values[3])
        return [values[0], normal, one, two, values[4]]

    left_end = [jnp.where(at_y, ended[1][f], jnp.where(at_z, ended[2][f], ended[0][f])) for f in range(FIELDS)]
    last = hllc(turned(left_end), turned(outer))

    total = [None] * FIELDS
    for direction in range(3):
        for place, f in enumerate(orders[direction]):
            flux = fluxes[direction][place]
            merged = jnp.where(first_row, roll_rows(last[place], -places[direction]), flux)
            change = turn(direction, flux - roll_rows(merged, -1))
            total[f] = change if total[f] is None else total[f] + change
    return total


def even_and_odd(even_refs, odd_refs):
    blocks = [primitives(*load_parts(even_refs))]
    return blocks + [load_primitives(ref) for ref in odd_refs]


def middle_of(own_refs, even_refs, odd_refs, ready_ref, pick_ref, out_ref, part_refs):
    own = load_parts(own_refs)
    change = rate(even_and_odd(even_refs, odd_refs), ready_ref, pick_ref)
    middle = [own[f] + TIME_STEP * change[f] for f in range(FIELDS)]
    store_parts(part_refs, middle)
    for f in range(FIELDS):
        out_ref[pl.ds(f * ROWS, ROWS), :] = middle[f]


def first_stage(waits_ref, ready_ref, pick_ref, own_ref, even_ref, *made):
    @pl.when(waits_ref[0, 0] == 0)
    def _():
        middle_of([own_ref], [even_ref], [], ready_ref, pick_ref, made[0], made[1:])


def first_stage_odd(waits_ref, ready_ref, pick_ref, own_ref, even_ref, odd_ref, *refs):
    made = refs[len(refs) // 2 :]

    @pl.when(waits_ref[0, 0] != 0)
    def _():
        middle_of([own_ref], [even_ref], [odd_ref], ready_ref, pick_ref, made[0], made[1:])


def advanced_of(start_refs, own_refs, even_refs, odd_refs, ready_ref, pick_ref, count_ref, out_ref, made_ref, sem):
    start, own = load_parts(start_refs), load_parts(own_refs)
    change = rate(even_and_odd(even_refs, odd_refs), ready_ref, pick_ref)
    sub, _ = positions()
    live = (sub & 1) < count_ref[0, 0]
    for f in range(FIELDS):
        value = 0.5 * start[f] + 0.5 * (own[f] + TIME_STEP * change[f])
        made_ref[pl.ds(f * ROWS, ROWS), :] = jnp.where(live, value, 0.0)
    copy = pltpu.make_async_copy(made_ref, out_ref, sem)
    copy.start()
    copy.wait()


def second_stage(waits_ref, count_ref, ready_ref, pick_ref, start_ref, *refs):
    n = len(PARTS)
    own_refs, even_refs, (out_ref, made_ref, sem) = refs[:n], refs[n : 2 * n], refs[2 * n :]

    @pl.when(waits_ref[0, 0] == 0)
    def _():
        advanced_of([start_ref], own_refs, even_refs, [], ready_ref, pick_ref, count_ref, out_ref, made_ref, sem)


def second_stage_odd(waits_ref, count_ref, ready_ref, pick_ref, start_ref, *refs):
    n = len(PARTS)
    own_refs, even_refs, (odd_ref, _, out_ref, made_ref, sem) = refs[:n], refs[n : 2 * n], refs[2 * n :]

    @pl.when(waits_ref[0, 0] != 0)
    def _():
        advanced_of([start_ref], own_refs, even_refs, [odd_ref], ready_ref, pick_ref, count_ref, out_ref, made_ref, sem)


def vmem_spec():
    return pl.BlockSpec(memory_space=pltpu.VMEM)


def smem_spec():
    return pl.BlockSpec(memory_space=pltpu.SMEM)


def hbm_spec():
    return pl.BlockSpec(memory_space=pltpu.HBM)


def body(fine_state, coarse_old, box_count, fine_links, coarse_links):
    members = lax.axis_size("sub")
    tile_rows = FIELDS * ROWS
    start = to_tiles(fine_state)
    coarse = coarse_old.transpose(0, 2, 1, 3).reshape(FIELDS, 1, -1, LANES).transpose(0, 2, 1, 3)
    coarse = coarse.reshape(-1, 1, LANES)

    odd = exchange(start, odd_partner)
    group = [in_vmem(exchange(coarse, group_shift(r))) for r in range(1, members)]

    links, corners, own_coarse, own = pl.pallas_call(
        fetch,
        out_shape=(
            pltpu.SMEM((2, 6), jnp.int32),
            pltpu.SMEM((2, 4, 6), jnp.int32),
            pltpu.VMEM((FIELDS * 4, 1, LANES), jnp.float32),
            pltpu.VMEM((tile_rows, LANES), jnp.float32),
        ),
        in_specs=[hbm_spec()] * 4,
        out_specs=(smem_spec(), smem_spec(), vmem_spec(), vmem_spec()),
        scratch_shapes=[pltpu.SemaphoreType.DMA((4,))],
        name="fetch",
    )(
        fine_links.reshape(2, 6),
        coarse_links.transpose(0, 1, 2, 4, 3).reshape(2, 4, 6),
        coarse,
        start,
    )
    even = in_vmem(exchange(own, even_partner))
    raw = pltpu.VMEM((4, ROWS, LANES), jnp.float32)
    picks, table, waits = pl.pallas_call(
        read_links,
        out_shape=(
            pltpu.VMEM((3 * ROWS, LANES), jnp.int32),
            pltpu.VMEM((16, ROWS, LANES), jnp.float32),
            pltpu.SMEM((2, 6), jnp.int32),
        ),
        in_specs=[smem_spec(), vmem_spec()],
        out_specs=(vmem_spec(), vmem_spec(), smem_spec()),
        scratch_shapes=[raw],
        name="read_links",
    )(in_smem(links), in_vmem(own_coarse))

    ghosts = pl.pallas_call(
        interpolate,
        out_shape=pltpu.VMEM((3 * tile_rows, LANES), jnp.float32),
        in_specs=[smem_spec()] + [vmem_spec()] * members,
        out_specs=vmem_spec(),
        scratch_shapes=[
            pltpu.VMEM((members * 16, ROWS, LANES), jnp.float32),
            raw,
            pltpu.VMEM((3 * tile_rows, LANES), jnp.float32),
        ],
        cost_estimate=pl.CostEstimate(flops=10**10, bytes_accessed=10**10, transcendentals=0),
        name="interpolate",
    )(in_smem(corners), in_vmem(table), *group)

    count = len(PARTS)
    tiles = (tile_rows, LANES)
    waits, picks, ghosts = in_smem(waits), in_vmem(picks), in_vmem(ghosts)
    own = in_vmem(own)

    def fold(parts):
        ready = pl.pallas_call(
            make_ready,
            out_shape=pltpu.VMEM((READY * ROWS, LANES), jnp.float32),
            in_specs=[vmem_spec()] * (2 + len(parts)),
            out_specs=vmem_spec(),
            name="fold",
        )(ghosts, picks, *parts)
        return in_vmem(ready)

    made = (pltpu.VMEM(tiles, jnp.float32),) + tuple(pltpu.VMEM((rows, LANES), jnp.float32) for _, rows in PARTS)
    ready = fold([own])
    middle = pl.pallas_call(
        first_stage,
        out_shape=made,
        in_specs=[smem_spec()] + [vmem_spec()] * 4,
        out_specs=(vmem_spec(),) * len(made),
        name="first_stage",
    )(waits, ready, picks, own, even)
    middle, *parts = pl.pallas_call(
        first_stage_odd,
        out_shape=made,
        in_specs=[smem_spec()] + [vmem_spec()] * (5 + len(made)),
        out_specs=(vmem_spec(),) * len(made),
        input_output_aliases={6 + k: k for k in range(len(made))},
        name="first_stage_odd",
    )(waits, ready, picks, own, even, in_vmem(odd), *[in_vmem(m) for m in middle])

    odd = exchange(middle, odd_partner)
    even = [in_vmem(exchange(part, even_partner)) for part in parts]
    parts = [in_vmem(part) for part in parts]
    ready = fold(parts)
    scratch = [pltpu.VMEM(tiles, jnp.float32), pltpu.SemaphoreType.DMA(())]
    result = pl.pallas_call(
        second_stage,
        out_shape=jax.ShapeDtypeStruct(tiles, jnp.float32),
        in_specs=[smem_spec()] * 2 + [vmem_spec()] * (3 + 2 * count),
        out_specs=hbm_spec(),
        scratch_shapes=scratch,
        name="second_stage",
    )(waits, box_count, ready, picks, own, *parts, *even)
    result = pl.pallas_call(
        second_stage_odd,
        out_shape=jax.ShapeDtypeStruct(tiles, jnp.float32),
        in_specs=[smem_spec()] * 2 + [vmem_spec()] * (4 + 2 * count) + [hbm_spec()],
        out_specs=hbm_spec(),
        scratch_shapes=scratch,
        input_output_aliases={6 + 2 * count: 0},
        name="second_stage_odd",
    )(waits, box_count, ready, picks, own, *parts, *even, in_vmem(odd), result)
    return from_tiles(result, fine_state.shape)


def solution(mesh):
    placed = (
        P("sfc", "sub", None, None, None),
        P("sfc", "sub", None, None),
        P("sfc", "sub"),
        P("sfc", "sub", None, None),
        P("sfc", "sub", None, None, None),
    )
    return jax.shard_map(
        body,
        mesh=mesh,
        in_specs=placed,
        out_specs=P("sfc", "sub", None, None, None),
        check_vma=False,
    )
```

```python
import jax
import jax.numpy as jnp
from jax import lax
from jax.experimental import pallas as pl
from jax.experimental.pallas import tpu as pltpu
from jax.sharding import PartitionSpec as P

FIELDS = 5
ROWS = 8
LANES = 128
GAMMA = 1.4
FLOOR = 0.1
WENO_EPS = 1e-06
TIME_STEP = 0.1
PARTS = ((0, 32), (32, 8))
HERE, EVEN, ODD = 1, 3, 5


def to_tiles(boxes):
    slots, fields = boxes.shape[2], boxes.shape[3]
    parts = boxes.reshape(slots, fields, -1, LANES)
    return parts.transpose(1, 2, 0, 3).reshape(-1, LANES)


def from_tiles(tiles, shape):
    slots, fields = shape[2], shape[3]
    parts = tiles.reshape(fields, -1, slots, LANES)
    return parts.transpose(2, 0, 1, 3).reshape(shape)


def in_vmem(value):
    return pltpu.with_memory_space_constraint(value, pltpu.VMEM)


def in_smem(value):
    return pltpu.with_memory_space_constraint(value, pltpu.SMEM)


def exchange(value, partner):
    count, members = lax.axis_size("sfc"), lax.axis_size("sub")
    pairs = []
    for segment in range(count):
        for member in range(members):
            other, other_member = partner(segment, member, count, members)
            pairs.append((segment * members + member, other * members + other_member))
    return lax.ppermute(value, ("sfc", "sub"), pairs)


def even_partner(segment, member, count, members):
    other = segment ^ 1
    return (other, member) if other < count else (segment, member)


def odd_partner(segment, member, count, members):
    other = ((segment - 1) ^ 1) + 1
    if 0 < segment and other < count:
        return (other, member)
    other_member = member ^ 1
    return (segment, other_member) if other_member < members else (segment, member)


def group_shift(steps):
    def partner(segment, member, count, members):
        return (segment, (member + steps) % members)

    return partner


def positions():
    sub = lax.broadcasted_iota(jnp.int32, (ROWS, LANES), 0)
    lane = lax.broadcasted_iota(jnp.int32, (ROWS, LANES), 1)
    return sub, lane


def gather_lanes(value, index):
    return jnp.take_along_axis(value, index, axis=1, mode="promise_in_bounds")


def gather_rows(value, index):
    return jnp.take_along_axis(value, index, axis=0, mode="promise_in_bounds")


def roll_lanes(value, steps):
    return pltpu.roll(value, steps % LANES, 1)


def roll_rows(value, steps):
    if steps % ROWS == 0:
        return value
    sub, _ = positions()
    return gather_rows(value, (sub - steps) & 7)


def reciprocal(value):
    return 1.0 / value


def primitives(mass, mom_x, mom_y, mom_z, energy):
    density = jnp.maximum(mass, FLOOR)
    inverse = reciprocal(density)
    vel_x, vel_y, vel_z = mom_x * inverse, mom_y * inverse, mom_z * inverse
    kinetic = 0.5 * density * (vel_x * vel_x + vel_y * vel_y + vel_z * vel_z)
    pressure = jnp.maximum((GAMMA - 1.0) * (energy - kinetic), FLOOR)
    return [density, vel_x, vel_y, vel_z, pressure]


def load_parts(refs):
    return [ref[pl.ds(at, ROWS), :] for ref in refs for at in range(0, ref.shape[0], ROWS)]


def store_parts(refs, fields):
    fields = list(fields)
    for ref, (_, rows) in zip(refs, PARTS):
        for at in range(0, rows, ROWS):
            ref[pl.ds(at, ROWS), :] = fields.pop(0)


def load_primitives(ref, base=0):
    return primitives(*[ref[pl.ds(base + ROWS * f, ROWS), :] for f in range(FIELDS)])


def minmod(p, q):
    return jnp.maximum(jnp.minimum(p, q), 0.0) + jnp.minimum(jnp.maximum(p, q), 0.0)


def build_table(coarse_ref, raw, table, base):
    sub, lane = positions()
    low = lane < 64
    for j in range(4):
        for f in range(FIELDS):
            raw[j, f : f + 1, :] = coarse_ref[f * 4 + j]
    cells = [raw[j] for j in range(4)]
    halves = [roll_lanes(c, 64) for c in cells]
    for j in range(4):
        u, other, after, before = cells[j], halves[j], min(j + 1, 3), max(j - 1, 0)

        def slope_of(up, value, down):
            return 0.25 * minmod(up - value, value - down)

        along_x = slope_of(jnp.where(low, other, halves[after]), u, jnp.where(low, halves[before], other))
        swapped_x = slope_of(jnp.where(low, cells[after], u), other, jnp.where(low, u, cells[before]))
        along_y, along_z = [slope_of(roll_lanes(u, -n), u, roll_lanes(u, n)) for n in (8, 1)]
        swapped_y, swapped_z = [slope_of(roll_lanes(u, 64 - n), other, roll_lanes(u, 64 + n)) for n in (8, 1)]
        for x in (2 * j, 2 * j + 1):
            if x in (0, 7):
                continue
            if x % 2 == 0:
                value, slope = jnp.where(low, u, halves[j]), jnp.where(low, along_x, swapped_x)
                sides = jnp.where(low, along_y, swapped_z)
            else:
                value, slope = jnp.where(low, halves[j], u), jnp.where(low, swapped_x, along_x)
                sides = jnp.where(low, swapped_y, along_z)
            value = jnp.where(low, value - slope, value + slope)
            table[base + x] = jnp.where(sub < FIELDS, value, gather_rows(sides, (sub + 3) & 7))
            table[base + 8 + x] = jnp.where(sub < FIELDS, sides, gather_rows(sides, (sub + 6) & 7))


def fetch(links_in, corner_in, coarse_in, start_in, links_ref, corner_ref, coarse_ref, own_ref, sems):
    copies = [(links_in, links_ref), (corner_in, corner_ref), (coarse_in, coarse_ref), (start_in, own_ref)]
    fetches = [pltpu.make_async_copy(src, dst, sems.at[i]) for i, (src, dst) in enumerate(copies)]
    for copy in fetches:
        copy.start()
    for copy in fetches:
        copy.wait()


def read_links(links_ref, coarse_ref, pick_ref, table, code_ref, raw):
    sub, lane = positions()
    y, z = (lane >> 3) & 7, lane & 7
    odd_segment = lax.axis_index("sfc") & 1
    build_table(coarse_ref, raw, table, 0)

    def choice(slot, face):
        link = links_ref[slot, face]
        offset = link >> 1
        below = jnp.where(offset == 0, 1, 0)
        block = jnp.where(offset == 1, 0, jnp.where(below == odd_segment, 1, 2))
        swapped = (link & 1) ^ slot
        return jnp.where(link < 0, 0, 1 + block * 2 + swapped)

    codes = [[choice(slot, face) for face in range(6)] for slot in range(2)]
    waits = jnp.int32(0)
    for code in codes[0] + codes[1]:
        waits = jnp.maximum(waits, jnp.where(code >= ODD, 1, 0))
    code_ref[0, 0] = waits

    first = (sub & 1) == 0
    for direction in range(3):
        lower = (sub < 4) if direction == 0 else ((y if direction == 1 else z) < 4)
        minus = jnp.where(first, codes[0][2 * direction], codes[1][2 * direction])
        plus = jnp.where(first, codes[0][2 * direction + 1], codes[1][2 * direction + 1])
        pick_ref[pl.ds(direction * ROWS, ROWS), :] = jnp.where(lower, plus, minus)


def interpolate(corner_ref, own_table, *refs):
    coarse_refs, (ghost_ref, table, raw, lines) = refs[:-4], refs[-4:]
    members = len(coarse_refs) + 1
    sub, lane = positions()
    y, z = (lane >> 3) & 7, lane & 7
    me = lax.axis_index("sub")
    table[0:16] = own_table[...]
    for m, coarse_ref in enumerate(coarse_refs):
        build_table(coarse_ref, raw, table, (m + 1) * 16)

    sign_y = jnp.where((y & 1) == 0, -1.0, 1.0)
    sign_z = jnp.where((z & 1) == 0, -1.0, 1.0)
    spread = (y >> 1) * 8 + (z >> 1)
    upper, whole = jnp.where(sub < FIELDS, lane & 64, 0), jnp.where(sub < FIELDS, 64, 0)

    def finder(slot, face):
        direction, minus = face // 2, face % 2 == 0
        start = [corner_ref[slot, 1 + a, face] + (-1 if minus and a == direction else 1) for a in range(3)]
        owner = me - corner_ref[slot, 0, face]
        owner = jnp.where(owner < 0, owner + members, owner)
        index = (spread + (start[1] * 8 + start[2])) & 63
        first, second, row = index | upper, index | whole, owner * 16 + start[0]

        def find(j):
            return gather_lanes(table[row + j], first), gather_lanes(table[row + 8 + j], second)

        return find

    for direction in range(3):
        for slot in range(2):
            minus, plus = finder(slot, 2 * direction), finder(slot, 2 * direction + 1)
            for j in range(4):
                if direction == 0:
                    value, sides = (minus if j >= 2 else plus)(j)
                else:
                    lower = (y if direction == 1 else z) < 4
                    value, sides = [jnp.where(lower, p, m) for p, m in zip(plus(j), minus(j))]
                along_y = jnp.where(sub < 3, gather_rows(value, (sub + 5) & 7), gather_rows(sides, (sub + 2) & 7))
                value = value + sign_y * along_y + sign_z * sides
                rows = pl.ds(direction * 40 + j * 2 + slot, FIELDS, stride=ROWS)
                lines[rows, :] = value[0:FIELDS, :]
        made = load_primitives(lines, direction * 40)
        for f in range(FIELDS):
            ghost_ref[pl.ds(direction * 40 + f * ROWS, ROWS), :] = made[f]


def weno(cells, both=True):
    centre = cells[2]
    e0, e1, e2, e3 = [cells[k + 1] - cells[k] for k in range(4)]
    d1, d2, d3 = e1 - e0, e2 - e1, e3 - e2
    a = ((4.0 / 3.0) * (d1 * d1) + WENO_EPS) + e1 * (e1 + d1)
    b = ((4.0 / 3.0) * (d2 * d2) + WENO_EPS) + e1 * e2
    c = ((4.0 / 3.0) * (d3 * d3) + WENO_EPS) + e2 * (e2 - d3)
    bc, ac, ab = b * c, a * c, a * b
    bc, ac, ab = bc * bc, 6.0 * (ac * ac), ab * ab
    with_ab, with_bc = 3.0 * ab + ac, 3.0 * bc + ac
    low, high = bc * d1, ab * d3
    twice = 2.0 * (high - low)
    up = with_bc * d2 + (twice + high)
    upper = (centre + 0.5 * e2) - up * ((1.0 / 6.0) * reciprocal(bc + with_ab))
    if not both:
        return upper
    down = with_ab * d2 + (low - twice)
    lower = (centre - 0.5 * e1) - down * ((1.0 / 6.0) * reciprocal(ab + with_bc))
    return upper, lower


def hllc(left, right):
    rl, ul, vl, wl, pl_ = jnp.maximum(left[0], FLOOR), left[1], left[2], left[3], jnp.maximum(left[4], FLOOR)
    rr, ur, vr, wr, pr = jnp.maximum(right[0], FLOOR), right[1], right[2], right[3], jnp.maximum(right[4], FLOOR)
    gl, gr = GAMMA * pl_, GAMMA * pr
    cl, cr = gl * lax.rsqrt(gl * rl), gr * lax.rsqrt(gr * rr)
    speed_left = jnp.minimum(ul - cl, ur - cr)
    speed_right = jnp.maximum(ul + cl, ur + cr)
    ml, mr = rl * (speed_left - ul), rr * (speed_right - ur)
    top, bottom = pr - pl_ + ml * ul - mr * ur, ml - mr
    contact = top * reciprocal(bottom)
    ahead = top <= 0.0
    from_left = (speed_left >= 0.0) | ahead
    r = jnp.where(from_left, rl, rr)
    u = jnp.where(from_left, ul, ur)
    v = jnp.where(from_left, vl, vr)
    w = jnp.where(from_left, wl, wr)
    p = jnp.where(from_left, pl_, pr)
    s = jnp.where(from_left, speed_left, speed_right)
    m = jnp.where(from_left, ml, mr)
    star = (speed_left < 0.0) & (ahead | (speed_right >= 0.0))
    energy = p * (1.0 / (GAMMA - 1.0)) + 0.5 * r * (u * u + v * v + w * w)
    inverse = reciprocal(s - contact)
    star_p = p + m * (contact - u)
    star_e = ((s - u) * energy - p * u + star_p * contact) * inverse
    density = jnp.where(star, m * inverse, r)
    normal = jnp.where(star, contact, u)
    pressure = jnp.where(star, star_p, p)
    energy = jnp.where(star, star_e, energy)
    mass = density * normal
    return [mass, mass * normal + pressure, mass * v, mass * w, normal * (energy + pressure)]


class Turns:
    def __init__(self):
        sub, lane = positions()
        self.sub = sub
        y, z = (lane >> 3) & 7, lane & 7
        high = lane >> 6
        self.steps = (
            (sub ^ high, lane ^ ((sub & 1) << 6), sub ^ high),
            ((sub - y) & 7, (lane & 71) | (((sub - y) & 7) << 3), (sub + y) & 7),
            ((sub - z) & 7, (lane & 120) | ((sub - z) & 7), (sub + z) & 7),
        )

    def __call__(self, direction, value):
        before, across, after = self.steps[direction]
        return gather_rows(gather_lanes(gather_rows(value, before), across), after)


def swapped_slots(value, sub):
    return gather_rows(value, sub ^ 1)


OWN, GHOST, SHIFTED, READY = 0, 15, 30, 90
SHIFTS = (-2, -1, 1, 2)


def make_ready(ghost_ref, pick_ref, *refs):
    own_refs, ready_ref = refs[:-1], refs[-1]
    turn = Turns()
    own = primitives(*load_parts(own_refs))
    candidates = [own, [swapped_slots(v, turn.sub) for v in own]]
    for direction in range(3):
        pick = pick_ref[pl.ds(direction * ROWS, ROWS), :]
        wanted = [pick == c + 1 for c in range(len(candidates))]
        remote = pick > len(candidates)
        for f in range(FIELDS):
            value = ghost_ref[pl.ds((direction * FIELDS + f) * ROWS, ROWS), :]
            for c, candidate in enumerate(candidates):
                value = jnp.where(wanted[c], candidate[f], value)
            value = jnp.where(remote, 0.0, value)
            tile = direction * FIELDS + f
            ready_ref[pl.ds((GHOST + tile) * ROWS, ROWS), :] = turn(direction, value)
            cells = turn(direction, own[f])
            ready_ref[pl.ds((OWN + tile) * ROWS, ROWS), :] = cells
            for k, s in enumerate(SHIFTS):
                ready_ref[pl.ds((SHIFTED + tile * len(SHIFTS) + k) * ROWS, ROWS), :] = roll_rows(cells, -s)


def rate(blocks, ready_ref, pick_ref):
    turn = Turns()
    sub = turn.sub
    first_row = sub == 0
    candidates = []
    for block in blocks:
        candidates += [block, [swapped_slots(v, sub) for v in block]]

    def line(direction, f):
        pick = pick_ref[pl.ds(direction * ROWS, ROWS), :]
        tile = direction * FIELDS + f
        remote = jnp.zeros((ROWS, LANES), jnp.float32)
        for c, candidate in enumerate(candidates):
            remote = jnp.where(pick == EVEN + c, candidate[f], remote)
        ghost = ready_ref[pl.ds((GHOST + tile) * ROWS, ROWS), :] + turn(direction, remote)
        return ready_ref[pl.ds((OWN + tile) * ROWS, ROWS), :], ghost

    is_x, is_y = (sub == 7) | first_row, (sub == 1) | (sub == 2)
    places = (0, 2, 4)
    sides = [[], [], []]
    outer = []
    for f in range(FIELDS):
        beside = []
        for direction in range(3):
            own, ghost = line(direction, f)
            cells, around = [], []
            rolled_own, rolled_ghost = {}, {}
            for s in range(-2, 3):
                if s == 0:
                    cells.append(own)
                    continue
                shifted = SHIFTED + (direction * FIELDS + f) * len(SHIFTS) + SHIFTS.index(s)
                own_s, ghost_s = ready_ref[pl.ds(shifted * ROWS, ROWS), :], roll_rows(ghost, -s)
                outside = (sub < -s) if s < 0 else (sub > 7 - s)
                cells.append(jnp.where(outside, ghost_s, own_s))
                rolled_own[s], rolled_ghost[s] = own_s, ghost_s
            for s in range(-2, 3):
                if s == 0:
                    around.append(ghost)
                elif s < 0:
                    around.append(jnp.where(first_row, rolled_ghost[-s], rolled_ghost[s]))
                else:
                    around.append(jnp.where(first_row, rolled_own[-s], rolled_own[s]))
            sides[direction].append(weno(cells))
            beside.append(around)
        outer.append(
            weno(
                [
                    jnp.where(is_x, vx, jnp.where(is_y, roll_rows(vy, 2), roll_rows(vz, 4)))
                    for vx, vy, vz in zip(*beside)
                ],
                both=False,
            )
        )

    ended = []
    fluxes = []
    orders = ((0, 1, 2, 3, 4), (0, 2, 1, 3, 4), (0, 3, 1, 2, 4))
    for direction in range(3):
        rolled = [roll_rows(side[0], 1) for side in sides[direction]]
        ended.append([roll_rows(v, places[direction]) for v in rolled])
        lefts = [jnp.where(first_row, roll_rows(o, 1 - places[direction]), v) for o, v in zip(outer, rolled)]
        rights = [side[1] for side in sides[direction]]
        order = orders[direction]
        fluxes.append(hllc([lefts[f] for f in order], [rights[f] for f in order]))

    at_y, at_z = sub == 2, sub == 4

    def turned(values):
        normal = jnp.where(at_y, values[2], jnp.where(at_z, values[3], values[1]))
        one = jnp.where(at_y | at_z, values[1], values[2])
        two = jnp.where(at_z, values[2], values[3])
        return [values[0], normal, one, two, values[4]]

    left_end = [jnp.where(at_y, ended[1][f], jnp.where(at_z, ended[2][f], ended[0][f])) for f in range(FIELDS)]
    last = hllc(turned(left_end), turned(outer))

    total = [None] * FIELDS
    for direction in range(3):
        for place, f in enumerate(orders[direction]):
            flux = fluxes[direction][place]
            merged = jnp.where(first_row, roll_rows(last[place], -places[direction]), flux)
            change = turn(direction, flux - roll_rows(merged, -1))
            total[f] = change if total[f] is None else total[f] + change
    return total


def even_and_odd(even_refs, odd_refs):
    blocks = [primitives(*load_parts(even_refs))]
    return blocks + [load_primitives(ref) for ref in odd_refs]


def middle_of(own_refs, even_refs, odd_refs, ready_ref, pick_ref, out_ref, part_refs):
    own = load_parts(own_refs)
    change = rate(even_and_odd(even_refs, odd_refs), ready_ref, pick_ref)
    middle = [own[f] + TIME_STEP * change[f] for f in range(FIELDS)]
    store_parts(part_refs, middle)
    for f in range(FIELDS):
        out_ref[pl.ds(f * ROWS, ROWS), :] = middle[f]


def first_stage(waits_ref, ready_ref, pick_ref, own_ref, even_ref, *made):
    @pl.when(waits_ref[0, 0] == 0)
    def _():
        middle_of([own_ref], [even_ref], [], ready_ref, pick_ref, made[0], made[1:])


def first_stage_odd(waits_ref, ready_ref, pick_ref, own_ref, even_ref, odd_ref, *refs):
    made = refs[len(refs) // 2 :]

    @pl.when(waits_ref[0, 0] != 0)
    def _():
        middle_of([own_ref], [even_ref], [odd_ref], ready_ref, pick_ref, made[0], made[1:])


def advanced_of(start_refs, own_refs, even_refs, odd_refs, ready_ref, pick_ref, count_ref, out_ref, made_ref, sem):
    start, own = load_parts(start_refs), load_parts(own_refs)
    change = rate(even_and_odd(even_refs, odd_refs), ready_ref, pick_ref)
    sub, _ = positions()
    live = (sub & 1) < count_ref[0, 0]
    for f in range(FIELDS):
        value = 0.5 * start[f] + 0.5 * (own[f] + TIME_STEP * change[f])
        made_ref[pl.ds(f * ROWS, ROWS), :] = jnp.where(live, value, 0.0)
    copy = pltpu.make_async_copy(made_ref, out_ref, sem)
    copy.start()
    copy.wait()


def second_stage(waits_ref, count_ref, ready_ref, pick_ref, start_ref, *refs):
    n = len(PARTS)
    own_refs, even_refs, (out_ref, made_ref, sem) = refs[:n], refs[n : 2 * n], refs[2 * n :]

    @pl.when(waits_ref[0, 0] == 0)
    def _():
        advanced_of([start_ref], own_refs, even_refs, [], ready_ref, pick_ref, count_ref, out_ref, made_ref, sem)


def second_stage_odd(waits_ref, count_ref, ready_ref, pick_ref, start_ref, *refs):
    n = len(PARTS)
    own_refs, even_refs, (odd_ref, _, out_ref, made_ref, sem) = refs[:n], refs[n : 2 * n], refs[2 * n :]

    @pl.when(waits_ref[0, 0] != 0)
    def _():
        advanced_of([start_ref], own_refs, even_refs, [odd_ref], ready_ref, pick_ref, count_ref, out_ref, made_ref, sem)


def vmem_spec():
    return pl.BlockSpec(memory_space=pltpu.VMEM)


def smem_spec():
    return pl.BlockSpec(memory_space=pltpu.SMEM)


def hbm_spec():
    return pl.BlockSpec(memory_space=pltpu.HBM)


def body(fine_state, coarse_old, box_count, fine_links, coarse_links):
    members = lax.axis_size("sub")
    tile_rows = FIELDS * ROWS
    start = to_tiles(fine_state)
    coarse = coarse_old.transpose(0, 2, 1, 3).reshape(FIELDS, 1, -1, LANES).transpose(0, 2, 1, 3)
    coarse = coarse.reshape(-1, 1, LANES)

    odd = exchange(start, odd_partner)
    group = [in_vmem(exchange(coarse, group_shift(r))) for r in range(1, members)]

    links, corners, own_coarse, own = pl.pallas_call(
        fetch,
        out_shape=(
            pltpu.SMEM((2, 6), jnp.int32),
            pltpu.SMEM((2, 4, 6), jnp.int32),
            pltpu.VMEM((FIELDS * 4, 1, LANES), jnp.float32),
            pltpu.VMEM((tile_rows, LANES), jnp.float32),
        ),
        in_specs=[hbm_spec()] * 4,
        out_specs=(smem_spec(), smem_spec(), vmem_spec(), vmem_spec()),
        scratch_shapes=[pltpu.SemaphoreType.DMA((4,))],
        name="fetch",
    )(
        fine_links.reshape(2, 6),
        coarse_links.transpose(0, 1, 2, 4, 3).reshape(2, 4, 6),
        coarse,
        start,
    )
    even = in_vmem(exchange(own, even_partner))
    raw = pltpu.VMEM((4, ROWS, LANES), jnp.float32)
    picks, table, waits = pl.pallas_call(
        read_links,
        out_shape=(
            pltpu.VMEM((3 * ROWS, LANES), jnp.int32),
            pltpu.VMEM((16, ROWS, LANES), jnp.float32),
            pltpu.SMEM((2, 6), jnp.int32),
        ),
        in_specs=[smem_spec(), vmem_spec()],
        out_specs=(vmem_spec(), vmem_spec(), smem_spec()),
        scratch_shapes=[raw],
        name="read_links",
    )(in_smem(links), in_vmem(own_coarse))

    ghosts = pl.pallas_call(
        interpolate,
        out_shape=pltpu.VMEM((3 * tile_rows, LANES), jnp.float32),
        in_specs=[smem_spec()] + [vmem_spec()] * members,
        out_specs=vmem_spec(),
        scratch_shapes=[
            pltpu.VMEM((members * 16, ROWS, LANES), jnp.float32),
            raw,
            pltpu.VMEM((3 * tile_rows, LANES), jnp.float32),
        ],
        cost_estimate=pl.CostEstimate(flops=10**10, bytes_accessed=10**10, transcendentals=0),
        name="interpolate",
    )(in_smem(corners), in_vmem(table), *group)

    count = len(PARTS)
    tiles = (tile_rows, LANES)
    waits, picks, ghosts = in_smem(waits), in_vmem(picks), in_vmem(ghosts)
    own = in_vmem(own)

    def fold(parts):
        ready = pl.pallas_call(
            make_ready,
            out_shape=pltpu.VMEM((READY * ROWS, LANES), jnp.float32),
            in_specs=[vmem_spec()] * (2 + len(parts)),
            out_specs=vmem_spec(),
            name="fold",
        )(ghosts, picks, *parts)
        return in_vmem(ready)

    made = (pltpu.VMEM(tiles, jnp.float32),) + tuple(pltpu.VMEM((rows, LANES), jnp.float32) for _, rows in PARTS)
    ready = fold([own])
    middle = pl.pallas_call(
        first_stage,
        out_shape=made,
        in_specs=[smem_spec()] + [vmem_spec()] * 4,
        out_specs=(vmem_spec(),) * len(made),
        name="first_stage",
    )(waits, ready, picks, own, even)
    middle, *parts = pl.pallas_call(
        first_stage_odd,
        out_shape=made,
        in_specs=[smem_spec()] + [vmem_spec()] * (5 + len(made)),
        out_specs=(vmem_spec(),) * len(made),
        input_output_aliases={6 + k: k for k in range(len(made))},
        name="first_stage_odd",
    )(waits, ready, picks, own, even, in_vmem(odd), *[in_vmem(m) for m in middle])

    odd = exchange(middle, odd_partner)
    even = [in_vmem(exchange(part, even_partner)) for part in parts]
    parts = [in_vmem(part) for part in parts]
    ready = fold(parts)
    scratch = [pltpu.VMEM(tiles, jnp.float32), pltpu.SemaphoreType.DMA(())]
    result = pl.pallas_call(
        second_stage,
        out_shape=jax.ShapeDtypeStruct(tiles, jnp.float32),
        in_specs=[smem_spec()] * 2 + [vmem_spec()] * (3 + 2 * count),
        out_specs=hbm_spec(),
        scratch_shapes=scratch,
        name="second_stage",
    )(waits, box_count, ready, picks, own, *parts, *even)
    result = pl.pallas_call(
        second_stage_odd,
        out_shape=jax.ShapeDtypeStruct(tiles, jnp.float32),
        in_specs=[smem_spec()] * 2 + [vmem_spec()] * (4 + 2 * count) + [hbm_spec()],
        out_specs=hbm_spec(),
        scratch_shapes=scratch,
        input_output_aliases={6 + 2 * count: 0},
        name="second_stage_odd",
    )(waits, box_count, ready, picks, own, *parts, *even, in_vmem(odd), result)
    return from_tiles(result, fine_state.shape)


def solution(mesh):
    placed = (
        P("sfc", "sub", None, None, None),
        P("sfc", "sub", None, None),
        P("sfc", "sub"),
        P("sfc", "sub", None, None),
        P("sfc", "sub", None, None, None),
    )
    return jax.shard_map(
        body,
        mesh=mesh,
        in_specs=placed,
        out_specs=P("sfc", "sub", None, None, None),
        check_vma=False,
    )
```
